128 devices in a mesh: tr: 8 (over z, core), tc: 16 (over x, y).
Axes of the slice: x: 4, y: 4, z: 4, core: 2. Of those that a mesh axis runs over, the one named last changes fastest.
Arguments:
- embeddings: bfloat16 [98304, 1024], P(('tr', 'tc')), may hold values from -100 to 100
- labels: int32 [98304], P(('tr', 'tc')), may hold values from 0 to 31, as said below
Outputs:
- best_sim: float32 [98304], P(('tr', 'tc'))
- weighted: float32 [98304], P(('tr', 'tc'))
- flag: float32 [98304], P(('tr', 'tc'))
The draws below stay inside these ranges and needn't reach their ends.
Inputs may be any that keep to these rules, and one draw needn't show every extreme that they name: In each aligned block of 768 files (one corpus shard), at most 288 files have labels // 4 equal to any one value g, and every shard has exactly 288 for some g; for every g and every c below 16, the shards c, c + 16, c + 32, ... together hold exactly 768 files with labels // 4 = g; every label is held by two or more files.
All inputs are finite; a program needn't handle non-finite values.
Results may differ from the reference program's by a relative error of at most 0.0013.
Values may be sent and summed in bfloat16 or wider, within the bound.
No kernel may reach another device: no remote copies, remote signals or barrier semaphores. Data moves between devices by JAX's collectives and lax.ppermute only.
A program may use at most 128 MiB of HBM per device.

```python
import jax
import jax.numpy as jnp
from jax import lax

D = 1024
ROWS_DEV = 768
GROUP_CLUSTERS = 4
ROWS = 98304
N_TR = 8
N_TC = 16


def plan_labels(key):
    key = jax.random.fold_in(key, 7)
    key_wiggle, key_shift, key_perm, key_sub, key_other, key_offset = jax.random.split(key, 6)
    shards = N_TR * N_TC
    capacity = 3 * ROWS_DEV // N_TR
    remain = ROWS_DEV - capacity
    base = remain // (N_TR - 1)
    extra = remain - base * (N_TR - 1)
    wiggle = jax.random.randint(key_wiggle, (N_TC, N_TR - 1), 0, base // 2 + 1)
    others = base + wiggle - jnp.roll(wiggle, 1, axis=1) + (jnp.arange(N_TR - 1) < extra).astype(jnp.int32)[None, :]
    weights = jnp.concatenate([jnp.full((N_TC, 1), capacity, jnp.int32), others], axis=1)
    shift = jax.random.randint(key_shift, (N_TC,), 0, N_TR)
    row_ids = jnp.arange(N_TR)[:, None, None]
    col_ids = jnp.arange(N_TC)[None, :, None]
    target_ids = jnp.arange(N_TR)[None, None, :]
    which = (target_ids - row_ids - shift[None, :, None]) % N_TR
    counts = weights[jnp.broadcast_to(col_ids, which.shape), which].reshape(shards, N_TR)
    bounds = jnp.cumsum(counts, axis=1)
    positions = jnp.arange(ROWS_DEV)
    ordered = jnp.sum((positions[None, :, None] >= bounds[:, None, :]).astype(jnp.int32), axis=2)
    perm_keys = jax.random.split(key_perm, shards)
    owner = jax.vmap(lambda single, row: jax.random.permutation(single, row))(perm_keys, ordered)
    onehot = (owner[:, :, None] == jnp.arange(N_TR)[None, None, :]).astype(jnp.int32)
    running = jnp.sum(jnp.cumsum(onehot, axis=1) * onehot, axis=2)
    offset = jax.random.randint(key_offset, (N_TR,), 0, GROUP_CLUSTERS)
    first_pick = jax.random.randint(key_sub, (shards, ROWS_DEV), 0, GROUP_CLUSTERS)
    second_pick = jax.random.randint(key_other, (shards, ROWS_DEV), 0, GROUP_CLUSTERS)
    skewed = (jnp.minimum(first_pick, second_pick) + offset[owner]) % GROUP_CLUSTERS
    source = (jnp.arange(shards)[:, None] + offset[owner]) % GROUP_CLUSTERS
    member = jnp.where(running == 1, source, skewed)
    return (owner * GROUP_CLUSTERS + member).reshape(-1).astype(jnp.int32)


def draw_labels(key, part):
    return plan_labels(key)


def draw_embeddings(key, part):
    labels = plan_labels(key)
    key = jax.random.fold_in(key, 3)
    key_noise, key_center, key_mix, key_scale = jax.random.split(key, 4)
    centers = jnp.clip(jax.random.normal(key_center, (GROUP_CLUSTERS * N_TR, D), jnp.float32), -4.0, 4.0)
    noise = jnp.clip(jax.random.normal(key_noise, (ROWS, D), jnp.float32), -4.0, 4.0)
    mix = jax.random.uniform(key_mix, (GROUP_CLUSTERS * N_TR,), jnp.float32, 0.3, 0.8)
    scale = jnp.exp(jax.random.uniform(key_scale, (ROWS,), jnp.float32, -0.69, 2.08))
    drawn = noise + mix[labels][:, None] * centers[labels]
    return (drawn * scale[:, None]).astype(jnp.bfloat16)


def setup_inputs(seed: int = 0) -> dict:
    streams_of = jax.random.split(jax.random.key(seed), 3)
    embeddings = draw_embeddings(jax.random.fold_in(streams_of[2], 71), 0)
    labels = draw_labels(jax.random.fold_in(streams_of[2], 71), 0)
    return {"embeddings": embeddings, "labels": labels}


SCALE = 256.0
NEGATIVE = -1e+30
EPSILON = 1e-06
THRESHOLD = 0.3
SHARPNESS = 50.0

def reference(embeddings, labels):
    values = embeddings.astype(jnp.float32)
    unit = (values * lax.rsqrt(lax.optimization_barrier(jnp.sum(values * values, axis=1, keepdims=True)) + EPSILON)).astype(jnp.bfloat16)
    group = (labels // GROUP_CLUSTERS).astype(jnp.int32)
    order = jnp.argsort(group, stable=True).astype(jnp.int32)
    members = N_TC * ROWS_DEV
    sorted_unit = unit[order].reshape(N_TR, members, D)
    sorted_labels = labels[order].reshape(N_TR, members)
    member_index = jnp.arange(members, dtype=jnp.int32)

    def one_group(item):
        group_unit, group_labels = item

        def one_block(inner):
            block_unit, block_labels, block_index = inner
            sims = jnp.dot(block_unit, group_unit.T, preferred_element_type=jnp.float32)
            mask = (block_labels[:, None] == group_labels[None, :]) & (block_index[:, None] != member_index[None, :])
            scores = SCALE * sims
            top = lax.optimization_barrier(jnp.max(jnp.where(mask, scores, NEGATIVE), axis=1))
            terms = jnp.where(mask, jnp.exp(scores - top[:, None]), 0.0)
            return (top / SCALE, lax.optimization_barrier(jnp.sum(terms * sims, axis=1)) / lax.optimization_barrier(jnp.sum(terms, axis=1)))
        best, mean_sim = lax.map(one_block, (group_unit.reshape(N_TC, ROWS_DEV, D), group_labels.reshape(N_TC, ROWS_DEV), member_index.reshape(N_TC, ROWS_DEV)))
        return (best.reshape(-1), mean_sim.reshape(-1))
    best, mean_sim = lax.map(one_group, (sorted_unit, sorted_labels))
    best_sim = jnp.zeros((ROWS,), jnp.float32).at[order].set(best.reshape(-1))
    weighted = jnp.zeros((ROWS,), jnp.float32).at[order].set(mean_sim.reshape(-1))
    flag = jax.nn.sigmoid(SHARPNESS * (best_sim - THRESHOLD))
    return (best_sim, weighted, flag)
```

```python
import functools

import jax
import jax.numpy as jnp
from jax import lax
from jax.experimental import pallas as pl
from jax.experimental.pallas import tpu as pltpu
from jax.sharding import PartitionSpec as P

GROUP_SHIFT = 2
TILE_ROWS = 8
SIDE = 4
ROWS = 768
WIDTH = 1024
CAP = 288
PAIR = 304
LANES = 384
BLOCK = ROWS + 16
SPAN = 1152
EPSILON = 1e-06
THRESHOLD = 0.3
SHARPNESS = 50.0
SCALE2 = 256.0 * 1.4426950408889634
NEGATIVE = -1e30
FLOOR = -5e29
CHUNK = 256
VMEM = 56 * 1024 * 1024
BF = jnp.bfloat16
F32 = jnp.float32


def iota(shape, axis):
    return lax.broadcasted_iota(jnp.int32, shape, axis)


def dot(a, b):
    return lax.dot_general(a, b, (((1,), (0,)), ((), ())), preferred_element_type=F32)


def dot_nt(a, b):
    return lax.dot_general(a, b, (((1,), (1,)), ((), ())), preferred_element_type=F32)


def params(**more):
    return pltpu.CompilerParams(vmem_limit_bytes=VMEM, **more)


def whole(shape):
    return pl.BlockSpec(shape, lambda *_: (0,) * len(shape))


def pack_kernel(emb_ref, lab_ref, out_ref, rank_ref, unit):
    g = pl.program_id(0)
    lab = lab_ref[...]
    owner = lax.shift_right_logical(lab, GROUP_SHIFT)

    @pl.when(g == 0)
    def _():
        values = emb_ref[...].astype(F32)
        total = jnp.sum(values * values, axis=1, keepdims=True)
        unit[...] = (values * lax.rsqrt(total + EPSILON)).astype(BF)
        onehot = (iota((TILE_ROWS, ROWS), 0) == owner).astype(F32)
        before = (iota((ROWS, ROWS), 0) < iota((ROWS, ROWS), 1)).astype(F32).astype(BF)
        seen = dot(onehot.astype(BF), before)
        rank_ref[...] = jnp.sum(onehot * seen, axis=0, keepdims=True).astype(jnp.int32)

    slot = jnp.where(owner == g, rank_ref[...], -1)
    pick = (iota((LANES, ROWS), 0) == slot).astype(F32).astype(BF)
    out_ref[0] = dot(pick[:PAIR], unit[...]).astype(BF)
    marks = jnp.broadcast_to(lab.astype(F32) + 1.0, (16, ROWS)).astype(BF)
    out_ref[0, CAP:, :LANES] = (dot_nt(marks, pick) - 1.0).astype(BF)
    out_ref[0, CAP:, LANES:] = jnp.zeros((16, WIDTH - LANES), BF)


def pack(embeddings, labels):
    return pl.pallas_call(
        pack_kernel,
        grid=(TILE_ROWS,),
        in_specs=[whole((ROWS, WIDTH)), whole((1, ROWS))],
        out_specs=[pl.BlockSpec((1, PAIR, WIDTH), lambda g: (g, 0, 0)), whole((1, ROWS))],
        out_shape=[
            jax.ShapeDtypeStruct((TILE_ROWS, PAIR, WIDTH), BF),
            jax.ShapeDtypeStruct((1, ROWS), jnp.int32),
        ],
        scratch_shapes=[pltpu.VMEM((ROWS, WIDTH), BF)],
        compiler_params=params(),
        name="pack",
    )(embeddings, labels)


def compact_kernel(got_ref, out_ref, offset_ref, rows, names, place):
    r = pl.program_id(0)

    @pl.when(r == 0)
    def _():
        place[0] = 0
        rows[:16] = jnp.zeros((16, WIDTH), BF)
        names[...] = jnp.zeros((8, SPAN), F32)

    offset = place[0]
    offset_ref[r] = offset
    lab = got_ref[0, CAP:, :LANES].astype(F32)[:8]
    count = jnp.sum((lab[:1] >= 0.0).astype(F32)).astype(jnp.int32)
    place[0] = offset + count
    base = pl.multiple_of(lax.div(offset, 16) * 16, 16)
    column = iota((PAIR, PAIR), 1)
    move = (iota((PAIR, PAIR), 0) == column + (offset - base)) & (column < count)
    moved = dot(move.astype(F32).astype(BF), got_ref[0]).astype(BF)
    rows[pl.ds(base, 16)] = rows[pl.ds(base, 16)] + moved[:16]
    rows[pl.ds(base + 16, PAIR - 16)] = moved[16:]
    held = jnp.concatenate([jnp.maximum(lab, 0.0), jnp.zeros((8, SPAN - LANES), F32)], axis=1)
    names[...] += pltpu.roll(held, offset, 1)

    @pl.when(r == TILE_ROWS - 1)
    def _():
        out_ref[:ROWS] = rows[:ROWS]
        out_ref[ROWS:, :ROWS] = jnp.broadcast_to(names[:1, :ROWS], (16, ROWS)).astype(BF)
        out_ref[ROWS:, ROWS:] = jnp.zeros((16, WIDTH - ROWS), BF)


def compact(got):
    return pl.pallas_call(
        compact_kernel,
        grid=(TILE_ROWS,),
        in_specs=[pl.BlockSpec((1, PAIR, WIDTH), lambda r: (r, 0, 0))],
        out_specs=[whole((BLOCK, WIDTH)), pl.BlockSpec(memory_space=pltpu.SMEM)],
        out_shape=[
            jax.ShapeDtypeStruct((BLOCK, WIDTH), BF),
            jax.ShapeDtypeStruct((TILE_ROWS,), jnp.int32),
        ],
        scratch_shapes=[
            pltpu.VMEM((ROWS + PAIR, WIDTH), BF),
            pltpu.VMEM((8, SPAN), F32),
            pltpu.SMEM((1,), jnp.int32),
        ],
        compiler_params=params(),
        name="compact",
    )(got)


def fold(tile):
    return tile.reshape(tile.shape[0] // 8, 8, tile.shape[1])


def column_stats(query, keys, scores):
    names = query[ROWS:, :ROWS].astype(F32)[:1]
    top = jnp.full((8, ROWS), NEGATIVE, F32)
    for k, (block, marks, same) in enumerate(keys):

        def score(i, top, k=k, block=block, marks=marks, same=same):
            start = pl.multiple_of(i * CHUNK, CHUNK)
            sims = dot_nt(block[pl.ds(start, CHUNK)], query[:ROWS]) * SCALE2
            mark = marks[pl.ds(start, CHUNK)]
            mask = jnp.concatenate([mark] * (ROWS // 128), axis=1) == names
            if same:
                mask = mask & (iota((CHUNK, ROWS), 0) + start != iota((CHUNK, ROWS), 1))
            sims = jnp.where(mask, sims, NEGATIVE)
            scores[pl.ds(pl.multiple_of(k * ROWS + start, CHUNK), CHUNK)] = sims
            return jnp.maximum(top, jnp.max(fold(sims), axis=0))

        top = lax.fori_loop(0, ROWS // CHUNK, score, top)
    top = jnp.maximum(jnp.max(top, axis=0, keepdims=True), FLOOR)

    def add(i, sums):
        sims = scores[pl.ds(pl.multiple_of(i * CHUNK, CHUNK), CHUNK)]
        terms = jnp.exp2(sims - top)
        return (
            sums[0] + jnp.sum(fold(terms), axis=0),
            sums[1] + jnp.sum(fold(terms * sims), axis=0),
        )

    zero = jnp.zeros((8, ROWS), F32)
    total, weight = lax.fori_loop(0, len(keys) * ROWS // CHUNK, add, (zero, zero))
    return top, jnp.sum(total, axis=0, keepdims=True), jnp.sum(weight, axis=0, keepdims=True)


def merge(parts):
    top = functools.reduce(jnp.maximum, [p[0] for p in parts])
    factors = [jnp.exp2(p[0] - top) for p in parts]
    total = sum(p[1] * f for p, f in zip(parts, factors))
    weight = sum(p[2] * f for p, f in zip(parts, factors))
    return top, total, weight


def put_stats(ref, stats):
    for k, value in enumerate(stats):
        ref[k : k + 1] = value


def get_stats(ref):
    return tuple(ref[k : k + 1] for k in range(3))


def pair_kernel(plan, blocks, old, *refs):
    n_old = len(old)
    ins, olds = refs[: len(blocks)], refs[len(blocks) : len(blocks) + n_old]
    outs = refs[len(blocks) + n_old : -2]
    marks, scores = refs[-2:]
    where = {b: i for i, b in enumerate(blocks)}
    used = sorted({k for _, keys in plan for k in keys})
    for b in used:
        names = ins[where[b]][ROWS:, :ROWS].astype(F32)
        marks[where[b]] = jnp.transpose(jnp.broadcast_to(names[:1], (128, ROWS)))
    before = {b: olds[i] for i, b in enumerate(old)}
    for out, (q, keys) in zip(outs, plan):
        stats = column_stats(
            ins[where[q]], [(ins[where[k]], marks.at[where[k]], k == q) for k in keys], scores
        )
        if q in before:
            stats = merge([stats, get_stats(before[q])])
        put_stats(out, stats)


def pairs(plan, blocks, old):
    names, n = list(blocks), len(plan)
    most = max(len(keys) for _, keys in plan)
    units = sum(len(keys) for _, keys in plan)
    return pl.pallas_call(
        functools.partial(pair_kernel, plan, names, list(old)),
        out_shape=[jax.ShapeDtypeStruct((8, ROWS), F32)] * n,
        in_specs=[pl.BlockSpec(memory_space=pltpu.VMEM)] * (len(blocks) + len(old)),
        out_specs=[pl.BlockSpec(memory_space=pltpu.VMEM)] * n,
        scratch_shapes=[
            pltpu.VMEM((len(blocks), ROWS, 128), F32),
            pltpu.VMEM((most * ROWS, ROWS), F32),
        ],
        compiler_params=params(),
        cost_estimate=pl.CostEstimate(
            flops=2 * units * ROWS * ROWS * WIDTH,
            bytes_accessed=2 * len(blocks) * BLOCK * WIDTH,
            transcendentals=units * ROWS * ROWS,
        ),
        name="pairs",
    )(*blocks.values(), *old.values())


def spread_kernel(offset_ref, *refs):
    out_ref = refs[-1]
    top, total, weight = merge([get_stats(r) for r in refs[:-1]])
    best = top / SCALE2
    mean = weight / total / SCALE2
    row = iota((8, ROWS), 0)
    values = jnp.where(row == 0, best, jnp.where(row == 1, mean, 0.0))
    values = jnp.concatenate([values, jnp.zeros((8, SPAN - ROWS), F32)], axis=1)
    for r in range(TILE_ROWS):
        offset = offset_ref[r]
        out_ref[r] = pltpu.roll(values, lax.rem(SPAN - offset, SPAN), 1)[:, :LANES]


def spread(offsets, stats):
    return pl.pallas_call(
        spread_kernel,
        out_shape=jax.ShapeDtypeStruct((TILE_ROWS, 8, LANES), F32),
        in_specs=[pl.BlockSpec(memory_space=pltpu.SMEM)]
        + [pl.BlockSpec(memory_space=pltpu.VMEM)] * len(stats),
        out_specs=pl.BlockSpec(memory_space=pltpu.VMEM),
        compiler_params=params(),
        name="spread",
    )(offsets, *stats)


def unpack_kernel(back_ref, lab_ref, rank_ref, best_ref, mean_ref, flag_ref):
    owner = lax.shift_right_logical(lab_ref[...], GROUP_SHIFT)
    found = jnp.zeros((24, ROWS), F32)
    for g in range(TILE_ROWS):
        slot = jnp.where(owner == g, rank_ref[...], -1)
        pick = (iota((LANES, ROWS), 0) == slot).astype(F32).astype(BF)
        values = back_ref[g]
        high = values.astype(BF).astype(F32)
        mid = (values - high).astype(BF).astype(F32)
        low = values - high - mid
        found += dot(jnp.concatenate([high, mid, low], axis=0).astype(BF), pick)
    found = found[:8] + (found[8:16] + found[16:])
    best = found[:1]
    best_ref[...] = best
    mean_ref[...] = found[1:2]
    flag_ref[...] = 1.0 / (1.0 + jnp.exp(-SHARPNESS * (best - THRESHOLD)))


def unpack(back, labels, rank):
    return pl.pallas_call(
        unpack_kernel,
        out_shape=[jax.ShapeDtypeStruct((1, ROWS), F32)] * 3,
        in_specs=[pl.BlockSpec(memory_space=pltpu.VMEM)] * 3,
        out_specs=[pl.BlockSpec(memory_space=pltpu.VMEM)] * 3,
        compiler_params=params(),
        name="unpack",
    )(back, labels, rank)


def shift(array, dx, dy):
    moves = []
    for tr in range(TILE_ROWS):
        sign = 1 - 2 * (tr % 2)
        for x in range(SIDE):
            for y in range(SIDE):
                to = ((x + sign * dx) % SIDE) * SIDE + (y + sign * dy) % SIDE
                base = tr * SIDE * SIDE
                moves.append((base + x * SIDE + y, base + to))
    return lax.ppermute(array, ("tr", "tc"), moves)


PLACES = {"O": (0, 0), "A": (1, 0), "B": (2, 0), "C": (0, 1), "D": (0, -1), "E": (0, 2)}
NEAR = [("O", "OAC"), ("A", "OCD"), ("C", "OA"), ("D", "AC")]
FAR = [("O", "B"), ("A", "E"), ("B", "CE"), ("C", "B"), ("E", "A")]


def per_device(embeddings, labels):
    lab = labels.reshape(1, ROWS)
    packed, rank = pack(embeddings, lab)
    got = lax.all_to_all(packed, "tr", split_axis=0, concat_axis=0, tiled=True)
    mine, offsets = compact(got)
    a = shift(mine, -1, 0)
    c = shift(mine, 0, -1)
    d = shift(mine, 0, 1)
    b = shift(a, -1, 0)
    e = shift(d, 0, 1)
    near = pairs(NEAR, {"O": mine, "A": a, "C": c, "D": d}, {})
    stats = dict(zip([q for q, _ in NEAR], near))
    far = pairs(
        FAR,
        {"O": mine, "A": a, "B": b, "C": c, "E": e},
        {q: stats[q] for q in "OAC"},
    )
    stats.update(zip([q for q, _ in FAR], far))
    parts = [stats["O"]] + [shift(stats[q], *PLACES[q]) for q in "ABCDE"]
    sent = spread(offsets, parts)
    back = lax.all_to_all(sent, "tr", split_axis=0, concat_axis=0, tiled=True)
    outs = unpack(back, lab, rank)
    return tuple(o.reshape(ROWS) for o in outs)


def solution(mesh):
    files = P(("tr", "tc"))
    return jax.shard_map(
        per_device,
        mesh=mesh,
        in_specs=(P(("tr", "tc"), None), files),
        out_specs=(files, files, files),
        check_vma=False,
    )
```

```python
import functools

import jax
import jax.numpy as jnp
from jax import lax
from jax.experimental import pallas as pl
from jax.experimental.pallas import tpu as pltpu
from jax.sharding import PartitionSpec as P

GROUP_SHIFT = 2
TILE_ROWS = 8
SIDE = 4
ROWS = 768
WIDTH = 1024
CAP = 288
PAIR = 304
LANES = 384
BLOCK = ROWS + 16
SPAN = 1152
EPSILON = 1e-06
THRESHOLD = 0.3
SHARPNESS = 50.0
SCALE2 = 256.0 * 1.4426950408889634
NEGATIVE = -1e30
FLOOR = -5e29
CHUNK = 256
HALF = 384
STRIP = 32
VMEM = 56 * 1024 * 1024
BF = jnp.bfloat16
F32 = jnp.float32


def iota(shape, axis):
    return lax.broadcasted_iota(jnp.int32, shape, axis)


def dot(a, b):
    return lax.dot_general(a, b, (((1,), (0,)), ((), ())), preferred_element_type=F32)


def dot_nt(a, b):
    return lax.dot_general(a, b, (((1,), (1,)), ((), ())), preferred_element_type=F32)


def params(**more):
    return pltpu.CompilerParams(vmem_limit_bytes=VMEM, **more)


def whole(shape):
    return pl.BlockSpec(shape, lambda *_: (0,) * len(shape))


def pack_kernel(emb_ref, lab_ref, out_ref, rank_ref, unit):
    g = pl.program_id(0)
    lab = lab_ref[...]
    owner = lax.shift_right_logical(lab, GROUP_SHIFT)

    @pl.when(g == 0)
    def _():
        values = emb_ref[...].astype(F32)
        total = jnp.sum(values * values, axis=1, keepdims=True)
        unit[...] = (values * lax.rsqrt(total + EPSILON)).astype(BF)
        onehot = (iota((TILE_ROWS, ROWS), 0) == owner).astype(F32)
        before = (iota((ROWS, ROWS), 0) < iota((ROWS, ROWS), 1)).astype(F32).astype(BF)
        seen = dot(onehot.astype(BF), before)
        rank_ref[...] = jnp.sum(onehot * seen, axis=0, keepdims=True).astype(jnp.int32)

    slot = jnp.where(owner == g, rank_ref[...], -1)
    pick = (iota((LANES, ROWS), 0) == slot).astype(F32).astype(BF)
    out_ref[0] = dot(pick[:PAIR], unit[...]).astype(BF)
    marks = jnp.broadcast_to(lab.astype(F32) + 1.0, (16, ROWS)).astype(BF)
    out_ref[0, CAP:, :LANES] = (dot_nt(marks, pick) - 1.0).astype(BF)
    out_ref[0, CAP:, LANES:] = jnp.zeros((16, WIDTH - LANES), BF)


def pack(embeddings, labels):
    return pl.pallas_call(
        pack_kernel,
        grid=(TILE_ROWS,),
        in_specs=[whole((ROWS, WIDTH)), whole((1, ROWS))],
        out_specs=[pl.BlockSpec((1, PAIR, WIDTH), lambda g: (g, 0, 0)), whole((1, ROWS))],
        out_shape=[
            jax.ShapeDtypeStruct((TILE_ROWS, PAIR, WIDTH), BF),
            jax.ShapeDtypeStruct((1, ROWS), jnp.int32),
        ],
        scratch_shapes=[pltpu.VMEM((ROWS, WIDTH), BF)],
        compiler_params=params(),
        name="pack",
    )(embeddings, labels)


def compact_kernel(got_ref, out_ref, offset_ref, rows, names, place):
    r = pl.program_id(0)

    @pl.when(r == 0)
    def _():
        place[0] = 0
        rows[:16] = jnp.zeros((16, WIDTH), BF)
        names[...] = jnp.zeros((8, SPAN), F32)

    offset = place[0]
    offset_ref[r] = offset
    lab = got_ref[0, CAP:, :LANES].astype(F32)[:8]
    count = jnp.sum((lab[:1] >= 0.0).astype(F32)).astype(jnp.int32)
    place[0] = offset + count
    base = pl.multiple_of(lax.div(offset, 16) * 16, 16)
    column = iota((PAIR, PAIR), 1)
    move = (iota((PAIR, PAIR), 0) == column + (offset - base)) & (column < count)
    moved = dot(move.astype(F32).astype(BF), got_ref[0]).astype(BF)
    rows[pl.ds(base, 16)] = rows[pl.ds(base, 16)] + moved[:16]
    rows[pl.ds(base + 16, PAIR - 16)] = moved[16:]
    held = jnp.concatenate([jnp.maximum(lab, 0.0), jnp.zeros((8, SPAN - LANES), F32)], axis=1)
    names[...] += pltpu.roll(held, offset, 1)

    @pl.when(r == TILE_ROWS - 1)
    def _():
        out_ref[:ROWS] = rows[:ROWS]
        out_ref[ROWS:, :ROWS] = jnp.broadcast_to(names[:1, :ROWS], (16, ROWS)).astype(BF)
        out_ref[ROWS:, ROWS:] = jnp.zeros((16, WIDTH - ROWS), BF)


def compact(got):
    return pl.pallas_call(
        compact_kernel,
        grid=(TILE_ROWS,),
        in_specs=[pl.BlockSpec((1, PAIR, WIDTH), lambda r: (r, 0, 0))],
        out_specs=[whole((BLOCK, WIDTH)), pl.BlockSpec(memory_space=pltpu.SMEM)],
        out_shape=[
            jax.ShapeDtypeStruct((BLOCK, WIDTH), BF),
            jax.ShapeDtypeStruct((TILE_ROWS,), jnp.int32),
        ],
        scratch_shapes=[
            pltpu.VMEM((ROWS + PAIR, WIDTH), BF),
            pltpu.VMEM((8, SPAN), F32),
            pltpu.SMEM((1,), jnp.int32),
        ],
        compiler_params=params(),
        name="compact",
    )(got)


def fold(tile):
    return tile.reshape(tile.shape[0] // 8, 8, tile.shape[1])


def merge(parts):
    top = functools.reduce(jnp.maximum, [p[0] for p in parts])
    factors = [jnp.exp2(p[0] - top) for p in parts]
    total = sum(p[1] * f for p, f in zip(parts, factors))
    weight = sum(p[2] * f for p, f in zip(parts, factors))
    return top, total, weight


def put_stats(ref, stats):
    for k, value in enumerate(stats):
        ref[k : k + 1] = value


def get_stats(ref):
    return tuple(ref[k : k + 1] for k in range(3))


def spread_names(block):
    names = block[ROWS:, :ROWS].astype(F32)[:1]
    return names, jnp.transpose(jnp.broadcast_to(names, (128, ROWS)))


def across(mark):
    return jnp.concatenate([mark] * (ROWS // 128), axis=1)


def gather_columns(top, total, weight):
    best = jnp.max(top, axis=0, keepdims=True)
    factor = jnp.exp2(top - best)
    return (
        best,
        jnp.sum(total * factor, axis=0, keepdims=True),
        jnp.sum(weight * factor, axis=0, keepdims=True),
    )


def own_kernel(block, out, scores):
    names, marks = spread_names(block)
    top = jnp.full((8, ROWS), FLOOR, F32)
    for start in range(0, ROWS, CHUNK):
        sims = dot_nt(block[start : start + CHUNK], block[:ROWS]) * SCALE2
        mask = (across(marks[start : start + CHUNK]) == names) & (
            iota((CHUNK, ROWS), 0) + start != iota((CHUNK, ROWS), 1)
        )
        sims = jnp.where(mask, sims, NEGATIVE)
        scores[start : start + CHUNK] = sims
        top = jnp.maximum(top, jnp.max(fold(sims), axis=0))
    total = jnp.zeros((8, ROWS), F32)
    weight = jnp.zeros((8, ROWS), F32)
    for start in range(0, ROWS, STRIP):
        sims = scores[start : start + STRIP]
        terms = jnp.exp2(fold(sims) - top)
        total += jnp.sum(terms, axis=0)
        weight += jnp.sum(terms * fold(sims), axis=0)
    put_stats(out, gather_columns(top, total, weight))


def own_pairs(block):
    return pl.pallas_call(
        own_kernel,
        out_shape=jax.ShapeDtypeStruct((8, ROWS), F32),
        in_specs=[pl.BlockSpec(memory_space=pltpu.VMEM)],
        out_specs=pl.BlockSpec(memory_space=pltpu.VMEM),
        scratch_shapes=[pltpu.VMEM((ROWS, ROWS), F32)],
        compiler_params=params(),
        cost_estimate=pl.CostEstimate(
            flops=2 * ROWS * ROWS * WIDTH,
            bytes_accessed=2 * BLOCK * WIDTH,
            transcendentals=ROWS * ROWS,
        ),
        name="own",
    )(block)


def pair_kernel(plan, blocks, old, half_ref, *refs):
    n, n_old = len(blocks), len(old)
    ins, olds = refs[:n], refs[n : n + n_old]
    outs = refs[n + n_old : n + n_old + n]
    held, marks, names, rows, tops, totals, weights, scores0, scores1, sems = refs[n + n_old + n :]
    scores = (scores0, scores1)
    place = {b: i for i, b in enumerate(blocks)}
    copies = [pltpu.make_async_copy(ins[i], held.at[i], sems.at[i]) for i in range(n)]
    for copy in copies:
        copy.start()
    lane = iota((1, 128), 1)
    empty = jnp.where(lane % 4 == 0, NEGATIVE, 0.0)
    for i in range(n):
        rows[i] = jnp.broadcast_to(empty, (ROWS, 128))
    tops[...] = jnp.full((n, 8, ROWS), FLOOR, F32)
    totals[...] = jnp.zeros((n, 8, ROWS), F32)
    weights[...] = jnp.zeros((n, 8, ROWS), F32)
    ready = set()

    def need(i):
        if i not in ready:
            ready.add(i)
            copies[i].wait()
            one, many = spread_names(held.at[i])
            names[i] = jnp.broadcast_to(one, (8, ROWS))
            marks[i] = many

    steps = []
    for k, (left, right, axis) in enumerate(plan):
        left, right = place[left], place[right]
        if axis is None:
            steps += [(k, left, right, 0, (left, right)), (k, left, right, HALF, (left, right))]
        else:
            half = half_ref[axis]
            first = jnp.where(half == 0, left, right)
            second = jnp.where(half == 0, right, left)
            start = pl.multiple_of(half * HALF, HALF)
            steps.append((k, first, second, start, (left, right)))

    def product(step, out):
        _, left, right, start, both = step
        for i in both:
            need(i)
        out[...] = dot_nt(held[left, pl.ds(start, HALF)], held[right, :ROWS])

    def reduce(step, data):
        k, left, right, start, _ = step
        name = names[right][:1]
        top = tops[right]
        peak = top
        for at in range(0, HALF, STRIP):
            here = pl.ds(start + at, STRIP)
            mask = across(marks[left, here]) == name
            sims = jnp.where(mask, data[at : at + STRIP] * SCALE2, NEGATIVE)
            data[at : at + STRIP] = sims
            peak = jnp.maximum(peak, jnp.max(fold(sims), axis=0))
            best = jnp.maximum(jnp.max(sims, axis=1, keepdims=True), FLOOR)
            terms = jnp.exp2(sims - best)
            total = jnp.sum(terms, axis=1, keepdims=True)
            weight = jnp.sum(terms * sims, axis=1, keepdims=True)
            rows[left, here] = jnp.where(
                lane == 4 * k,
                best,
                jnp.where(
                    lane == 4 * k + 1, total, jnp.where(lane == 4 * k + 2, weight, rows[left, here])
                ),
            )
        factor = jnp.exp2(top - peak)
        total = totals[right] * factor
        weight = weights[right] * factor
        for at in range(0, HALF, STRIP):
            sims = fold(data[at : at + STRIP])
            terms = jnp.exp2(sims - peak)
            total += jnp.sum(terms, axis=0)
            weight += jnp.sum(terms * sims, axis=0)
        tops[right] = peak
        totals[right] = total
        weights[right] = weight

    product(steps[0], scores[0])
    for t, step in enumerate(steps):
        if t + 1 < len(steps):
            product(steps[t + 1], scores[(t + 1) % 2])
        reduce(step, scores[t % 2])

    for i, b in enumerate(blocks):
        parts = [gather_columns(tops[i], totals[i], weights[i])]
        mine = [k for k, (left, right, axis) in enumerate(plan) if left == b or (axis is not None and right == b)]
        if mine:
            turned = jnp.transpose(rows[i])
            parts += [tuple(turned[4 * k + j : 4 * k + j + 1] for j in range(3)) for k in mine]
        if b in old:
            parts.append(get_stats(olds[old.index(b)]))
        put_stats(outs[i], merge(parts))


def pairs(plan, blocks, old, halves):
    names, n = list(blocks), len(blocks)
    steps = sum(2 if axis is None else 1 for _, _, axis in plan)
    anywhere = pl.BlockSpec(memory_space=pl.ANY)
    vmem = pl.BlockSpec(memory_space=pltpu.VMEM)
    return pl.pallas_call(
        functools.partial(pair_kernel, plan, names, list(old)),
        out_shape=[jax.ShapeDtypeStruct((8, ROWS), F32)] * n,
        in_specs=[pl.BlockSpec(memory_space=pltpu.SMEM)] + [anywhere] * n + [vmem] * len(old),
        out_specs=[vmem] * n,
        scratch_shapes=[
            pltpu.VMEM((n, BLOCK, WIDTH), BF),
            pltpu.VMEM((n, ROWS, 128), F32),
            pltpu.VMEM((n, 8, ROWS), F32),
            pltpu.VMEM((n, ROWS, 128), F32),
            pltpu.VMEM((n, 8, ROWS), F32),
            pltpu.VMEM((n, 8, ROWS), F32),
            pltpu.VMEM((n, 8, ROWS), F32),
            pltpu.VMEM((HALF, ROWS), F32),
            pltpu.VMEM((HALF, ROWS), F32),
            pltpu.SemaphoreType.DMA((n,)),
        ],
        compiler_params=params(),
        cost_estimate=pl.CostEstimate(
            flops=2 * steps * HALF * ROWS * WIDTH,
            bytes_accessed=2 * n * BLOCK * WIDTH,
            transcendentals=2 * steps * HALF * ROWS,
        ),
        name="pairs",
    )(halves, *blocks.values(), *old.values())


def spread_kernel(offset_ref, *refs):
    out_ref = refs[-1]
    top, total, weight = merge([get_stats(r) for r in refs[:-1]])
    best = top / SCALE2
    mean = weight / total / SCALE2
    row = iota((8, ROWS), 0)
    values = jnp.where(row == 0, best, jnp.where(row == 1, mean, 0.0))
    values = jnp.concatenate([values, jnp.zeros((8, SPAN - ROWS), F32)], axis=1)
    for r in range(TILE_ROWS):
        offset = offset_ref[r]
        out_ref[r] = pltpu.roll(values, lax.rem(SPAN - offset, SPAN), 1)[:, :LANES]


def spread(offsets, stats):
    return pl.pallas_call(
        spread_kernel,
        out_shape=jax.ShapeDtypeStruct((TILE_ROWS, 8, LANES), F32),
        in_specs=[pl.BlockSpec(memory_space=pltpu.SMEM)]
        + [pl.BlockSpec(memory_space=pltpu.VMEM)] * len(stats),
        out_specs=pl.BlockSpec(memory_space=pltpu.VMEM),
        compiler_params=params(),
        name="spread",
    )(offsets, *stats)


def unpack_kernel(back_ref, lab_ref, rank_ref, best_ref, mean_ref, flag_ref):
    owner = lax.shift_right_logical(lab_ref[...], GROUP_SHIFT)
    found = jnp.zeros((24, ROWS), F32)
    for g in range(TILE_ROWS):
        slot = jnp.where(owner == g, rank_ref[...], -1)
        pick = (iota((LANES, ROWS), 0) == slot).astype(F32).astype(BF)
        values = back_ref[g]
        high = values.astype(BF).astype(F32)
        mid = (values - high).astype(BF).astype(F32)
        low = values - high - mid
        found += dot(jnp.concatenate([high, mid, low], axis=0).astype(BF), pick)
    found = found[:8] + (found[8:16] + found[16:])
    best = found[:1]
    best_ref[...] = best.reshape(ROWS)
    mean_ref[...] = found[1:2].reshape(ROWS)
    flag_ref[...] = (1.0 / (1.0 + jnp.exp(-SHARPNESS * (best - THRESHOLD)))).reshape(ROWS)


def unpack(back, labels, rank):
    return pl.pallas_call(
        unpack_kernel,
        out_shape=[jax.ShapeDtypeStruct((ROWS,), F32)] * 3,
        in_specs=[pl.BlockSpec(memory_space=pltpu.VMEM)] * 3,
        out_specs=[pl.BlockSpec(memory_space=pltpu.VMEM)] * 3,
        compiler_params=params(),
        name="unpack",
    )(back, labels, rank)


def shift(array, dx, dy):
    moves = []
    for tr in range(TILE_ROWS):
        sign = 1 - 2 * (tr % 2)
        for x in range(SIDE):
            for y in range(SIDE):
                to = ((x + sign * dx) % SIDE) * SIDE + (y + sign * dy) % SIDE
                base = tr * SIDE * SIDE
                moves.append((base + x * SIDE + y, base + to))
    return lax.ppermute(array, ("tr", "tc"), moves)


PLACES = {"O": (0, 0), "A": (1, 0), "B": (2, 0), "C": (0, 1), "D": (0, -1), "E": (0, 2)}
NEAR = [("O", "A", None), ("O", "C", None), ("A", "C", None), ("D", "A", None), ("C", "D", 1)]
FAR = [("B", "O", 0), ("B", "C", None), ("E", "A", None), ("E", "B", 0)]


def per_device(embeddings, labels):
    lab = labels.reshape(1, ROWS)
    tc = lax.axis_index("tc")
    halves = jnp.stack([tc // (2 * SIDE), (tc % SIDE) // 2]).astype(jnp.int32)
    packed, rank = pack(embeddings, lab)
    got = lax.all_to_all(packed, "tr", split_axis=0, concat_axis=0, tiled=True)
    mine, offsets = compact(got)
    a = shift(mine, -1, 0)
    c = shift(mine, 0, -1)
    d = shift(mine, 0, 1)
    own = own_pairs(mine)
    b = shift(a, -1, 0)
    e = shift(d, 0, 1)
    blocks = {"O": mine, "A": a, "C": c, "D": d}
    stats = dict(zip(blocks, pairs(NEAR, blocks, {"O": own}, halves)))
    blocks = {"O": mine, "B": b, "C": c, "E": e, "A": a}
    far = pairs(FAR, blocks, {q: stats[q] for q in "OAC"}, halves)
    stats.update(zip(blocks, far))
    parts = [stats["O"]] + [shift(stats[q], *PLACES[q]) for q in "ABCDE"]
    sent = spread(offsets, parts)
    back = lax.all_to_all(sent, "tr", split_axis=0, concat_axis=0, tiled=True)
    return unpack(back, lab, rank)


def solution(mesh):
    files = P(("tr", "tc"))
    return jax.shard_map(
        per_device,
        mesh=mesh,
        in_specs=(P(("tr", "tc"), None), files),
        out_specs=(files, files, files),
        check_vma=False,
    )
```

```python
import functools

import jax
import jax.numpy as jnp
from jax import lax
from jax.experimental import pallas as pl
from jax.experimental.pallas import tpu as pltpu
from jax.sharding import PartitionSpec as P

GROUP_SHIFT = 2
TILE_ROWS = 8
SIDE = 4
ROWS = 768
WIDTH = 1024
PIECE = 512
CAP = 288
TAIL = 16
PAIR = CAP + TAIL
LANES = 384
BLOCK = ROWS + TAIL
SPAN = 1152
EPSILON = 1e-06
THRESHOLD = 0.3
SHARPNESS = 50.0
SCALE2 = 256.0 * 1.4426950408889634
NEGATIVE = -1e30
FLOOR = -5e29
CHUNK = 256
HALF = 384
STRIP = 32
VMEM = 56 * 1024 * 1024
BF = jnp.bfloat16
F32 = jnp.float32


def iota(shape, axis):
    return lax.broadcasted_iota(jnp.int32, shape, axis)


def dot(a, b):
    return lax.dot_general(a, b, (((1,), (0,)), ((), ())), preferred_element_type=F32)


def dot_nt(a, b):
    return lax.dot_general(a, b, (((1,), (1,)), ((), ())), preferred_element_type=F32)


def params(**more):
    return pltpu.CompilerParams(vmem_limit_bytes=VMEM, **more)


def whole(shape):
    return pl.BlockSpec(shape, lambda *_: (0,) * len(shape))


def vmem():
    return pl.BlockSpec(memory_space=pltpu.VMEM)


def smem():
    return pl.BlockSpec(memory_space=pltpu.SMEM)


def pick(lab_ref, rank_ref, g, slots):
    owner = lax.shift_right_logical(lab_ref[...].reshape(1, ROWS), GROUP_SHIFT)
    slot = jnp.where(owner == g, rank_ref[...], -1)
    return (iota((slots, ROWS), 0) == slot).astype(F32).astype(BF)


def pack_first_kernel(emb_ref, lab_ref, out_ref, rank_ref, rest_ref, unit):
    g = pl.program_id(0)
    lab = lab_ref[...].reshape(1, ROWS)

    @pl.when(g == 0)
    def _():
        values = emb_ref[...].astype(F32)
        total = jnp.sum(values * values, axis=1, keepdims=True)
        rows = (values * lax.rsqrt(total + EPSILON)).astype(BF)
        unit[...] = rows[:, :PIECE]
        rest_ref[...] = rows[:, PIECE:]
        owner = lax.shift_right_logical(lab, GROUP_SHIFT)
        onehot = (iota((TILE_ROWS, ROWS), 0) == owner).astype(F32)
        before = (iota((ROWS, ROWS), 0) < iota((ROWS, ROWS), 1)).astype(F32).astype(BF)
        seen = dot(onehot.astype(BF), before)
        rank_ref[...] = jnp.sum(onehot * seen, axis=0, keepdims=True).astype(jnp.int32)

    chosen = pick(lab_ref, rank_ref, g, LANES)
    out_ref[0] = dot(chosen[:PAIR], unit[...]).astype(BF)
    marks = jnp.broadcast_to(lab.astype(F32) + 1.0, (TAIL, ROWS)).astype(BF)
    out_ref[0, CAP:, :LANES] = (dot_nt(marks, chosen) - 1.0).astype(BF)
    out_ref[0, CAP:, LANES:] = jnp.zeros((TAIL, PIECE - LANES), BF)


def pack_first(embeddings, labels):
    return pl.pallas_call(
        pack_first_kernel,
        grid=(TILE_ROWS,),
        in_specs=[whole((ROWS, WIDTH)), whole((ROWS,))],
        out_specs=[
            pl.BlockSpec((1, PAIR, PIECE), lambda g: (g, 0, 0)),
            whole((1, ROWS)),
            whole((ROWS, WIDTH - PIECE)),
        ],
        out_shape=[
            jax.ShapeDtypeStruct((TILE_ROWS, PAIR, PIECE), BF),
            jax.ShapeDtypeStruct((1, ROWS), jnp.int32),
            jax.ShapeDtypeStruct((ROWS, WIDTH - PIECE), BF),
        ],
        scratch_shapes=[pltpu.VMEM((ROWS, PIECE), BF)],
        compiler_params=params(),
        name="pack_first",
    )(embeddings, labels)


def pack_rest_kernel(unit_ref, lab_ref, rank_ref, out_ref):
    chosen = pick(lab_ref, rank_ref, pl.program_id(0), CAP)
    out_ref[0] = dot(chosen, unit_ref[...]).astype(BF)


def pack_rest(unit, labels, rank):
    width = unit.shape[1]
    return pl.pallas_call(
        pack_rest_kernel,
        grid=(TILE_ROWS,),
        in_specs=[whole((ROWS, width)), whole((ROWS,)), whole((1, ROWS))],
        out_specs=pl.BlockSpec((1, CAP, width), lambda g: (g, 0, 0)),
        out_shape=jax.ShapeDtypeStruct((TILE_ROWS, CAP, width), BF),
        compiler_params=params(),
        cost_estimate=pl.CostEstimate(
            flops=2 * TILE_ROWS * CAP * ROWS * width,
            bytes_accessed=2 * TILE_ROWS * CAP * width,
            transcendentals=0,
        ),
        name="pack_rest",
    )(unit, labels, rank)


def close_gaps(got_ref, rows, offsets, counts):
    sent = got_ref.shape[1]
    rows[:16] = jnp.zeros((16, rows.shape[1]), BF)
    column = iota((PAIR, sent), 1)
    apart = iota((PAIR, sent), 0) - column
    for r in range(TILE_ROWS):
        base = pl.multiple_of(lax.shift_right_logical(offsets[r], 4) * 16, 16)
        move = (apart == offsets[r] - base) & (column < counts[r])
        moved = dot(move.astype(F32).astype(BF), got_ref[r]).astype(BF)
        rows[pl.ds(base, 16)] = rows[pl.ds(base, 16)] + moved[:16]
        rows[pl.ds(base + 16, PAIR - 16)] = moved[16:]


def compact_first_kernel(got_ref, out_ref, place_ref, rows):
    names = jnp.zeros((8, SPAN), F32)
    offset = jnp.int32(0)
    offsets, counts = [], []
    for r in range(TILE_ROWS):
        lab = got_ref[r, CAP:, :LANES].astype(F32)[:8]
        count = jnp.sum((lab[:1] >= 0.0).astype(F32)).astype(jnp.int32)
        held = jnp.concatenate(
            [jnp.maximum(lab, 0.0), jnp.zeros((8, SPAN - LANES), F32)], axis=1
        )
        names += pltpu.roll(held, offset, 1)
        place_ref[r] = offset
        place_ref[TILE_ROWS + r] = count
        offsets.append(offset)
        counts.append(count)
        offset = offset + count
    close_gaps(got_ref, rows, offsets, counts)
    out_ref[:ROWS] = rows[:ROWS]
    second = jnp.concatenate(
        [names[:, PIECE:ROWS], jnp.zeros((8, 2 * PIECE - ROWS), F32)], axis=1
    )
    out_ref[ROWS:] = jnp.concatenate([names[:, :PIECE], second], axis=0).astype(BF)


def compact_first(got):
    return pl.pallas_call(
        compact_first_kernel,
        in_specs=[vmem()],
        out_specs=[vmem(), smem()],
        out_shape=[
            jax.ShapeDtypeStruct((BLOCK, PIECE), BF),
            jax.ShapeDtypeStruct((2 * TILE_ROWS,), jnp.int32),
        ],
        scratch_shapes=[pltpu.VMEM((ROWS + PAIR, PIECE), BF)],
        compiler_params=params(),
        name="compact_first",
    )(got)


def compact_rest_kernel(place_ref, got_ref, out_ref, rows):
    places = [place_ref[i] for i in range(2 * TILE_ROWS)]
    close_gaps(got_ref, rows, places[:TILE_ROWS], places[TILE_ROWS:])
    out_ref[...] = rows[:ROWS]


def compact_rest(place, got):
    width = got.shape[2]
    return pl.pallas_call(
        compact_rest_kernel,
        in_specs=[smem(), vmem()],
        out_specs=vmem(),
        out_shape=jax.ShapeDtypeStruct((ROWS, width), BF),
        scratch_shapes=[pltpu.VMEM((ROWS + PAIR, width), BF)],
        compiler_params=params(),
        name="compact_rest",
    )(place, got)


def fold(tile):
    return tile.reshape(tile.shape[0] // 8, 8, tile.shape[1])


def merge(parts):
    top = functools.reduce(jnp.maximum, [p[0] for p in parts])
    factors = [jnp.exp2(p[0] - top) for p in parts]
    total = sum(p[1] * f for p, f in zip(parts, factors))
    weight = sum(p[2] * f for p, f in zip(parts, factors))
    return top, total, weight


def put_stats(ref, stats):
    for k, value in enumerate(stats):
        ref[k : k + 1] = value


def get_stats(ref):
    return tuple(ref[k : k + 1] for k in range(3))


def spread_names(block):
    tail = block[ROWS:].astype(F32)
    names = jnp.concatenate([tail[:1], tail[8:9, : ROWS - PIECE]], axis=1)
    return names, jnp.transpose(jnp.broadcast_to(names, (128, ROWS)))


def across(mark):
    return jnp.concatenate([mark] * (ROWS // 128), axis=1)


def gather_columns(top, total, weight):
    best = jnp.max(top, axis=0, keepdims=True)
    factor = jnp.exp2(top - best)
    return (
        best,
        jnp.sum(total * factor, axis=0, keepdims=True),
        jnp.sum(weight * factor, axis=0, keepdims=True),
    )


def own_kernel(block, rest, out, scores):
    names, marks = spread_names(block)
    top = jnp.full((8, ROWS), FLOOR, F32)
    for start in range(0, ROWS, CHUNK):
        sims = dot_nt(block[start : start + CHUNK], block[:ROWS])
        sims = (sims + dot_nt(rest[start : start + CHUNK], rest[...])) * SCALE2
        mask = (across(marks[start : start + CHUNK]) == names) & (
            iota((CHUNK, ROWS), 0) + start != iota((CHUNK, ROWS), 1)
        )
        sims = jnp.where(mask, sims, NEGATIVE)
        scores[start : start + CHUNK] = sims
        top = jnp.maximum(top, jnp.max(fold(sims), axis=0))
    total = jnp.zeros((8, ROWS), F32)
    weight = jnp.zeros((8, ROWS), F32)
    for start in range(0, ROWS, STRIP):
        sims = scores[start : start + STRIP]
        terms = jnp.exp2(fold(sims) - top)
        total += jnp.sum(terms, axis=0)
        weight += jnp.sum(terms * fold(sims), axis=0)
    put_stats(out, gather_columns(top, total, weight))


def own_pairs(block, rest):
    return pl.pallas_call(
        own_kernel,
        out_shape=jax.ShapeDtypeStruct((8, ROWS), F32),
        in_specs=[vmem(), vmem()],
        out_specs=vmem(),
        scratch_shapes=[pltpu.VMEM((ROWS, ROWS), F32)],
        compiler_params=params(),
        cost_estimate=pl.CostEstimate(
            flops=2 * ROWS * ROWS * WIDTH,
            bytes_accessed=2 * BLOCK * WIDTH,
            transcendentals=ROWS * ROWS,
        ),
        name="own",
    )(block, rest)


def pair_kernel(plan, blocks, old, half_ref, *refs):
    n, n_old = len(blocks), len(old)
    ins, rests, olds = refs[:n], refs[n : 2 * n], refs[2 * n : 2 * n + n_old]
    outs = refs[2 * n + n_old : 3 * n + n_old]
    held, held2, marks, names, rows, tops, totals, weights, scores0, scores1, sems = refs[
        3 * n + n_old :
    ]
    scores = (scores0, scores1)
    place = {b: i for i, b in enumerate(blocks)}
    copies = [
        (
            pltpu.make_async_copy(ins[i], held.at[i], sems.at[2 * i]),
            pltpu.make_async_copy(rests[i], held2.at[i], sems.at[2 * i + 1]),
        )
        for i in range(n)
    ]
    for first, second in copies:
        first.start()
        second.start()
    lane = iota((1, 128), 1)
    empty = jnp.where(lane % 4 == 0, NEGATIVE, 0.0)
    for i in range(n):
        rows[i] = jnp.broadcast_to(empty, (ROWS, 128))
    tops[...] = jnp.full((n, 8, ROWS), FLOOR, F32)
    totals[...] = jnp.zeros((n, 8, ROWS), F32)
    weights[...] = jnp.zeros((n, 8, ROWS), F32)
    ready = set()

    def need(i):
        if i not in ready:
            ready.add(i)
            copies[i][0].wait()
            copies[i][1].wait()
            one, many = spread_names(held.at[i])
            names[i] = jnp.broadcast_to(one, (8, ROWS))
            marks[i] = many

    steps = []
    for k, (left, right, axis) in enumerate(plan):
        left, right = place[left], place[right]
        if axis is None:
            steps += [(k, left, right, 0, (left, right)), (k, left, right, HALF, (left, right))]
        else:
            half = half_ref[axis]
            first = jnp.where(half == 0, left, right)
            second = jnp.where(half == 0, right, left)
            start = pl.multiple_of(half * HALF, HALF)
            steps.append((k, first, second, start, (left, right)))

    def product(step, out):
        _, left, right, start, both = step
        for i in both:
            need(i)
        here = pl.ds(start, HALF)
        out[...] = dot_nt(held[left, here], held[right, :ROWS]) + dot_nt(
            held2[left, here], held2[right]
        )

    def reduce(step, data):
        k, left, right, start, _ = step
        name = names[right][:1]
        top = tops[right]
        peak = top
        for at in range(0, HALF, STRIP):
            here = pl.ds(start + at, STRIP)
            mask = across(marks[left, here]) == name
            sims = jnp.where(mask, data[at : at + STRIP] * SCALE2, NEGATIVE)
            data[at : at + STRIP] = sims
            peak = jnp.maximum(peak, jnp.max(fold(sims), axis=0))
            best = jnp.maximum(jnp.max(sims, axis=1, keepdims=True), FLOOR)
            terms = jnp.exp2(sims - best)
            total = jnp.sum(terms, axis=1, keepdims=True)
            weight = jnp.sum(terms * sims, axis=1, keepdims=True)
            rows[left, here] = jnp.where(
                lane == 4 * k,
                best,
                jnp.where(
                    lane == 4 * k + 1, total, jnp.where(lane == 4 * k + 2, weight, rows[left, here])
                ),
            )
        factor = jnp.exp2(top - peak)
        total = totals[right] * factor
        weight = weights[right] * factor
        for at in range(0, HALF, STRIP):
            sims = fold(data[at : at + STRIP])
            terms = jnp.exp2(sims - peak)
            total += jnp.sum(terms, axis=0)
            weight += jnp.sum(terms * sims, axis=0)
        tops[right] = peak
        totals[right] = total
        weights[right] = weight

    product(steps[0], scores[0])
    for t, step in enumerate(steps):
        if t + 1 < len(steps):
            product(steps[t + 1], scores[(t + 1) % 2])
        reduce(step, scores[t % 2])

    for i, b in enumerate(blocks):
        parts = [gather_columns(tops[i], totals[i], weights[i])]
        mine = [k for k, (left, right, axis) in enumerate(plan) if left == b or (axis is not None and right == b)]
        if mine:
            turned = jnp.transpose(rows[i])
            parts += [tuple(turned[4 * k + j : 4 * k + j + 1] for j in range(3)) for k in mine]
        if b in old:
            parts.append(get_stats(olds[old.index(b)]))
        put_stats(outs[i], merge(parts))


def pairs(plan, blocks, old, halves):
    names, n = list(blocks), len(blocks)
    steps = sum(2 if axis is None else 1 for _, _, axis in plan)
    anywhere = pl.BlockSpec(memory_space=pl.ANY)
    return pl.pallas_call(
        functools.partial(pair_kernel, plan, names, list(old)),
        out_shape=[jax.ShapeDtypeStruct((8, ROWS), F32)] * n,
        in_specs=[smem()] + [anywhere] * (2 * n) + [vmem()] * len(old),
        out_specs=[vmem()] * n,
        scratch_shapes=[
            pltpu.VMEM((n, BLOCK, PIECE), BF),
            pltpu.VMEM((n, ROWS, WIDTH - PIECE), BF),
            pltpu.VMEM((n, ROWS, 128), F32),
            pltpu.VMEM((n, 8, ROWS), F32),
            pltpu.VMEM((n, ROWS, 128), F32),
            pltpu.VMEM((n, 8, ROWS), F32),
            pltpu.VMEM((n, 8, ROWS), F32),
            pltpu.VMEM((n, 8, ROWS), F32),
            pltpu.VMEM((HALF, ROWS), F32),
            pltpu.VMEM((HALF, ROWS), F32),
            pltpu.SemaphoreType.DMA((2 * n,)),
        ],
        compiler_params=params(),
        cost_estimate=pl.CostEstimate(
            flops=2 * steps * HALF * ROWS * WIDTH,
            bytes_accessed=2 * n * BLOCK * WIDTH,
            transcendentals=2 * steps * HALF * ROWS,
        ),
        name="pairs",
    )(halves, *[b[0] for b in blocks.values()], *[b[1] for b in blocks.values()], *old.values())


def spread_kernel(offset_ref, *refs):
    out_ref = refs[-1]
    top, total, weight = merge([get_stats(r) for r in refs[:-1]])
    best = top / SCALE2
    mean = weight / total / SCALE2
    row = iota((8, ROWS), 0)
    values = jnp.where(row == 0, best, jnp.where(row == 1, mean, 0.0))
    values = jnp.concatenate([values, jnp.zeros((8, SPAN - ROWS), F32)], axis=1)
    for r in range(TILE_ROWS):
        offset = offset_ref[r]
        out_ref[r] = pltpu.roll(values, lax.rem(SPAN - offset, SPAN), 1)[:, :LANES]


def spread(offsets, stats):
    return pl.pallas_call(
        spread_kernel,
        out_shape=jax.ShapeDtypeStruct((TILE_ROWS, 8, LANES), F32),
        in_specs=[pl.BlockSpec(memory_space=pltpu.SMEM)]
        + [pl.BlockSpec(memory_space=pltpu.VMEM)] * len(stats),
        out_specs=pl.BlockSpec(memory_space=pltpu.VMEM),
        compiler_params=params(),
        name="spread",
    )(offsets, *stats)


def unpack_kernel(back_ref, lab_ref, rank_ref, best_ref, mean_ref, flag_ref):
    found = jnp.zeros((24, ROWS), F32)
    for g in range(TILE_ROWS):
        chosen = pick(lab_ref, rank_ref, g, LANES)
        values = back_ref[g]
        high = values.astype(BF).astype(F32)
        mid = (values - high).astype(BF).astype(F32)
        low = values - high - mid
        found += dot(jnp.concatenate([high, mid, low], axis=0).astype(BF), chosen)
    found = found[:8] + (found[8:16] + found[16:])
    best = found[:1]
    best_ref[...] = best.reshape(ROWS)
    mean_ref[...] = found[1:2].reshape(ROWS)
    flag_ref[...] = (1.0 / (1.0 + jnp.exp(-SHARPNESS * (best - THRESHOLD)))).reshape(ROWS)


def unpack(back, labels, rank):
    return pl.pallas_call(
        unpack_kernel,
        out_shape=[jax.ShapeDtypeStruct((ROWS,), F32)] * 3,
        in_specs=[pl.BlockSpec(memory_space=pltpu.VMEM)] * 3,
        out_specs=[pl.BlockSpec(memory_space=pltpu.VMEM)] * 3,
        compiler_params=params(),
        name="unpack",
    )(back, labels, rank)


def shift(array, dx, dy):
    moves = []
    for tr in range(TILE_ROWS):
        sign = 1 - 2 * (tr % 2)
        for x in range(SIDE):
            for y in range(SIDE):
                to = ((x + sign * dx) % SIDE) * SIDE + (y + sign * dy) % SIDE
                base = tr * SIDE * SIDE
                moves.append((base + x * SIDE + y, base + to))
    return lax.ppermute(array, ("tr", "tc"), moves)


PLACES = {"O": (0, 0), "A": (1, 0), "B": (2, 0), "C": (0, 1), "D": (0, -1), "E": (0, 2)}
FIRST = [("O", "A", None)]
NEAR = [("O", "C", None), ("A", "C", None), ("D", "A", None), ("C", "D", 1)]
FAR = [("B", "O", 0), ("B", "C", None), ("E", "A", None), ("E", "B", 0)]


def per_device(embeddings, labels):
    tie = lax.optimization_barrier
    tc = lax.axis_index("tc")
    halves = jnp.stack([tc // (2 * SIDE), (tc % SIDE) // 2]).astype(jnp.int32)

    def exchange(packed):
        return lax.all_to_all(packed, "tr", split_axis=0, concat_axis=0, tiled=True)

    packed, rank, unit = pack_first(embeddings, labels)
    got = exchange(packed)
    packed = pack_rest(unit, labels, rank)
    packed, got = tie((packed, got))
    got_rest = exchange(packed)
    mine, place = compact_first(got)
    a, c, d = shift(mine, -1, 0), shift(mine, 0, -1), shift(mine, 0, 1)
    b, e = shift(a, -1, 0), shift(d, 0, 1)
    got_rest, a, b, c, d, e = tie((got_rest, a, b, c, d, e))
    mine2 = compact_rest(place, got_rest)
    a2, c2, d2 = shift(mine2, -1, 0), shift(mine2, 0, -1), shift(mine2, 0, 1)
    own = own_pairs(mine, mine2)
    a2, own, halves = tie((a2, own, halves))
    b2 = shift(a2, -1, 0)
    blocks = {"O": (mine, mine2), "A": (a, a2)}
    stats = dict(zip(blocks, pairs(FIRST, blocks, {"O": own}, halves)))
    d2, stats["O"] = tie((d2, stats["O"]))
    e2 = shift(d2, 0, 1)
    blocks.update(C=(c, c2), D=(d, d2))
    stats.update(zip(blocks, pairs(NEAR, blocks, stats, halves)))
    blocks.update(B=(b, b2), E=(e, e2))
    del blocks["D"]
    far = pairs(FAR, blocks, {q: stats[q] for q in "OAC"}, halves)
    stats.update(zip(blocks, far))
    parts = [stats["O"]] + [shift(stats[q], *PLACES[q]) for q in "ABCDE"]
    sent = spread(place, parts)
    back = exchange(sent)
    return unpack(back, labels, rank)


def solution(mesh):
    files = P(("tr", "tc"))
    return jax.shard_map(
        per_device,
        mesh=mesh,
        in_specs=(P(("tr", "tc"), None), files),
        out_specs=(files, files, files),
        check_vma=False,
    )
```

```python
import functools

import jax
import jax.numpy as jnp
from jax import lax
from jax.experimental import pallas as pl
from jax.experimental.pallas import tpu as pltpu
from jax.sharding import PartitionSpec as P

GROUP_SHIFT = 2
TILE_ROWS = 8
SIDE = 4
ROWS = 768
WIDTH = 1024
PIECE = 512
CAP = 288
TAIL = 16
PAIR = CAP + TAIL
LANES = 384
BLOCK = ROWS + TAIL
SPAN = 1152
EPSILON = 1e-06
THRESHOLD = 0.3
SHARPNESS = 50.0
SCALE2 = 256.0 * 1.4426950408889634
NEGATIVE = -1e30
FLOOR = -5e29
CHUNK = 256
HALF = 384
STRIP = 32
VMEM = 24 * 1024 * 1024
BF = jnp.bfloat16
F32 = jnp.float32


def iota(shape, axis):
    return lax.broadcasted_iota(jnp.int32, shape, axis)


def dot(a, b):
    return lax.dot_general(a, b, (((1,), (0,)), ((), ())), preferred_element_type=F32)


def dot_nt(a, b):
    return lax.dot_general(a, b, (((1,), (1,)), ((), ())), preferred_element_type=F32)


def params(**more):
    return pltpu.CompilerParams(vmem_limit_bytes=VMEM, **more)


def whole(shape):
    return pl.BlockSpec(shape, lambda *_: (0,) * len(shape))


def vmem():
    return pl.BlockSpec(memory_space=pltpu.VMEM)


def smem():
    return pl.BlockSpec(memory_space=pltpu.SMEM)


def pick(lab_ref, rank_ref, g, slots):
    owner = lax.shift_right_logical(lab_ref[...].reshape(1, ROWS), GROUP_SHIFT)
    slot = jnp.where(owner == g, rank_ref[...], -1)
    return (iota((slots, ROWS), 0) == slot).astype(F32).astype(BF)


def pack_first_kernel(emb_ref, lab_ref, out_ref, rank_ref, rest_ref, unit):
    g = pl.program_id(0)
    lab = lab_ref[...].reshape(1, ROWS)

    @pl.when(g == 0)
    def _():
        values = emb_ref[...].astype(F32)
        total = jnp.sum(values * values, axis=1, keepdims=True)
        rows = (values * lax.rsqrt(total + EPSILON)).astype(BF)
        unit[...] = rows[:, :PIECE]
        rest_ref[...] = rows[:, PIECE:]
        owner = lax.shift_right_logical(lab, GROUP_SHIFT)
        onehot = (iota((TILE_ROWS, ROWS), 0) == owner).astype(F32)
        before = (iota((ROWS, ROWS), 0) < iota((ROWS, ROWS), 1)).astype(F32).astype(BF)
        seen = dot(onehot.astype(BF), before)
        rank_ref[...] = jnp.sum(onehot * seen, axis=0, keepdims=True).astype(jnp.int32)

    chosen = pick(lab_ref, rank_ref, g, LANES)
    out_ref[0] = dot(chosen[:PAIR], unit[...]).astype(BF)
    marks = jnp.broadcast_to(lab.astype(F32) + 1.0, (TAIL, ROWS)).astype(BF)
    out_ref[0, CAP:, :LANES] = (dot_nt(marks, chosen) - 1.0).astype(BF)
    out_ref[0, CAP:, LANES:] = jnp.zeros((TAIL, PIECE - LANES), BF)


def pack_first(embeddings, labels):
    return pl.pallas_call(
        pack_first_kernel,
        grid=(TILE_ROWS,),
        in_specs=[whole((ROWS, WIDTH)), whole((ROWS,))],
        out_specs=[
            pl.BlockSpec((1, PAIR, PIECE), lambda g: (g, 0, 0)),
            whole((1, ROWS)),
            whole((ROWS, WIDTH - PIECE)),
        ],
        out_shape=[
            jax.ShapeDtypeStruct((TILE_ROWS, PAIR, PIECE), BF),
            jax.ShapeDtypeStruct((1, ROWS), jnp.int32),
            jax.ShapeDtypeStruct((ROWS, WIDTH - PIECE), BF),
        ],
        scratch_shapes=[pltpu.VMEM((ROWS, PIECE), BF)],
        compiler_params=params(),
        name="pack_first",
    )(embeddings, labels)


def pack_rest_kernel(unit_ref, lab_ref, rank_ref, out_ref):
    chosen = pick(lab_ref, rank_ref, pl.program_id(0), CAP)
    out_ref[0] = dot(chosen, unit_ref[...]).astype(BF)


def pack_rest(unit, labels, rank):
    width = unit.shape[1]
    return pl.pallas_call(
        pack_rest_kernel,
        grid=(TILE_ROWS,),
        in_specs=[whole((ROWS, width)), whole((ROWS,)), whole((1, ROWS))],
        out_specs=pl.BlockSpec((1, CAP, width), lambda g: (g, 0, 0)),
        out_shape=jax.ShapeDtypeStruct((TILE_ROWS, CAP, width), BF),
        compiler_params=params(),
        cost_estimate=pl.CostEstimate(
            flops=2 * TILE_ROWS * CAP * ROWS * width,
            bytes_accessed=2 * TILE_ROWS * CAP * width,
            transcendentals=0,
        ),
        name="pack_rest",
    )(unit, labels, rank)


def close_gaps(got_ref, rows, offsets, counts):
    sent = got_ref.shape[1]
    rows[:16] = jnp.zeros((16, rows.shape[1]), BF)
    column = iota((PAIR, sent), 1)
    apart = iota((PAIR, sent), 0) - column
    for r in range(TILE_ROWS):
        base = pl.multiple_of(lax.shift_right_logical(offsets[r], 4) * 16, 16)
        move = (apart == offsets[r] - base) & (column < counts[r])
        moved = dot(move.astype(F32).astype(BF), got_ref[r]).astype(BF)
        rows[pl.ds(base, 16)] = rows[pl.ds(base, 16)] + moved[:16]
        rows[pl.ds(base + 16, PAIR - 16)] = moved[16:]


def compact_first_kernel(got_ref, out_ref, place_ref, rows):
    names = jnp.zeros((8, SPAN), F32)
    offset = jnp.int32(0)
    offsets, counts = [], []
    for r in range(TILE_ROWS):
        lab = got_ref[r, CAP:, :LANES].astype(F32)[:8]
        count = jnp.sum((lab[:1] >= 0.0).astype(F32)).astype(jnp.int32)
        held = jnp.concatenate(
            [jnp.maximum(lab, 0.0), jnp.zeros((8, SPAN - LANES), F32)], axis=1
        )
        names += pltpu.roll(held, offset, 1)
        place_ref[r] = offset
        place_ref[TILE_ROWS + r] = count
        offsets.append(offset)
        counts.append(count)
        offset = offset + count
    close_gaps(got_ref, rows, offsets, counts)
    out_ref[:ROWS] = rows[:ROWS]
    second = jnp.concatenate(
        [names[:, PIECE:ROWS], jnp.zeros((8, 2 * PIECE - ROWS), F32)], axis=1
    )
    out_ref[ROWS:] = jnp.concatenate([names[:, :PIECE], second], axis=0).astype(BF)


def compact_first(got):
    return pl.pallas_call(
        compact_first_kernel,
        in_specs=[vmem()],
        out_specs=[vmem(), smem()],
        out_shape=[
            jax.ShapeDtypeStruct((BLOCK, PIECE), BF),
            jax.ShapeDtypeStruct((2 * TILE_ROWS,), jnp.int32),
        ],
        scratch_shapes=[pltpu.VMEM((ROWS + PAIR, PIECE), BF)],
        compiler_params=params(),
        name="compact_first",
    )(got)


def compact_rest_kernel(place_ref, got_ref, out_ref, rows):
    places = [place_ref[i] for i in range(2 * TILE_ROWS)]
    close_gaps(got_ref, rows, places[:TILE_ROWS], places[TILE_ROWS:])
    out_ref[...] = rows[:ROWS]


def compact_rest(place, got):
    width = got.shape[2]
    return pl.pallas_call(
        compact_rest_kernel,
        in_specs=[smem(), vmem()],
        out_specs=vmem(),
        out_shape=jax.ShapeDtypeStruct((ROWS, width), BF),
        scratch_shapes=[pltpu.VMEM((ROWS + PAIR, width), BF)],
        compiler_params=params(),
        name="compact_rest",
    )(place, got)


def fold(tile):
    return tile.reshape(tile.shape[0] // 8, 8, tile.shape[1])


def merge(parts):
    top = functools.reduce(jnp.maximum, [p[0] for p in parts])
    factors = [jnp.exp2(p[0] - top) for p in parts]
    total = sum(p[1] * f for p, f in zip(parts, factors))
    weight = sum(p[2] * f for p, f in zip(parts, factors))
    return top, total, weight


def put_stats(ref, stats):
    for k, value in enumerate(stats):
        ref[k : k + 1] = value


def get_stats(ref):
    return tuple(ref[k : k + 1] for k in range(3))


def spread_names(block):
    tail = block[ROWS:].astype(F32)
    names = jnp.concatenate([tail[:1], tail[8:9, : ROWS - PIECE]], axis=1)
    return names, jnp.transpose(jnp.broadcast_to(names, (128, ROWS)))


def across(mark):
    return jnp.concatenate([mark] * (ROWS // 128), axis=1)


def gather_columns(top, total, weight):
    best = jnp.max(top, axis=0, keepdims=True)
    factor = jnp.exp2(top - best)
    return (
        best,
        jnp.sum(total * factor, axis=0, keepdims=True),
        jnp.sum(weight * factor, axis=0, keepdims=True),
    )


def own_kernel(block, rest, out, scores):
    names, marks = spread_names(block)
    top = jnp.full((8, ROWS), FLOOR, F32)
    for start in range(0, ROWS, CHUNK):
        sims = dot_nt(block[start : start + CHUNK], block[:ROWS])
        sims = (sims + dot_nt(rest[start : start + CHUNK], rest[...])) * SCALE2
        mask = (across(marks[start : start + CHUNK]) == names) & (
            iota((CHUNK, ROWS), 0) + start != iota((CHUNK, ROWS), 1)
        )
        sims = jnp.where(mask, sims, NEGATIVE)
        scores[start : start + CHUNK] = sims
        top = jnp.maximum(top, jnp.max(fold(sims), axis=0))
    total = jnp.zeros((8, ROWS), F32)
    weight = jnp.zeros((8, ROWS), F32)
    for start in range(0, ROWS, STRIP):
        sims = scores[start : start + STRIP]
        terms = jnp.exp2(fold(sims) - top)
        total += jnp.sum(terms, axis=0)
        weight += jnp.sum(terms * fold(sims), axis=0)
    put_stats(out, gather_columns(top, total, weight))


def own_pairs(block, rest):
    return pl.pallas_call(
        own_kernel,
        out_shape=jax.ShapeDtypeStruct((8, ROWS), F32),
        in_specs=[vmem(), vmem()],
        out_specs=vmem(),
        scratch_shapes=[pltpu.VMEM((ROWS, ROWS), F32)],
        compiler_params=params(),
        cost_estimate=pl.CostEstimate(
            flops=2 * ROWS * ROWS * WIDTH,
            bytes_accessed=2 * BLOCK * WIDTH,
            transcendentals=ROWS * ROWS,
        ),
        name="own",
    )(block, rest)


def pair_kernel(plan, blocks, old, half_ref, *refs):
    n, n_old = len(blocks), len(old)
    ins, rests, olds = refs[:n], refs[n : 2 * n], refs[2 * n : 2 * n + n_old]
    outs = refs[2 * n + n_old : 3 * n + n_old]
    marks, names, rows, tops, totals, weights, scores0, scores1 = refs[3 * n + n_old :]
    scores = (scores0, scores1)
    place = {b: i for i, b in enumerate(blocks)}
    lane = iota((1, 128), 1)
    empty = jnp.where(lane % 4 == 0, NEGATIVE, 0.0)
    for i in range(n):
        rows[i] = jnp.broadcast_to(empty, (ROWS, 128))
    tops[...] = jnp.full((n, 8, ROWS), FLOOR, F32)
    totals[...] = jnp.zeros((n, 8, ROWS), F32)
    weights[...] = jnp.zeros((n, 8, ROWS), F32)
    ready = set()

    def need(i):
        if i not in ready:
            ready.add(i)
            one, many = spread_names(ins[i])
            names[i] = jnp.broadcast_to(one, (8, ROWS))
            marks[i] = many

    steps = []
    for k, (left, right, axis) in enumerate(plan):
        left, right = place[left], place[right]
        if axis is None:
            steps += [(k, left, right, s, (left, right), None) for s in (0, HALF)]
        else:
            half = half_ref[axis]
            first = jnp.where(half == 0, left, right)
            second = jnp.where(half == 0, right, left)
            start = pl.multiple_of(half * HALF, HALF)
            steps.append((k, first, second, start, (left, right), half == 0))

    def product(step, out):
        _, _, _, start, both, first = step
        for i in both:
            need(i)
        here = pl.ds(start, HALF)

        def multiply(pieces):
            left, right = pieces[both[0]], pieces[both[1]]
            if first is None:
                return dot_nt(left[here], right[:ROWS])
            keys = jnp.where(first, left[here], right[here])
            return dot_nt(keys, jnp.where(first, right[:ROWS], left[:ROWS]))

        out[...] = multiply(ins) + multiply(rests)

    def reduce(step, data):
        k, left, right, start, _, _ = step
        name = names[right][:1]
        top = tops[right]
        peak = top
        for at in range(0, HALF, STRIP):
            here = pl.ds(start + at, STRIP)
            mask = across(marks[left, here]) == name
            sims = jnp.where(mask, data[at : at + STRIP] * SCALE2, NEGATIVE)
            data[at : at + STRIP] = sims
            peak = jnp.maximum(peak, jnp.max(fold(sims), axis=0))
            best = jnp.maximum(jnp.max(sims, axis=1, keepdims=True), FLOOR)
            terms = jnp.exp2(sims - best)
            total = jnp.sum(terms, axis=1, keepdims=True)
            weight = jnp.sum(terms * sims, axis=1, keepdims=True)
            rows[left, here] = jnp.where(
                lane == 4 * k,
                best,
                jnp.where(
                    lane == 4 * k + 1, total, jnp.where(lane == 4 * k + 2, weight, rows[left, here])
                ),
            )
        factor = jnp.exp2(top - peak)
        total = totals[right] * factor
        weight = weights[right] * factor
        for at in range(0, HALF, STRIP):
            sims = fold(data[at : at + STRIP])
            terms = jnp.exp2(sims - peak)
            total += jnp.sum(terms, axis=0)
            weight += jnp.sum(terms * sims, axis=0)
        tops[right] = peak
        totals[right] = total
        weights[right] = weight

    product(steps[0], scores[0])
    for t, step in enumerate(steps):
        if t + 1 < len(steps):
            product(steps[t + 1], scores[(t + 1) % 2])
        reduce(step, scores[t % 2])

    for i, b in enumerate(blocks):
        parts = [gather_columns(tops[i], totals[i], weights[i])]
        mine = [k for k, (left, right, axis) in enumerate(plan) if left == b or (axis is not None and right == b)]
        if mine:
            turned = jnp.transpose(rows[i])
            parts += [tuple(turned[4 * k + j : 4 * k + j + 1] for j in range(3)) for k in mine]
        if b in old:
            parts.append(get_stats(olds[old.index(b)]))
        put_stats(outs[i], merge(parts))


def pairs(plan, blocks, old, halves):
    names, n = list(blocks), len(blocks)
    steps = sum(2 if axis is None else 1 for _, _, axis in plan)
    return pl.pallas_call(
        functools.partial(pair_kernel, plan, names, list(old)),
        out_shape=[jax.ShapeDtypeStruct((8, ROWS), F32)] * n,
        in_specs=[smem()] + [vmem()] * (2 * n) + [vmem()] * len(old),
        out_specs=[vmem()] * n,
        scratch_shapes=[
            pltpu.VMEM((n, ROWS, 128), F32),
            pltpu.VMEM((n, 8, ROWS), F32),
            pltpu.VMEM((n, ROWS, 128), F32),
            pltpu.VMEM((n, 8, ROWS), F32),
            pltpu.VMEM((n, 8, ROWS), F32),
            pltpu.VMEM((n, 8, ROWS), F32),
            pltpu.VMEM((HALF, ROWS), F32),
            pltpu.VMEM((HALF, ROWS), F32),
        ],
        compiler_params=params(),
        cost_estimate=pl.CostEstimate(
            flops=2 * steps * HALF * ROWS * WIDTH,
            bytes_accessed=2 * n * BLOCK * WIDTH,
            transcendentals=2 * steps * HALF * ROWS,
        ),
        name="pairs",
    )(halves, *[b[0] for b in blocks.values()], *[b[1] for b in blocks.values()], *old.values())


def spread_kernel(offset_ref, *refs):
    out_ref = refs[-1]
    top, total, weight = merge([get_stats(r) for r in refs[:-1]])
    best = top / SCALE2
    mean = weight / total / SCALE2
    row = iota((8, ROWS), 0)
    values = jnp.where(row == 0, best, jnp.where(row == 1, mean, 0.0))
    values = jnp.concatenate([values, jnp.zeros((8, SPAN - ROWS), F32)], axis=1)
    for r in range(TILE_ROWS):
        offset = offset_ref[r]
        out_ref[r] = pltpu.roll(values, lax.rem(SPAN - offset, SPAN), 1)[:, :LANES]


def spread(offsets, stats):
    return pl.pallas_call(
        spread_kernel,
        out_shape=jax.ShapeDtypeStruct((TILE_ROWS, 8, LANES), F32),
        in_specs=[pl.BlockSpec(memory_space=pltpu.SMEM)]
        + [pl.BlockSpec(memory_space=pltpu.VMEM)] * len(stats),
        out_specs=pl.BlockSpec(memory_space=pltpu.VMEM),
        compiler_params=params(),
        name="spread",
    )(offsets, *stats)


def unpack_kernel(back_ref, lab_ref, rank_ref, best_ref, mean_ref, flag_ref):
    found = jnp.zeros((24, ROWS), F32)
    for g in range(TILE_ROWS):
        chosen = pick(lab_ref, rank_ref, g, LANES)
        values = back_ref[g]
        high = values.astype(BF).astype(F32)
        mid = (values - high).astype(BF).astype(F32)
        low = values - high - mid
        found += dot(jnp.concatenate([high, mid, low], axis=0).astype(BF), chosen)
    found = found[:8] + (found[8:16] + found[16:])
    best = found[:1]
    best_ref[...] = best.reshape(ROWS)
    mean_ref[...] = found[1:2].reshape(ROWS)
    flag_ref[...] = (1.0 / (1.0 + jnp.exp(-SHARPNESS * (best - THRESHOLD)))).reshape(ROWS)


def unpack(back, labels, rank):
    return pl.pallas_call(
        unpack_kernel,
        out_shape=[jax.ShapeDtypeStruct((ROWS,), F32)] * 3,
        in_specs=[pl.BlockSpec(memory_space=pltpu.VMEM)] * 3,
        out_specs=[pl.BlockSpec(memory_space=pltpu.VMEM)] * 3,
        compiler_params=params(),
        name="unpack",
    )(back, labels, rank)


def shift(array, dx, dy):
    moves = []
    for tr in range(TILE_ROWS):
        sign = 1 - 2 * (tr % 2)
        for x in range(SIDE):
            for y in range(SIDE):
                to = ((x + sign * dx) % SIDE) * SIDE + (y + sign * dy) % SIDE
                base = tr * SIDE * SIDE
                moves.append((base + x * SIDE + y, base + to))
    return lax.ppermute(array, ("tr", "tc"), moves)


PLACES = {"O": (0, 0), "A": (1, 0), "B": (2, 0), "C": (0, 1), "D": (0, -1), "E": (0, 2)}
FIRST = [("O", "A", None)]
NEAR = [("O", "C", None), ("A", "C", None), ("D", "A", None), ("C", "D", 1)]
FAR = [("B", "O", 0), ("B", "C", None), ("E", "A", None), ("E", "B", 0)]


def per_device(embeddings, labels):
    tie = lax.optimization_barrier
    tc = lax.axis_index("tc")
    halves = jnp.stack([tc // (2 * SIDE), (tc % SIDE) // 2]).astype(jnp.int32)

    def exchange(packed):
        return lax.all_to_all(packed, "tr", split_axis=0, concat_axis=0, tiled=True)

    packed, rank, unit = pack_first(embeddings, labels)
    got = exchange(packed)
    packed = pack_rest(unit, labels, rank)
    packed, got = tie((packed, got))
    got_rest = exchange(packed)
    mine, place = compact_first(got)
    a, c, d = shift(mine, -1, 0), shift(mine, 0, -1), shift(mine, 0, 1)
    b, e = shift(a, -1, 0), shift(d, 0, 1)
    got_rest, a, b, c, d, e = tie((got_rest, a, b, c, d, e))
    mine2 = compact_rest(place, got_rest)
    a2, c2, d2 = shift(mine2, -1, 0), shift(mine2, 0, -1), shift(mine2, 0, 1)
    own = own_pairs(mine, mine2)
    a2, own, halves = tie((a2, own, halves))
    b2 = shift(a2, -1, 0)
    blocks = {"O": (mine, mine2), "A": (a, a2)}
    stats = dict(zip(blocks, pairs(FIRST, blocks, {"O": own}, halves)))
    d2, stats["O"] = tie((d2, stats["O"]))
    e2 = shift(d2, 0, 1)
    blocks.update(C=(c, c2), D=(d, d2))
    stats.update(zip(blocks, pairs(NEAR, blocks, stats, halves)))
    blocks.update(B=(b, b2), E=(e, e2))
    del blocks["D"]
    far = pairs(FAR, blocks, {q: stats[q] for q in "OAC"}, halves)
    stats.update(zip(blocks, far))
    parts = [stats["O"]] + [shift(stats[q], *PLACES[q]) for q in "ABCDE"]
    sent = spread(place, parts)
    back = exchange(sent)
    return unpack(back, labels, rank)


def solution(mesh):
    files = P(("tr", "tc"))
    return jax.shard_map(
        per_device,
        mesh=mesh,
        in_specs=(P(("tr", "tc"), None), files),
        out_specs=(files, files, files),
        check_vma=False,
    )
```

```python
import functools

import jax
import jax.numpy as jnp
from jax import lax
from jax.experimental import pallas as pl
from jax.experimental.pallas import tpu as pltpu
from jax.sharding import PartitionSpec as P

GROUP_SHIFT = 2
TILE_ROWS = 8
SIDE = 4
ROWS = 768
WIDTH = 1024
PIECES = (384, 384, 256)
PIECE = PIECES[0]
CAP = 288
TAIL = 16
PAIR = CAP + TAIL
LANES = 384
BLOCK = ROWS + TAIL
SPAN = 1152
EPSILON = 1e-06
THRESHOLD = 0.3
SHARPNESS = 50.0
SCALE2 = 256.0 * 1.4426950408889634
NEGATIVE = -1e30
FLOOR = -5e29
CHUNK = 256
HALF = 384
STRIP = 32
VMEM = 24 * 1024 * 1024
BF = jnp.bfloat16
F32 = jnp.float32


def iota(shape, axis):
    return lax.broadcasted_iota(jnp.int32, shape, axis)


def dot(a, b):
    return lax.dot_general(a, b, (((1,), (0,)), ((), ())), preferred_element_type=F32)


def dot_nt(a, b):
    return lax.dot_general(a, b, (((1,), (1,)), ((), ())), preferred_element_type=F32)


def params(**more):
    return pltpu.CompilerParams(vmem_limit_bytes=VMEM, **more)


def whole(shape):
    return pl.BlockSpec(shape, lambda *_: (0,) * len(shape))


def vmem():
    return pl.BlockSpec(memory_space=pltpu.VMEM)


def smem():
    return pl.BlockSpec(memory_space=pltpu.SMEM)


def pick(lab_ref, rank_ref, g, slots):
    owner = lax.shift_right_logical(lab_ref[...].reshape(1, ROWS), GROUP_SHIFT)
    slot = jnp.where(owner == g, rank_ref[...], -1)
    return (iota((slots, ROWS), 0) == slot).astype(F32).astype(BF)


def pack_first_kernel(emb_ref, lab_ref, out_ref, rank_ref, *refs):
    *rests, unit = refs
    g = pl.program_id(0)
    lab = lab_ref[...].reshape(1, ROWS)

    @pl.when(g == 0)
    def _():
        values = emb_ref[...].astype(F32)
        total = jnp.sum(values * values, axis=1, keepdims=True)
        rows = (values * lax.rsqrt(total + EPSILON)).astype(BF)
        start = 0
        for ref in (unit, *rests):
            stop = start + ref.shape[1]
            ref[...] = rows[:, start:stop]
            start = stop
        owner = lax.shift_right_logical(lab, GROUP_SHIFT)
        onehot = (iota((TILE_ROWS, ROWS), 0) == owner).astype(F32)
        before = (iota((ROWS, ROWS), 0) < iota((ROWS, ROWS), 1)).astype(F32).astype(BF)
        seen = dot(onehot.astype(BF), before)
        rank_ref[...] = jnp.sum(onehot * seen, axis=0, keepdims=True).astype(jnp.int32)

    chosen = pick(lab_ref, rank_ref, g, LANES)
    out_ref[0] = dot(chosen[:PAIR], unit[...]).astype(BF)
    marks = jnp.broadcast_to(lab.astype(F32) + 1.0, (TAIL, ROWS)).astype(BF)
    out_ref[0, CAP:] = (dot_nt(marks, chosen) - 1.0).astype(BF)


def pack_first(embeddings, labels):
    return pl.pallas_call(
        pack_first_kernel,
        grid=(TILE_ROWS,),
        in_specs=[whole((ROWS, WIDTH)), whole((ROWS,))],
        out_specs=[
            pl.BlockSpec((1, PAIR, PIECE), lambda g: (g, 0, 0)),
            whole((1, ROWS)),
        ]
        + [whole((ROWS, w)) for w in PIECES[1:]],
        out_shape=[
            jax.ShapeDtypeStruct((TILE_ROWS, PAIR, PIECE), BF),
            jax.ShapeDtypeStruct((1, ROWS), jnp.int32),
        ]
        + [jax.ShapeDtypeStruct((ROWS, w), BF) for w in PIECES[1:]],
        scratch_shapes=[pltpu.VMEM((ROWS, PIECE), BF)],
        compiler_params=params(),
        name="pack_first",
    )(embeddings, labels)


def pack_rest_kernel(unit_ref, lab_ref, rank_ref, out_ref):
    chosen = pick(lab_ref, rank_ref, pl.program_id(0), CAP)
    out_ref[0] = dot(chosen, unit_ref[...]).astype(BF)


def pack_rest(unit, labels, rank):
    width = unit.shape[1]
    return pl.pallas_call(
        pack_rest_kernel,
        grid=(TILE_ROWS,),
        in_specs=[whole((ROWS, width)), whole((ROWS,)), whole((1, ROWS))],
        out_specs=pl.BlockSpec((1, CAP, width), lambda g: (g, 0, 0)),
        out_shape=jax.ShapeDtypeStruct((TILE_ROWS, CAP, width), BF),
        compiler_params=params(),
        cost_estimate=pl.CostEstimate(
            flops=2 * TILE_ROWS * CAP * ROWS * width,
            bytes_accessed=2 * TILE_ROWS * CAP * width,
            transcendentals=0,
        ),
        name="pack_rest",
    )(unit, labels, rank)


def close_gaps(got_ref, rows, offsets, counts):
    sent = got_ref.shape[1]
    rows[:16] = jnp.zeros((16, rows.shape[1]), BF)
    column = iota((PAIR, sent), 1)
    apart = iota((PAIR, sent), 0) - column
    for r in range(TILE_ROWS):
        base = pl.multiple_of(lax.shift_right_logical(offsets[r], 4) * 16, 16)
        move = (apart == offsets[r] - base) & (column < counts[r])
        moved = dot(move.astype(F32).astype(BF), got_ref[r]).astype(BF)
        rows[pl.ds(base, 16)] = rows[pl.ds(base, 16)] + moved[:16]
        rows[pl.ds(base + 16, PAIR - 16)] = moved[16:]


def compact_first_kernel(got_ref, out_ref, place_ref, rows):
    names = jnp.zeros((8, SPAN), F32)
    offset = jnp.int32(0)
    offsets, counts = [], []
    for r in range(TILE_ROWS):
        lab = got_ref[r, CAP:, :LANES].astype(F32)[:8]
        count = jnp.sum((lab[:1] >= 0.0).astype(F32)).astype(jnp.int32)
        held = jnp.concatenate(
            [jnp.maximum(lab, 0.0), jnp.zeros((8, SPAN - LANES), F32)], axis=1
        )
        names += pltpu.roll(held, offset, 1)
        place_ref[r] = offset
        place_ref[TILE_ROWS + r] = count
        offsets.append(offset)
        counts.append(count)
        offset = offset + count
    close_gaps(got_ref, rows, offsets, counts)
    out_ref[:ROWS] = rows[:ROWS]
    out_ref[ROWS:] = jnp.concatenate([names[:, :PIECE], names[:, PIECE:ROWS]], axis=0).astype(BF)


def compact_first(got):
    return pl.pallas_call(
        compact_first_kernel,
        in_specs=[vmem()],
        out_specs=[vmem(), smem()],
        out_shape=[
            jax.ShapeDtypeStruct((BLOCK, PIECE), BF),
            jax.ShapeDtypeStruct((2 * TILE_ROWS,), jnp.int32),
        ],
        scratch_shapes=[pltpu.VMEM((ROWS + PAIR, PIECE), BF)],
        compiler_params=params(),
        name="compact_first",
    )(got)


def compact_rest_kernel(place_ref, got_ref, out_ref, rows):
    places = [place_ref[i] for i in range(2 * TILE_ROWS)]
    close_gaps(got_ref, rows, places[:TILE_ROWS], places[TILE_ROWS:])
    out_ref[...] = rows[:ROWS]


def compact_rest(place, got):
    width = got.shape[2]
    return pl.pallas_call(
        compact_rest_kernel,
        in_specs=[smem(), vmem()],
        out_specs=vmem(),
        out_shape=jax.ShapeDtypeStruct((ROWS, width), BF),
        scratch_shapes=[pltpu.VMEM((ROWS + PAIR, width), BF)],
        compiler_params=params(),
        name="compact_rest",
    )(place, got)


def fold(tile):
    return tile.reshape(tile.shape[0] // 8, 8, tile.shape[1])


def merge(parts):
    top = functools.reduce(jnp.maximum, [p[0] for p in parts])
    factors = [jnp.exp2(p[0] - top) for p in parts]
    total = sum(p[1] * f for p, f in zip(parts, factors))
    weight = sum(p[2] * f for p, f in zip(parts, factors))
    return top, total, weight


def put_stats(ref, stats):
    for k, value in enumerate(stats):
        ref[k : k + 1] = value


def get_stats(ref):
    return tuple(ref[k : k + 1] for k in range(3))


def spread_names(block):
    tail = block[ROWS:].astype(F32)
    names = jnp.concatenate([tail[:1], tail[8:9]], axis=1)
    return names, jnp.transpose(jnp.broadcast_to(names, (128, ROWS)))


def across(mark):
    return jnp.concatenate([mark] * (ROWS // 128), axis=1)


def gather_columns(top, total, weight):
    best = jnp.max(top, axis=0, keepdims=True)
    factor = jnp.exp2(top - best)
    return (
        best,
        jnp.sum(total * factor, axis=0, keepdims=True),
        jnp.sum(weight * factor, axis=0, keepdims=True),
    )


def own_kernel(block, *refs):
    *rests, out, scores = refs
    names, marks = spread_names(block)
    top = jnp.full((8, ROWS), FLOOR, F32)
    for start in range(0, ROWS, CHUNK):
        sims = dot_nt(block[start : start + CHUNK], block[:ROWS])
        for rest in rests:
            sims += dot_nt(rest[start : start + CHUNK], rest[...])
        sims = sims * SCALE2
        mask = (across(marks[start : start + CHUNK]) == names) & (
            iota((CHUNK, ROWS), 0) + start != iota((CHUNK, ROWS), 1)
        )
        sims = jnp.where(mask, sims, NEGATIVE)
        scores[start : start + CHUNK] = sims
        top = jnp.maximum(top, jnp.max(fold(sims), axis=0))
    total = jnp.zeros((8, ROWS), F32)
    weight = jnp.zeros((8, ROWS), F32)
    for start in range(0, ROWS, STRIP):
        sims = scores[start : start + STRIP]
        terms = jnp.exp2(fold(sims) - top)
        total += jnp.sum(terms, axis=0)
        weight += jnp.sum(terms * fold(sims), axis=0)
    put_stats(out, gather_columns(top, total, weight))


def own_pairs(pieces):
    return pl.pallas_call(
        own_kernel,
        out_shape=jax.ShapeDtypeStruct((8, ROWS), F32),
        in_specs=[vmem()] * len(pieces),
        out_specs=vmem(),
        scratch_shapes=[pltpu.VMEM((ROWS, ROWS), F32)],
        compiler_params=params(),
        cost_estimate=pl.CostEstimate(
            flops=2 * ROWS * ROWS * WIDTH,
            bytes_accessed=2 * BLOCK * WIDTH,
            transcendentals=ROWS * ROWS,
        ),
        name="own",
    )(*pieces)


def pair_kernel(plan, blocks, old, half_ref, *refs):
    n, n_old = len(blocks), len(old)
    m = len(PIECES)
    pieces = [refs[i * n : (i + 1) * n] for i in range(m)]
    ins, olds = pieces[0], refs[m * n : m * n + n_old]
    outs = refs[m * n + n_old : (m + 1) * n + n_old]
    marks, names, rows, tops, totals, weights, scores0, scores1 = refs[(m + 1) * n + n_old :]
    scores = (scores0, scores1)
    place = {b: i for i, b in enumerate(blocks)}
    lane = iota((1, 128), 1)
    empty = jnp.where(lane % 4 == 0, NEGATIVE, 0.0)
    for i in range(n):
        rows[i] = jnp.broadcast_to(empty, (ROWS, 128))
    tops[...] = jnp.full((n, 8, ROWS), FLOOR, F32)
    totals[...] = jnp.zeros((n, 8, ROWS), F32)
    weights[...] = jnp.zeros((n, 8, ROWS), F32)
    ready = set()

    def need(i):
        if i not in ready:
            ready.add(i)
            one, many = spread_names(ins[i])
            names[i] = jnp.broadcast_to(one, (8, ROWS))
            marks[i] = many

    steps = []
    for k, (left, right, axis) in enumerate(plan):
        left, right = place[left], place[right]
        if axis is None:
            steps += [(k, left, right, s, (left, right), None) for s in (0, HALF)]
        else:
            half = half_ref[axis]
            first = jnp.where(half == 0, left, right)
            second = jnp.where(half == 0, right, left)
            start = pl.multiple_of(half * HALF, HALF)
            steps.append((k, first, second, start, (left, right), half == 0))

    def product(step, out):
        _, _, _, start, both, first = step
        for i in both:
            need(i)
        here = pl.ds(start, HALF)

        def multiply(pieces):
            left, right = pieces[both[0]], pieces[both[1]]
            if first is None:
                return dot_nt(left[here], right[:ROWS])
            keys = jnp.where(first, left[here], right[here])
            return dot_nt(keys, jnp.where(first, right[:ROWS], left[:ROWS]))

        out[...] = sum(multiply(p) for p in pieces)

    def reduce(step, data):
        k, left, right, start, _, _ = step
        name = names[right][:1]
        top = tops[right]
        peak = top
        for at in range(0, HALF, STRIP):
            here = pl.ds(start + at, STRIP)
            mask = across(marks[left, here]) == name
            sims = jnp.where(mask, data[at : at + STRIP] * SCALE2, NEGATIVE)
            data[at : at + STRIP] = sims
            peak = jnp.maximum(peak, jnp.max(fold(sims), axis=0))
            best = jnp.maximum(jnp.max(sims, axis=1, keepdims=True), FLOOR)
            terms = jnp.exp2(sims - best)
            total = jnp.sum(terms, axis=1, keepdims=True)
            weight = jnp.sum(terms * sims, axis=1, keepdims=True)
            rows[left, here] = jnp.where(
                lane == 4 * k,
                best,
                jnp.where(
                    lane == 4 * k + 1, total, jnp.where(lane == 4 * k + 2, weight, rows[left, here])
                ),
            )
        factor = jnp.exp2(top - peak)
        total = totals[right] * factor
        weight = weights[right] * factor
        for at in range(0, HALF, STRIP):
            sims = fold(data[at : at + STRIP])
            terms = jnp.exp2(sims - peak)
            total += jnp.sum(terms, axis=0)
            weight += jnp.sum(terms * sims, axis=0)
        tops[right] = peak
        totals[right] = total
        weights[right] = weight

    product(steps[0], scores[0])
    for t, step in enumerate(steps):
        if t + 1 < len(steps):
            product(steps[t + 1], scores[(t + 1) % 2])
        reduce(step, scores[t % 2])

    for i, b in enumerate(blocks):
        parts = [gather_columns(tops[i], totals[i], weights[i])]
        mine = [k for k, (left, right, axis) in enumerate(plan) if left == b or (axis is not None and right == b)]
        if mine:
            turned = jnp.transpose(rows[i])
            parts += [tuple(turned[4 * k + j : 4 * k + j + 1] for j in range(3)) for k in mine]
        if b in old:
            parts.append(get_stats(olds[old.index(b)]))
        put_stats(outs[i], merge(parts))


def pairs(plan, blocks, old, halves):
    names, n = list(blocks), len(blocks)
    steps = sum(2 if axis is None else 1 for _, _, axis in plan)
    return pl.pallas_call(
        functools.partial(pair_kernel, plan, names, list(old)),
        out_shape=[jax.ShapeDtypeStruct((8, ROWS), F32)] * n,
        in_specs=[smem()] + [vmem()] * (len(PIECES) * n) + [vmem()] * len(old),
        out_specs=[vmem()] * n,
        scratch_shapes=[
            pltpu.VMEM((n, ROWS, 128), F32),
            pltpu.VMEM((n, 8, ROWS), F32),
            pltpu.VMEM((n, ROWS, 128), F32),
            pltpu.VMEM((n, 8, ROWS), F32),
            pltpu.VMEM((n, 8, ROWS), F32),
            pltpu.VMEM((n, 8, ROWS), F32),
            pltpu.VMEM((HALF, ROWS), F32),
            pltpu.VMEM((HALF, ROWS), F32),
        ],
        compiler_params=params(),
        cost_estimate=pl.CostEstimate(
            flops=2 * steps * HALF * ROWS * WIDTH,
            bytes_accessed=2 * n * BLOCK * WIDTH,
            transcendentals=2 * steps * HALF * ROWS,
        ),
        name="pairs",
    )(halves, *[b[i] for i in range(len(PIECES)) for b in blocks.values()], *old.values())


def spread_kernel(offset_ref, *refs):
    out_ref = refs[-1]
    top, total, weight = merge([get_stats(r) for r in refs[:-1]])
    best = top / SCALE2
    mean = weight / total / SCALE2
    row = iota((8, ROWS), 0)
    values = jnp.where(row == 0, best, jnp.where(row == 1, mean, 0.0))
    values = jnp.concatenate([values, jnp.zeros((8, SPAN - ROWS), F32)], axis=1)
    for r in range(TILE_ROWS):
        offset = offset_ref[r]
        moved = pltpu.roll(values, lax.rem(SPAN - offset, SPAN), 1)
        for k in range(6):
            lanes = slice(k % 3 * 128, k % 3 * 128 + 128)
            out_ref[r, k : k + 1] = moved[k // 3 : k // 3 + 1, lanes]
        out_ref[r, 6:] = jnp.zeros((2, 128), F32)


def spread(offsets, stats):
    return pl.pallas_call(
        spread_kernel,
        out_shape=jax.ShapeDtypeStruct((TILE_ROWS, 8, 128), F32),
        in_specs=[pl.BlockSpec(memory_space=pltpu.SMEM)]
        + [pl.BlockSpec(memory_space=pltpu.VMEM)] * len(stats),
        out_specs=pl.BlockSpec(memory_space=pltpu.VMEM),
        compiler_params=params(),
        name="spread",
    )(offsets, *stats)


def unpack_kernel(back_ref, lab_ref, rank_ref, best_ref, mean_ref, flag_ref):
    found = jnp.zeros((24, ROWS), F32)
    for g in range(TILE_ROWS):
        chosen = pick(lab_ref, rank_ref, g, LANES)
        rows = [back_ref[g, k : k + 1] for k in range(6)]
        best, mean = jnp.concatenate(rows[:3], axis=1), jnp.concatenate(rows[3:], axis=1)
        values = jnp.concatenate([best, mean, jnp.zeros((6, LANES), F32)], axis=0)
        high = values.astype(BF).astype(F32)
        mid = (values - high).astype(BF).astype(F32)
        low = values - high - mid
        found += dot(jnp.concatenate([high, mid, low], axis=0).astype(BF), chosen)
    found = found[:8] + (found[8:16] + found[16:])
    best = found[:1]
    best_ref[...] = best.reshape(ROWS)
    mean_ref[...] = found[1:2].reshape(ROWS)
    flag_ref[...] = (1.0 / (1.0 + jnp.exp(-SHARPNESS * (best - THRESHOLD)))).reshape(ROWS)


def unpack(back, labels, rank):
    return pl.pallas_call(
        unpack_kernel,
        out_shape=[jax.ShapeDtypeStruct((ROWS,), F32)] * 3,
        in_specs=[pl.BlockSpec(memory_space=pltpu.VMEM)] * 3,
        out_specs=[pl.BlockSpec(memory_space=pltpu.VMEM)] * 3,
        compiler_params=params(),
        name="unpack",
    )(back, labels, rank)


def shift(array, dx, dy):
    moves = []
    for tr in range(TILE_ROWS):
        sign = 1 - 2 * (tr % 2)
        for x in range(SIDE):
            for y in range(SIDE):
                to = ((x + sign * dx) % SIDE) * SIDE + (y + sign * dy) % SIDE
                base = tr * SIDE * SIDE
                moves.append((base + x * SIDE + y, base + to))
    return lax.ppermute(array, ("tr", "tc"), moves)


PLACES = {"O": (0, 0), "A": (1, 0), "B": (2, 0), "C": (0, 1), "D": (0, -1), "E": (0, 2)}
FIRST = [("O", "A", None)]
NEAR = [("O", "C", None), ("A", "C", None), ("D", "A", None), ("C", "D", 1)]
FAR = [("B", "O", 0), ("B", "C", None), ("E", "A", None), ("E", "B", 0)]


def per_device(embeddings, labels):
    tie = lax.optimization_barrier
    tc = lax.axis_index("tc")
    halves = jnp.stack([tc // (2 * SIDE), (tc % SIDE) // 2]).astype(jnp.int32)

    def exchange(packed):
        return lax.all_to_all(packed, "tr", split_axis=0, concat_axis=0, tiled=True)

    packed, rank, *units = pack_first(embeddings, labels)
    got = exchange(packed)
    blocks = {q: [] for q in "OABCDE"}
    place = None
    last = len(PIECES) - 1
    for k in range(len(PIECES)):
        if k < last:
            packed = pack_rest(units[k], labels, rank)
            packed, got = tie((packed, got))
            later = exchange(packed)
        if k == 0:
            mine, place = compact_first(got)
        else:
            mine = compact_rest(place, got)
        a, c, d = shift(mine, -1, 0), shift(mine, 0, -1), shift(mine, 0, 1)
        if k == last:
            own = own_pairs([*blocks["O"], mine])
            a, own, halves = tie((a, own, halves))
        b = shift(a, -1, 0)
        if k == last:
            sides = {"O": [*blocks["O"], mine], "A": [*blocks["A"], a]}
            stats = dict(zip(sides, pairs(FIRST, sides, {"O": own}, halves)))
            d, stats["O"] = tie((d, stats["O"]))
        e = shift(d, 0, 1)
        if k < last:
            got, a, b, c, d, e = tie((later, a, b, c, d, e))
        for q, piece in zip("OABCDE", (mine, a, b, c, d, e)):
            blocks[q].append(piece)
    near = {q: blocks[q] for q in "OACD"}
    stats.update(zip(near, pairs(NEAR, near, stats, halves)))
    wide = {q: blocks[q] for q in "OACBE"}
    far = pairs(FAR, wide, {q: stats[q] for q in "OAC"}, halves)
    stats.update(zip(wide, far))
    stats["D"], stats["B"] = tie((stats["D"], stats["B"]))
    parts = [stats["O"]] + [shift(stats[q], *PLACES[q]) for q in "ABCDE"]
    sent = spread(place, parts)
    back = exchange(sent)
    return unpack(back, labels, rank)


def solution(mesh):
    files = P(("tr", "tc"))
    return jax.shard_map(
        per_device,
        mesh=mesh,
        in_specs=(P(("tr", "tc"), None), files),
        out_specs=(files, files, files),
        check_vma=False,
    )
```

```python
import functools

import jax
import jax.numpy as jnp
from jax import lax
from jax.experimental import pallas as pl
from jax.experimental.pallas import tpu as pltpu
from jax.sharding import PartitionSpec as P

GROUP_SHIFT = 2
TILE_ROWS = 8
SIDE = 4
ROWS = 768
WIDTH = 1024
PIECES = (512, 512)
PIECE = PIECES[0]
CAP = 288
TAIL = 16
PAIR = CAP + TAIL
LANES = 384
BLOCK = ROWS + TAIL
SPAN = 1152
EPSILON = 1e-06
THRESHOLD = 0.3
SHARPNESS = 50.0
SCALE2 = 256.0 * 1.4426950408889634
NEGATIVE = -1e30
FLOOR = -5e29
CHUNK = 256
HALF = 384
STRIP = 32
VMEM = 24 * 1024 * 1024
PACK_VMEM = 56 * 1024 * 1024
BF = jnp.bfloat16
F32 = jnp.float32


def iota(shape, axis):
    return lax.broadcasted_iota(jnp.int32, shape, axis)


def dot(a, b):
    return lax.dot_general(a, b, (((1,), (0,)), ((), ())), preferred_element_type=F32)


def dot_nt(a, b):
    return lax.dot_general(a, b, (((1,), (1,)), ((), ())), preferred_element_type=F32)


def params(limit=VMEM):
    return pltpu.CompilerParams(vmem_limit_bytes=limit)


def whole(shape):
    return pl.BlockSpec(shape, lambda *_: (0,) * len(shape))


def vmem():
    return pl.BlockSpec(memory_space=pltpu.VMEM)


def smem():
    return pl.BlockSpec(memory_space=pltpu.SMEM)


def pick(lab_ref, rank_ref, g, slots):
    owner = lax.shift_right_logical(lab_ref[...].reshape(1, ROWS), GROUP_SHIFT)
    slot = jnp.where(owner == g, rank_ref[...], -1)
    return (iota((slots, ROWS), 0) == slot).astype(F32).astype(BF)


def pack_first_kernel(emb_ref, lab_ref, out_ref, rank_ref, *refs):
    *rests, unit = refs
    g = pl.program_id(0)
    lab = lab_ref[...].reshape(1, ROWS)

    @pl.when(g == 0)
    def _():
        values = emb_ref[...].astype(F32)
        total = jnp.sum(values * values, axis=1, keepdims=True)
        rows = (values * lax.rsqrt(total + EPSILON)).astype(BF)
        start = 0
        for ref in (unit, *rests):
            stop = start + ref.shape[1]
            ref[...] = rows[:, start:stop]
            start = stop
        owner = lax.shift_right_logical(lab, GROUP_SHIFT)
        onehot = (iota((TILE_ROWS, ROWS), 0) == owner).astype(F32)
        before = (iota((ROWS, ROWS), 0) < iota((ROWS, ROWS), 1)).astype(F32).astype(BF)
        seen = dot(onehot.astype(BF), before)
        rank_ref[...] = jnp.sum(onehot * seen, axis=0, keepdims=True).astype(jnp.int32)

    chosen = pick(lab_ref, rank_ref, g, LANES)
    out_ref[0] = dot(chosen[:PAIR], unit[...]).astype(BF)
    marks = jnp.broadcast_to(lab.astype(F32) + 1.0, (TAIL, ROWS)).astype(BF)
    out_ref[0, CAP:, :LANES] = (dot_nt(marks, chosen) - 1.0).astype(BF)
    out_ref[0, CAP:, LANES:] = jnp.zeros((TAIL, PIECE - LANES), BF)


def pack_first(embeddings, labels):
    return pl.pallas_call(
        pack_first_kernel,
        grid=(TILE_ROWS,),
        in_specs=[whole((ROWS, WIDTH)), whole((ROWS,))],
        out_specs=[
            pl.BlockSpec((1, PAIR, PIECE), lambda g: (g, 0, 0)),
            whole((1, ROWS)),
        ]
        + [whole((ROWS, w)) for w in PIECES[1:]],
        out_shape=[
            jax.ShapeDtypeStruct((TILE_ROWS, PAIR, PIECE), BF),
            jax.ShapeDtypeStruct((1, ROWS), jnp.int32),
        ]
        + [jax.ShapeDtypeStruct((ROWS, w), BF) for w in PIECES[1:]],
        scratch_shapes=[pltpu.VMEM((ROWS, PIECE), BF)],
        compiler_params=params(PACK_VMEM),
        name="pack_first",
    )(embeddings, labels)


def pack_rest_kernel(unit_ref, lab_ref, rank_ref, out_ref):
    chosen = pick(lab_ref, rank_ref, pl.program_id(0), CAP)
    out_ref[0] = dot(chosen, unit_ref[...]).astype(BF)


def pack_rest(unit, labels, rank):
    width = unit.shape[1]
    return pl.pallas_call(
        pack_rest_kernel,
        grid=(TILE_ROWS,),
        in_specs=[whole((ROWS, width)), whole((ROWS,)), whole((1, ROWS))],
        out_specs=pl.BlockSpec((1, CAP, width), lambda g: (g, 0, 0)),
        out_shape=jax.ShapeDtypeStruct((TILE_ROWS, CAP, width), BF),
        compiler_params=params(PACK_VMEM),
        cost_estimate=pl.CostEstimate(
            flops=2 * TILE_ROWS * CAP * ROWS * width,
            bytes_accessed=2 * TILE_ROWS * CAP * width,
            transcendentals=0,
        ),
        name="pack_rest",
    )(unit, labels, rank)


def close_gaps(got_ref, rows, offsets, counts):
    sent = got_ref.shape[1]
    rows[:16] = jnp.zeros((16, rows.shape[1]), BF)
    column = iota((PAIR, sent), 1)
    apart = iota((PAIR, sent), 0) - column
    for r in range(TILE_ROWS):
        base = pl.multiple_of(lax.shift_right_logical(offsets[r], 4) * 16, 16)
        move = (apart == offsets[r] - base) & (column < counts[r])
        moved = dot(move.astype(F32).astype(BF), got_ref[r]).astype(BF)
        rows[pl.ds(base, 16)] = rows[pl.ds(base, 16)] + moved[:16]
        rows[pl.ds(base + 16, PAIR - 16)] = moved[16:]


def compact_first_kernel(got_ref, out_ref, place_ref, rows):
    names = jnp.zeros((8, SPAN), F32)
    offset = jnp.int32(0)
    offsets, counts = [], []
    for r in range(TILE_ROWS):
        lab = got_ref[r, CAP:, :LANES].astype(F32)[:8]
        count = jnp.sum((lab[:1] >= 0.0).astype(F32)).astype(jnp.int32)
        held = jnp.concatenate(
            [jnp.maximum(lab, 0.0), jnp.zeros((8, SPAN - LANES), F32)], axis=1
        )
        names += pltpu.roll(held, offset, 1)
        place_ref[r] = offset
        place_ref[TILE_ROWS + r] = count
        offsets.append(offset)
        counts.append(count)
        offset = offset + count
    close_gaps(got_ref, rows, offsets, counts)
    out_ref[:ROWS] = rows[:ROWS]
    out_ref[ROWS:] = jnp.concatenate([names[:, :PIECE], names[:, PIECE : 2 * PIECE]], axis=0).astype(BF)


def compact_first(got):
    return pl.pallas_call(
        compact_first_kernel,
        in_specs=[vmem()],
        out_specs=[vmem(), smem()],
        out_shape=[
            jax.ShapeDtypeStruct((BLOCK, PIECE), BF),
            jax.ShapeDtypeStruct((2 * TILE_ROWS,), jnp.int32),
        ],
        scratch_shapes=[pltpu.VMEM((ROWS + PAIR, PIECE), BF)],
        compiler_params=params(),
        name="compact_first",
    )(got)


def compact_rest_kernel(place_ref, got_ref, out_ref, rows):
    places = [place_ref[i] for i in range(2 * TILE_ROWS)]
    close_gaps(got_ref, rows, places[:TILE_ROWS], places[TILE_ROWS:])
    out_ref[...] = rows[:ROWS]


def compact_rest(place, got):
    width = got.shape[2]
    return pl.pallas_call(
        compact_rest_kernel,
        in_specs=[smem(), vmem()],
        out_specs=vmem(),
        out_shape=jax.ShapeDtypeStruct((ROWS, width), BF),
        scratch_shapes=[pltpu.VMEM((ROWS + PAIR, width), BF)],
        compiler_params=params(),
        name="compact_rest",
    )(place, got)


def fold(tile):
    return tile.reshape(tile.shape[0] // 8, 8, tile.shape[1])


def merge(parts):
    top = functools.reduce(jnp.maximum, [p[0] for p in parts])
    factors = [jnp.exp2(p[0] - top) for p in parts]
    total = sum(p[1] * f for p, f in zip(parts, factors))
    weight = sum(p[2] * f for p, f in zip(parts, factors))
    return top, total, weight


def put_stats(ref, stats):
    for k, value in enumerate(stats):
        ref[k : k + 1] = value


def get_stats(ref):
    return tuple(ref[k : k + 1] for k in range(3))


def spread_names(block):
    tail = block[ROWS:].astype(F32)
    names = jnp.concatenate([tail[:1], tail[8:9, : ROWS - PIECE]], axis=1)
    return names, jnp.transpose(jnp.broadcast_to(names, (128, ROWS)))


def across(mark):
    return jnp.concatenate([mark] * (ROWS // 128), axis=1)


def gather_columns(top, total, weight):
    best = jnp.max(top, axis=0, keepdims=True)
    factor = jnp.exp2(top - best)
    return (
        best,
        jnp.sum(total * factor, axis=0, keepdims=True),
        jnp.sum(weight * factor, axis=0, keepdims=True),
    )


def own_kernel(block, *refs):
    *rests, out, scores = refs
    names, marks = spread_names(block)
    top = jnp.full((8, ROWS), FLOOR, F32)
    for start in range(0, ROWS, CHUNK):
        sims = dot_nt(block[start : start + CHUNK], block[:ROWS])
        for rest in rests:
            sims += dot_nt(rest[start : start + CHUNK], rest[...])
        sims = sims * SCALE2
        mask = (across(marks[start : start + CHUNK]) == names) & (
            iota((CHUNK, ROWS), 0) + start != iota((CHUNK, ROWS), 1)
        )
        sims = jnp.where(mask, sims, NEGATIVE)
        scores[start : start + CHUNK] = sims
        top = jnp.maximum(top, jnp.max(fold(sims), axis=0))
    total = jnp.zeros((8, ROWS), F32)
    weight = jnp.zeros((8, ROWS), F32)
    for start in range(0, ROWS, STRIP):
        sims = scores[start : start + STRIP]
        terms = jnp.exp2(fold(sims) - top)
        total += jnp.sum(terms, axis=0)
        weight += jnp.sum(terms * fold(sims), axis=0)
    put_stats(out, gather_columns(top, total, weight))


def own_pairs(pieces):
    return pl.pallas_call(
        own_kernel,
        out_shape=jax.ShapeDtypeStruct((8, ROWS), F32),
        in_specs=[vmem()] * len(pieces),
        out_specs=vmem(),
        scratch_shapes=[pltpu.VMEM((ROWS, ROWS), F32)],
        compiler_params=params(),
        cost_estimate=pl.CostEstimate(
            flops=2 * ROWS * ROWS * WIDTH,
            bytes_accessed=2 * BLOCK * WIDTH,
            transcendentals=ROWS * ROWS,
        ),
        name="own",
    )(*pieces)


def pair_kernel(plan, blocks, old, half_ref, *refs):
    n, n_old = len(blocks), len(old)
    m = len(PIECES)
    pieces = [refs[i * n : (i + 1) * n] for i in range(m)]
    ins, olds = pieces[0], refs[m * n : m * n + n_old]
    outs = refs[m * n + n_old : (m + 1) * n + n_old]
    marks, names, rows, tops, totals, weights, scores0, scores1 = refs[(m + 1) * n + n_old :]
    scores = (scores0, scores1)
    place = {b: i for i, b in enumerate(blocks)}
    lane = iota((1, 128), 1)
    empty = jnp.where(lane % 4 == 0, NEGATIVE, 0.0)
    for i in range(n):
        rows[i] = jnp.broadcast_to(empty, (ROWS, 128))
    tops[...] = jnp.full((n, 8, ROWS), FLOOR, F32)
    totals[...] = jnp.zeros((n, 8, ROWS), F32)
    weights[...] = jnp.zeros((n, 8, ROWS), F32)
    ready = set()

    def need(i):
        if i not in ready:
            ready.add(i)
            one, many = spread_names(ins[i])
            names[i] = jnp.broadcast_to(one, (8, ROWS))
            marks[i] = many

    steps = []
    for k, (left, right, axis) in enumerate(plan):
        left, right = place[left], place[right]
        if axis is None:
            steps += [(k, left, right, s, (left, right), None) for s in (0, HALF)]
        else:
            half = half_ref[axis]
            first = jnp.where(half == 0, left, right)
            second = jnp.where(half == 0, right, left)
            start = pl.multiple_of(half * HALF, HALF)
            steps.append((k, first, second, start, (left, right), half == 0))

    def product(step, out):
        _, _, _, start, both, first = step
        for i in both:
            need(i)
        here = pl.ds(start, HALF)

        def multiply(pieces):
            left, right = pieces[both[0]], pieces[both[1]]
            if first is None:
                return dot_nt(left[here], right[:ROWS])
            keys = jnp.where(first, left[here], right[here])
            return dot_nt(keys, jnp.where(first, right[:ROWS], left[:ROWS]))

        out[...] = sum(multiply(p) for p in pieces)

    def reduce(step, data):
        k, left, right, start, _, _ = step
        name = names[right][:1]
        top = tops[right]
        peak = top
        for at in range(0, HALF, STRIP):
            here = pl.ds(start + at, STRIP)
            mask = across(marks[left, here]) == name
            sims = jnp.where(mask, data[at : at + STRIP] * SCALE2, NEGATIVE)
            data[at : at + STRIP] = sims
            peak = jnp.maximum(peak, jnp.max(fold(sims), axis=0))
            best = jnp.maximum(jnp.max(sims, axis=1, keepdims=True), FLOOR)
            terms = jnp.exp2(sims - best)
            total = jnp.sum(terms, axis=1, keepdims=True)
            weight = jnp.sum(terms * sims, axis=1, keepdims=True)
            rows[left, here] = jnp.where(
                lane == 4 * k,
                best,
                jnp.where(
                    lane == 4 * k + 1, total, jnp.where(lane == 4 * k + 2, weight, rows[left, here])
                ),
            )
        factor = jnp.exp2(top - peak)
        total = totals[right] * factor
        weight = weights[right] * factor
        for at in range(0, HALF, STRIP):
            sims = fold(data[at : at + STRIP])
            terms = jnp.exp2(sims - peak)
            total += jnp.sum(terms, axis=0)
            weight += jnp.sum(terms * sims, axis=0)
        tops[right] = peak
        totals[right] = total
        weights[right] = weight

    product(steps[0], scores[0])
    for t, step in enumerate(steps):
        if t + 1 < len(steps):
            product(steps[t + 1], scores[(t + 1) % 2])
        reduce(step, scores[t % 2])

    for i, b in enumerate(blocks):
        parts = [gather_columns(tops[i], totals[i], weights[i])]
        mine = [k for k, (left, right, axis) in enumerate(plan) if left == b or (axis is not None and right == b)]
        if mine:
            turned = jnp.transpose(rows[i])
            parts += [tuple(turned[4 * k + j : 4 * k + j + 1] for j in range(3)) for k in mine]
        if b in old:
            parts.append(get_stats(olds[old.index(b)]))
        put_stats(outs[i], merge(parts))


def pairs(plan, blocks, old, halves):
    names, n = list(blocks), len(blocks)
    steps = sum(2 if axis is None else 1 for _, _, axis in plan)
    return pl.pallas_call(
        functools.partial(pair_kernel, plan, names, list(old)),
        out_shape=[jax.ShapeDtypeStruct((8, ROWS), F32)] * n,
        in_specs=[smem()] + [vmem()] * (len(PIECES) * n) + [vmem()] * len(old),
        out_specs=[vmem()] * n,
        scratch_shapes=[
            pltpu.VMEM((n, ROWS, 128), F32),
            pltpu.VMEM((n, 8, ROWS), F32),
            pltpu.VMEM((n, ROWS, 128), F32),
            pltpu.VMEM((n, 8, ROWS), F32),
            pltpu.VMEM((n, 8, ROWS), F32),
            pltpu.VMEM((n, 8, ROWS), F32),
            pltpu.VMEM((HALF, ROWS), F32),
            pltpu.VMEM((HALF, ROWS), F32),
        ],
        compiler_params=params(),
        cost_estimate=pl.CostEstimate(
            flops=2 * steps * HALF * ROWS * WIDTH,
            bytes_accessed=2 * n * BLOCK * WIDTH,
            transcendentals=2 * steps * HALF * ROWS,
        ),
        name="pairs",
    )(halves, *[b[i] for i in range(len(PIECES)) for b in blocks.values()], *old.values())


def spread_kernel(offset_ref, *refs):
    out_ref = refs[-1]
    top, total, weight = merge([get_stats(r) for r in refs[:-1]])
    best = top / SCALE2
    mean = weight / total / SCALE2
    row = iota((8, ROWS), 0)
    values = jnp.where(row == 0, best, jnp.where(row == 1, mean, 0.0))
    values = jnp.concatenate([values, jnp.zeros((8, SPAN - ROWS), F32)], axis=1)
    for r in range(TILE_ROWS):
        offset = offset_ref[r]
        moved = pltpu.roll(values, lax.rem(SPAN - offset, SPAN), 1)
        for k in range(6):
            lanes = slice(k % 3 * 128, k % 3 * 128 + 128)
            out_ref[r, k : k + 1] = moved[k // 3 : k // 3 + 1, lanes]
        out_ref[r, 6:] = jnp.zeros((2, 128), F32)


def spread(offsets, stats):
    return pl.pallas_call(
        spread_kernel,
        out_shape=jax.ShapeDtypeStruct((TILE_ROWS, 8, 128), F32),
        in_specs=[pl.BlockSpec(memory_space=pltpu.SMEM)]
        + [pl.BlockSpec(memory_space=pltpu.VMEM)] * len(stats),
        out_specs=pl.BlockSpec(memory_space=pltpu.VMEM),
        compiler_params=params(),
        name="spread",
    )(offsets, *stats)


def unpack_kernel(back_ref, lab_ref, rank_ref, best_ref, mean_ref, flag_ref):
    found = jnp.zeros((24, ROWS), F32)
    for g in range(TILE_ROWS):
        chosen = pick(lab_ref, rank_ref, g, LANES)
        rows = [back_ref[g, k : k + 1] for k in range(6)]
        best, mean = jnp.concatenate(rows[:3], axis=1), jnp.concatenate(rows[3:], axis=1)
        values = jnp.concatenate([best, mean, jnp.zeros((6, LANES), F32)], axis=0)
        high = values.astype(BF).astype(F32)
        mid = (values - high).astype(BF).astype(F32)
        low = values - high - mid
        found += dot(jnp.concatenate([high, mid, low], axis=0).astype(BF), chosen)
    found = found[:8] + (found[8:16] + found[16:])
    best = found[:1]
    best_ref[...] = best.reshape(ROWS)
    mean_ref[...] = found[1:2].reshape(ROWS)
    flag_ref[...] = (1.0 / (1.0 + jnp.exp(-SHARPNESS * (best - THRESHOLD)))).reshape(ROWS)


def unpack(back, labels, rank):
    return pl.pallas_call(
        unpack_kernel,
        out_shape=[jax.ShapeDtypeStruct((ROWS,), F32)] * 3,
        in_specs=[pl.BlockSpec(memory_space=pltpu.VMEM)] * 3,
        out_specs=[pl.BlockSpec(memory_space=pltpu.VMEM)] * 3,
        compiler_params=params(),
        name="unpack",
    )(back, labels, rank)


def shift(array, dx, dy):
    moves = []
    for tr in range(TILE_ROWS):
        sign = 1 - 2 * (tr % 2)
        for x in range(SIDE):
            for y in range(SIDE):
                to = ((x + sign * dx) % SIDE) * SIDE + (y + sign * dy) % SIDE
                base = tr * SIDE * SIDE
                moves.append((base + x * SIDE + y, base + to))
    return lax.ppermute(array, ("tr", "tc"), moves)


PLACES = {"O": (0, 0), "A": (1, 0), "B": (2, 0), "C": (0, 1), "D": (0, -1), "E": (0, 2)}
FIRST = [("O", "A", None)]
NEAR = [("O", "C", None), ("A", "C", None), ("D", "A", None), ("C", "D", 1)]
FAR = [("B", "O", 0), ("B", "C", None), ("E", "A", None), ("E", "B", 0)]


def per_device(embeddings, labels):
    tie = lax.optimization_barrier
    tc = lax.axis_index("tc")
    halves = jnp.stack([tc // (2 * SIDE), (tc % SIDE) // 2]).astype(jnp.int32)

    def exchange(packed):
        return lax.all_to_all(packed, "tr", split_axis=0, concat_axis=0, tiled=True)

    packed, rank, *units = pack_first(embeddings, labels)
    got = exchange(packed)
    blocks = {q: [] for q in "OABCDE"}
    place = None
    last = len(PIECES) - 1
    for k in range(len(PIECES)):
        if k < last:
            packed = pack_rest(units[k], labels, rank)
            packed, got = tie((packed, got))
            later = exchange(packed)
        if k == 0:
            mine, place = compact_first(got)
        else:
            mine = compact_rest(place, got)
        a, c, d = shift(mine, -1, 0), shift(mine, 0, -1), shift(mine, 0, 1)
        if k == last:
            own = own_pairs([*blocks["O"], mine])
            a, own, halves = tie((a, own, halves))
        b = shift(a, -1, 0)
        if k == last:
            sides = {"O": [*blocks["O"], mine], "A": [*blocks["A"], a]}
            stats = dict(zip(sides, pairs(FIRST, sides, {"O": own}, halves)))
            d, stats["O"] = tie((d, stats["O"]))
        e = shift(d, 0, 1)
        if k < last:
            got, e, d, c, b, a = tie((later, e, d, c, b, a))
        for q, piece in zip("OABCDE", (mine, a, b, c, d, e)):
            blocks[q].append(piece)
    near = {q: blocks[q] for q in "OACD"}
    stats.update(zip(near, pairs(NEAR, near, stats, halves)))
    wide = {q: blocks[q] for q in "OACBE"}
    far = pairs(FAR, wide, {q: stats[q] for q in "OAC"}, halves)
    stats.update(zip(wide, far))
    stats["D"], stats["B"] = tie((stats["D"], stats["B"]))
    parts = [stats["O"]] + [shift(stats[q], *PLACES[q]) for q in "ABCDE"]
    sent = spread(place, parts)
    back = exchange(sent)
    return unpack(back, labels, rank)


def solution(mesh):
    files = P(("tr", "tc"))
    return jax.shard_map(
        per_device,
        mesh=mesh,
        in_specs=(P(("tr", "tc"), None), files),
        out_specs=(files, files, files),
        check_vma=False,
    )
```

```python
import functools

import jax
import jax.numpy as jnp
from jax import lax
from jax.experimental import pallas as pl
from jax.experimental.pallas import tpu as pltpu
from jax.sharding import PartitionSpec as P

GROUP_SHIFT = 2
TILE_ROWS = 8
SIDE = 4
ROWS = 768
WIDTH = 1024
PIECES = (512, 512)
PIECE = PIECES[0]
CAP = 288
TAIL = 16
PAIR = CAP + TAIL
LANES = 384
BLOCK = ROWS + TAIL
SPAN = 1152
EPSILON = 1e-06
THRESHOLD = 0.3
SHARPNESS = 50.0
SCALE2 = 256.0 * 1.4426950408889634
NEGATIVE = -1e30
FLOOR = -5e29
CHUNK = 256
HALF = 384
STRIP = 32
VMEM = 24 * 1024 * 1024
PACK_VMEM = 56 * 1024 * 1024
BF = jnp.bfloat16
F32 = jnp.float32


def iota(shape, axis):
    return lax.broadcasted_iota(jnp.int32, shape, axis)


def dot(a, b):
    return lax.dot_general(a, b, (((1,), (0,)), ((), ())), preferred_element_type=F32)


def dot_nt(a, b):
    return lax.dot_general(a, b, (((1,), (1,)), ((), ())), preferred_element_type=F32)


def params(limit=VMEM):
    return pltpu.CompilerParams(vmem_limit_bytes=limit)


def whole(shape):
    return pl.BlockSpec(shape, lambda *_: (0,) * len(shape))


def vmem():
    return pl.BlockSpec(memory_space=pltpu.VMEM)


def smem():
    return pl.BlockSpec(memory_space=pltpu.SMEM)


def pick(lab_ref, rank_ref, g, slots):
    owner = lax.shift_right_logical(lab_ref[...].reshape(1, ROWS), GROUP_SHIFT)
    slot = jnp.where(owner == g, rank_ref[...], -1)
    return (iota((slots, ROWS), 0) == slot).astype(F32).astype(BF)


def pack_first_kernel(emb_ref, lab_ref, out_ref, rank_ref, *refs):
    *rests, unit = refs
    g = pl.program_id(0)
    lab = lab_ref[...].reshape(1, ROWS)

    @pl.when(g == 0)
    def _():
        values = emb_ref[...].astype(F32)
        total = jnp.sum(values * values, axis=1, keepdims=True)
        rows = (values * lax.rsqrt(total + EPSILON)).astype(BF)
        start = 0
        for ref in (unit, *rests):
            stop = start + ref.shape[1]
            ref[...] = rows[:, start:stop]
            start = stop
        owner = lax.shift_right_logical(lab, GROUP_SHIFT)
        onehot = (iota((TILE_ROWS, ROWS), 0) == owner).astype(F32)
        before = (iota((ROWS, ROWS), 0) < iota((ROWS, ROWS), 1)).astype(F32).astype(BF)
        seen = dot(onehot.astype(BF), before)
        rank_ref[...] = jnp.sum(onehot * seen, axis=0, keepdims=True).astype(jnp.int32)

    chosen = pick(lab_ref, rank_ref, g, LANES)
    out_ref[0] = dot(chosen[:PAIR], unit[...]).astype(BF)
    marks = jnp.broadcast_to(lab.astype(F32) + 1.0, (TAIL, ROWS)).astype(BF)
    out_ref[0, CAP:, :LANES] = (dot_nt(marks, chosen) - 1.0).astype(BF)
    out_ref[0, CAP:, LANES:] = jnp.zeros((TAIL, PIECE - LANES), BF)


def pack_first(embeddings, labels):
    return pl.pallas_call(
        pack_first_kernel,
        grid=(TILE_ROWS,),
        in_specs=[whole((ROWS, WIDTH)), whole((ROWS,))],
        out_specs=[
            pl.BlockSpec((1, PAIR, PIECE), lambda g: (g, 0, 0)),
            whole((1, ROWS)),
        ]
        + [whole((ROWS, w)) for w in PIECES[1:]],
        out_shape=[
            jax.ShapeDtypeStruct((TILE_ROWS, PAIR, PIECE), BF),
            jax.ShapeDtypeStruct((1, ROWS), jnp.int32),
        ]
        + [jax.ShapeDtypeStruct((ROWS, w), BF) for w in PIECES[1:]],
        scratch_shapes=[pltpu.VMEM((ROWS, PIECE), BF)],
        compiler_params=params(PACK_VMEM),
        name="pack_first",
    )(embeddings, labels)


def pack_rest_kernel(unit_ref, lab_ref, rank_ref, out_ref):
    chosen = pick(lab_ref, rank_ref, pl.program_id(0), CAP)
    out_ref[0] = dot(chosen, unit_ref[...]).astype(BF)


def pack_rest(unit, labels, rank):
    width = unit.shape[1]
    return pl.pallas_call(
        pack_rest_kernel,
        grid=(TILE_ROWS,),
        in_specs=[whole((ROWS, width)), whole((ROWS,)), whole((1, ROWS))],
        out_specs=pl.BlockSpec((1, CAP, width), lambda g: (g, 0, 0)),
        out_shape=jax.ShapeDtypeStruct((TILE_ROWS, CAP, width), BF),
        compiler_params=params(PACK_VMEM),
        cost_estimate=pl.CostEstimate(
            flops=2 * TILE_ROWS * CAP * ROWS * width,
            bytes_accessed=2 * TILE_ROWS * CAP * width,
            transcendentals=0,
        ),
        name="pack_rest",
    )(unit, labels, rank)


def close_gaps(got_ref, rows, offsets, counts):
    sent = got_ref.shape[1]
    rows[:16] = jnp.zeros((16, rows.shape[1]), BF)
    column = iota((PAIR, sent), 1)
    apart = iota((PAIR, sent), 0) - column
    for r in range(TILE_ROWS):
        base = pl.multiple_of(lax.shift_right_logical(offsets[r], 4) * 16, 16)
        move = (apart == offsets[r] - base) & (column < counts[r])
        moved = dot(move.astype(F32).astype(BF), got_ref[r]).astype(BF)
        rows[pl.ds(base, 16)] = rows[pl.ds(base, 16)] + moved[:16]
        rows[pl.ds(base + 16, PAIR - 16)] = moved[16:]


def compact_first_kernel(got_ref, out_ref, place_ref, rows):
    names = jnp.zeros((8, SPAN), F32)
    offset = jnp.int32(0)
    offsets, counts = [], []
    for r in range(TILE_ROWS):
        lab = got_ref[r, CAP:, :LANES].astype(F32)[:8]
        count = jnp.sum((lab[:1] >= 0.0).astype(F32)).astype(jnp.int32)
        held = jnp.concatenate(
            [jnp.maximum(lab, 0.0), jnp.zeros((8, SPAN - LANES), F32)], axis=1
        )
        names += pltpu.roll(held, offset, 1)
        place_ref[r] = offset
        place_ref[TILE_ROWS + r] = count
        offsets.append(offset)
        counts.append(count)
        offset = offset + count
    close_gaps(got_ref, rows, offsets, counts)
    out_ref[:ROWS] = rows[:ROWS]
    out_ref[ROWS:] = jnp.concatenate([names[:, :PIECE], names[:, PIECE : 2 * PIECE]], axis=0).astype(BF)


def compact_first(got):
    return pl.pallas_call(
        compact_first_kernel,
        in_specs=[vmem()],
        out_specs=[vmem(), smem()],
        out_shape=[
            jax.ShapeDtypeStruct((BLOCK, PIECE), BF),
            jax.ShapeDtypeStruct((2 * TILE_ROWS,), jnp.int32),
        ],
        scratch_shapes=[pltpu.VMEM((ROWS + PAIR, PIECE), BF)],
        compiler_params=params(),
        name="compact_first",
    )(got)


def compact_rest_kernel(place_ref, got_ref, out_ref, rows):
    places = [place_ref[i] for i in range(2 * TILE_ROWS)]
    close_gaps(got_ref, rows, places[:TILE_ROWS], places[TILE_ROWS:])
    out_ref[...] = rows[:ROWS]


def compact_rest(place, got):
    width = got.shape[2]
    return pl.pallas_call(
        compact_rest_kernel,
        in_specs=[smem(), vmem()],
        out_specs=vmem(),
        out_shape=jax.ShapeDtypeStruct((ROWS, width), BF),
        scratch_shapes=[pltpu.VMEM((ROWS + PAIR, width), BF)],
        compiler_params=params(),
        name="compact_rest",
    )(place, got)


def fold(tile):
    return tile.reshape(tile.shape[0] // 8, 8, tile.shape[1])


def merge(parts):
    top = functools.reduce(jnp.maximum, [p[0] for p in parts])
    factors = [jnp.exp2(p[0] - top) for p in parts]
    total = sum(p[1] * f for p, f in zip(parts, factors))
    weight = sum(p[2] * f for p, f in zip(parts, factors))
    return top, total, weight


def put_stats(ref, stats):
    for k, value in enumerate(stats):
        ref[k : k + 1] = value


def get_stats(ref):
    return tuple(ref[k : k + 1] for k in range(3))


def spread_names(block):
    tail = block[ROWS:].astype(F32)
    names = jnp.concatenate([tail[:1], tail[8:9, : ROWS - PIECE]], axis=1)
    return names, jnp.transpose(jnp.broadcast_to(names, (128, ROWS)))


def across(mark):
    return jnp.concatenate([mark] * (ROWS // 128), axis=1)


def gather_columns(top, total, weight):
    best = jnp.max(top, axis=0, keepdims=True)
    factor = jnp.exp2(top - best)
    return (
        best,
        jnp.sum(total * factor, axis=0, keepdims=True),
        jnp.sum(weight * factor, axis=0, keepdims=True),
    )


def own_kernel(block, *refs):
    *rests, out, scores = refs
    names, marks = spread_names(block)
    top = jnp.full((8, ROWS), FLOOR, F32)
    for start in range(0, ROWS, CHUNK):
        sims = dot_nt(block[start : start + CHUNK], block[:ROWS])
        for rest in rests:
            sims += dot_nt(rest[start : start + CHUNK], rest[...])
        sims = sims * SCALE2
        mask = (across(marks[start : start + CHUNK]) == names) & (
            iota((CHUNK, ROWS), 0) + start != iota((CHUNK, ROWS), 1)
        )
        sims = jnp.where(mask, sims, NEGATIVE)
        scores[start : start + CHUNK] = sims
        top = jnp.maximum(top, jnp.max(fold(sims), axis=0))
    total = jnp.zeros((8, ROWS), F32)
    weight = jnp.zeros((8, ROWS), F32)
    for start in range(0, ROWS, STRIP):
        sims = scores[start : start + STRIP]
        terms = jnp.exp2(fold(sims) - top)
        total += jnp.sum(terms, axis=0)
        weight += jnp.sum(terms * fold(sims), axis=0)
    put_stats(out, gather_columns(top, total, weight))


def own_pairs(pieces):
    return pl.pallas_call(
        own_kernel,
        out_shape=jax.ShapeDtypeStruct((8, ROWS), F32),
        in_specs=[vmem()] * len(pieces),
        out_specs=vmem(),
        scratch_shapes=[pltpu.VMEM((ROWS, ROWS), F32)],
        compiler_params=params(),
        cost_estimate=pl.CostEstimate(
            flops=2 * ROWS * ROWS * WIDTH,
            bytes_accessed=2 * BLOCK * WIDTH,
            transcendentals=ROWS * ROWS,
        ),
        name="own",
    )(*pieces)


def pair_kernel(plan, blocks, old, half_ref, *refs):
    n, n_old = len(blocks), len(old)
    m = len(PIECES)
    pieces = [refs[i * n : (i + 1) * n] for i in range(m)]
    ins, olds = pieces[0], refs[m * n : m * n + n_old]
    outs = refs[m * n + n_old : (m + 1) * n + n_old]
    marks, names, rows, tops, totals, weights, scores0, scores1 = refs[(m + 1) * n + n_old :]
    scores = (scores0, scores1)
    place = {b: i for i, b in enumerate(blocks)}
    lane = iota((1, 128), 1)
    empty = jnp.where(lane % 4 == 0, NEGATIVE, 0.0)
    for i in range(n):
        rows[i] = jnp.broadcast_to(empty, (ROWS, 128))
    tops[...] = jnp.full((n, 8, ROWS), FLOOR, F32)
    totals[...] = jnp.zeros((n, 8, ROWS), F32)
    weights[...] = jnp.zeros((n, 8, ROWS), F32)
    ready = set()

    def need(i):
        if i not in ready:
            ready.add(i)
            one, many = spread_names(ins[i])
            names[i] = jnp.broadcast_to(one, (8, ROWS))
            marks[i] = many

    steps = []
    for k, (left, right, axis) in enumerate(plan):
        left, right = place[left], place[right]
        if axis is None:
            steps += [(k, left, right, s, (left, right), None) for s in (0, HALF)]
        else:
            half = half_ref[axis]
            first = jnp.where(half == 0, left, right)
            second = jnp.where(half == 0, right, left)
            start = pl.multiple_of(half * HALF, HALF)
            steps.append((k, first, second, start, (left, right), half == 0))

    def product(step, out):
        _, _, _, start, both, first = step
        for i in both:
            need(i)
        here = pl.ds(start, HALF)

        def multiply(pieces):
            left, right = pieces[both[0]], pieces[both[1]]
            if first is None:
                return dot_nt(left[here], right[:ROWS])
            keys = jnp.where(first, left[here], right[here])
            return dot_nt(keys, jnp.where(first, right[:ROWS], left[:ROWS]))

        out[...] = sum(multiply(p) for p in pieces)

    def reduce(step, data):
        k, left, right, start, _, _ = step
        name = names[right][:1]
        top = tops[right]
        peak = top
        for at in range(0, HALF, STRIP):
            here = pl.ds(start + at, STRIP)
            mask = across(marks[left, here]) == name
            sims = jnp.where(mask, data[at : at + STRIP] * SCALE2, NEGATIVE)
            data[at : at + STRIP] = sims
            peak = jnp.maximum(peak, jnp.max(fold(sims), axis=0))
            best = jnp.maximum(jnp.max(sims, axis=1, keepdims=True), FLOOR)
            terms = jnp.exp2(sims - best)
            total = jnp.sum(terms, axis=1, keepdims=True)
            weight = jnp.sum(terms * sims, axis=1, keepdims=True)
            rows[left, here] = jnp.where(
                lane == 4 * k,
                best,
                jnp.where(
                    lane == 4 * k + 1, total, jnp.where(lane == 4 * k + 2, weight, rows[left, here])
                ),
            )
        factor = jnp.exp2(top - peak)
        total = totals[right] * factor
        weight = weights[right] * factor
        for at in range(0, HALF, STRIP):
            sims = fold(data[at : at + STRIP])
            terms = jnp.exp2(sims - peak)
            total += jnp.sum(terms, axis=0)
            weight += jnp.sum(terms * sims, axis=0)
        tops[right] = peak
        totals[right] = total
        weights[right] = weight

    product(steps[0], scores[0])
    for t, step in enumerate(steps):
        if t + 1 < len(steps):
            product(steps[t + 1], scores[(t + 1) % 2])
        reduce(step, scores[t % 2])

    for i, b in enumerate(blocks):
        parts = [gather_columns(tops[i], totals[i], weights[i])]
        mine = [k for k, (left, right, axis) in enumerate(plan) if left == b or (axis is not None and right == b)]
        if mine:
            turned = jnp.transpose(rows[i])
            parts += [tuple(turned[4 * k + j : 4 * k + j + 1] for j in range(3)) for k in mine]
        if b in old:
            parts.append(get_stats(olds[old.index(b)]))
        put_stats(outs[i], merge(parts))


def pairs(plan, blocks, old, halves):
    names, n = list(blocks), len(blocks)
    steps = sum(2 if axis is None else 1 for _, _, axis in plan)
    return pl.pallas_call(
        functools.partial(pair_kernel, plan, names, list(old)),
        out_shape=[jax.ShapeDtypeStruct((8, ROWS), F32)] * n,
        in_specs=[smem()] + [vmem()] * (len(PIECES) * n) + [vmem()] * len(old),
        out_specs=[vmem()] * n,
        scratch_shapes=[
            pltpu.VMEM((n, ROWS, 128), F32),
            pltpu.VMEM((n, 8, ROWS), F32),
            pltpu.VMEM((n, ROWS, 128), F32),
            pltpu.VMEM((n, 8, ROWS), F32),
            pltpu.VMEM((n, 8, ROWS), F32),
            pltpu.VMEM((n, 8, ROWS), F32),
            pltpu.VMEM((HALF, ROWS), F32),
            pltpu.VMEM((HALF, ROWS), F32),
        ],
        compiler_params=params(),
        cost_estimate=pl.CostEstimate(
            flops=2 * steps * HALF * ROWS * WIDTH,
            bytes_accessed=2 * n * BLOCK * WIDTH,
            transcendentals=2 * steps * HALF * ROWS,
        ),
        name="pairs",
    )(halves, *[b[i] for i in range(len(PIECES)) for b in blocks.values()], *old.values())


def spread_kernel(offset_ref, *refs):
    out_ref = refs[-1]
    top, total, weight = merge([get_stats(r) for r in refs[:-1]])
    best = top / SCALE2
    mean = weight / total / SCALE2
    row = iota((8, ROWS), 0)
    values = jnp.where(row == 0, best, jnp.where(row == 1, mean, 0.0))
    values = jnp.concatenate([values, jnp.zeros((8, SPAN - ROWS), F32)], axis=1)
    for r in range(TILE_ROWS):
        offset = offset_ref[r]
        moved = pltpu.roll(values, lax.rem(SPAN - offset, SPAN), 1)
        for k in range(6):
            lanes = slice(k % 3 * 128, k % 3 * 128 + 128)
            out_ref[r, k : k + 1] = moved[k // 3 : k // 3 + 1, lanes]
        out_ref[r, 6:] = jnp.zeros((2, 128), F32)


def spread(offsets, stats):
    return pl.pallas_call(
        spread_kernel,
        out_shape=jax.ShapeDtypeStruct((TILE_ROWS, 8, 128), F32),
        in_specs=[pl.BlockSpec(memory_space=pltpu.SMEM)]
        + [pl.BlockSpec(memory_space=pltpu.VMEM)] * len(stats),
        out_specs=pl.BlockSpec(memory_space=pltpu.VMEM),
        compiler_params=params(),
        name="spread",
    )(offsets, *stats)


def unpack_kernel(back_ref, lab_ref, rank_ref, best_ref, mean_ref, flag_ref):
    found = jnp.zeros((24, ROWS), F32)
    for g in range(TILE_ROWS):
        chosen = pick(lab_ref, rank_ref, g, LANES)
        rows = [back_ref[g, k : k + 1] for k in range(6)]
        best, mean = jnp.concatenate(rows[:3], axis=1), jnp.concatenate(rows[3:], axis=1)
        values = jnp.concatenate([best, mean, jnp.zeros((6, LANES), F32)], axis=0)
        high = values.astype(BF).astype(F32)
        mid = (values - high).astype(BF).astype(F32)
        low = values - high - mid
        found += dot(jnp.concatenate([high, mid, low], axis=0).astype(BF), chosen)
    found = found[:8] + (found[8:16] + found[16:])
    best = found[:1]
    best_ref[...] = best.reshape(ROWS)
    mean_ref[...] = found[1:2].reshape(ROWS)
    flag_ref[...] = (1.0 / (1.0 + jnp.exp(-SHARPNESS * (best - THRESHOLD)))).reshape(ROWS)


def unpack(back, labels, rank):
    return pl.pallas_call(
        unpack_kernel,
        out_shape=[jax.ShapeDtypeStruct((ROWS,), F32)] * 3,
        in_specs=[pl.BlockSpec(memory_space=pltpu.VMEM)] * 3,
        out_specs=[pl.BlockSpec(memory_space=pltpu.VMEM)] * 3,
        compiler_params=params(),
        name="unpack",
    )(back, labels, rank)


def shift(array, dx, dy):
    moves = []
    for tr in range(TILE_ROWS):
        sign = 1 - 2 * (tr % 2)
        for x in range(SIDE):
            for y in range(SIDE):
                to = ((x + sign * dx) % SIDE) * SIDE + (y + sign * dy) % SIDE
                base = tr * SIDE * SIDE
                moves.append((base + x * SIDE + y, base + to))
    return lax.ppermute(array, ("tr", "tc"), moves)


PLACES = {"O": (0, 0), "A": (1, 0), "B": (2, 0), "C": (0, 1), "D": (0, -1), "E": (0, 2)}
FIRST = [("O", "A", None)]
NEAR = [("O", "C", None), ("A", "C", None), ("D", "A", None), ("C", "D", 1)]
FAR_X = [("B", "O", 0), ("B", "C", None)]
FAR_Y = [("E", "A", None), ("E", "B", 0)]


def per_device(embeddings, labels):
    tie = lax.optimization_barrier
    tc = lax.axis_index("tc")
    halves = jnp.stack([tc // (2 * SIDE), (tc % SIDE) // 2]).astype(jnp.int32)

    def exchange(packed):
        return lax.all_to_all(packed, "tr", split_axis=0, concat_axis=0, tiled=True)

    packed, rank, *units = pack_first(embeddings, labels)
    got = exchange(packed)
    blocks = {q: [] for q in "OABCDE"}
    place = None
    last = len(PIECES) - 1
    for k in range(len(PIECES)):
        if k < last:
            packed = pack_rest(units[k], labels, rank)
            packed, got = tie((packed, got))
            later = exchange(packed)
        if k == 0:
            mine, place = compact_first(got)
        else:
            mine = compact_rest(place, got)
        a, c, d = shift(mine, -1, 0), shift(mine, 0, -1), shift(mine, 0, 1)
        if k == last:
            own = own_pairs([*blocks["O"], mine])
            a, own, halves = tie((a, own, halves))
        b = shift(a, -1, 0)
        if k == last:
            sides = {"O": [*blocks["O"], mine], "A": [*blocks["A"], a]}
            stats = dict(zip(sides, pairs(FIRST, sides, {"O": own}, halves)))
            d, stats["O"] = tie((d, stats["O"]))
        e = shift(d, 0, 1)
        if k < last:
            got, e, d, c, b, a = tie((later, e, d, c, b, a))
        for q, piece in zip("OABCDE", (mine, a, b, c, d, e)):
            blocks[q].append(piece)
    near = {q: blocks[q] for q in "OACD"}
    stats.update(zip(near, pairs(NEAR, near, stats, halves)))
    wide = {q: blocks[q] for q in "OCB"}
    stats.update(zip(wide, pairs(FAR_X, wide, {q: stats[q] for q in "OC"}, halves)))
    wide = {q: blocks[q] for q in "ABE"}
    stats.update(zip(wide, pairs(FAR_Y, wide, {q: stats[q] for q in "AB"}, halves)))
    stats["D"], stats["B"] = tie((stats["D"], stats["B"]))
    parts = [stats["O"]] + [shift(stats[q], *PLACES[q]) for q in "ABCDE"]
    sent = spread(place, parts)
    back = exchange(sent)
    return unpack(back, labels, rank)


def solution(mesh):
    files = P(("tr", "tc"))
    return jax.shard_map(
        per_device,
        mesh=mesh,
        in_specs=(P(("tr", "tc"), None), files),
        out_specs=(files, files, files),
        check_vma=False,
    )
```

```python
import functools

import jax
import jax.numpy as jnp
from jax import lax
from jax.experimental import pallas as pl
from jax.experimental.pallas import tpu as pltpu
from jax.sharding import PartitionSpec as P

GROUP_SHIFT = 2
TILE_ROWS = 8
SIDE = 4
ROWS = 768
WIDTH = 1024
PIECES = (512, 512)
PIECE = PIECES[0]
CAP = 288
TAIL = 16
PAIR = CAP + TAIL
LANES = 384
BLOCK = ROWS + TAIL
SPAN = 1152
EPSILON = 1e-06
THRESHOLD = 0.3
SHARPNESS = 50.0
SCALE2 = 256.0 * 1.4426950408889634
NEGATIVE = -1e30
FLOOR = -5e29
CHUNK = 256
HALF = 384
STRIP = 32
VMEM = 24 * 1024 * 1024
PACK_VMEM = 56 * 1024 * 1024
BF = jnp.bfloat16
F32 = jnp.float32


def iota(shape, axis):
    return lax.broadcasted_iota(jnp.int32, shape, axis)


def dot(a, b):
    return lax.dot_general(a, b, (((1,), (0,)), ((), ())), preferred_element_type=F32)


def dot_nt(a, b):
    return lax.dot_general(a, b, (((1,), (1,)), ((), ())), preferred_element_type=F32)


def params(limit=VMEM):
    return pltpu.CompilerParams(vmem_limit_bytes=limit)


def whole(shape):
    return pl.BlockSpec(shape, lambda *_: (0,) * len(shape))


def vmem():
    return pl.BlockSpec(memory_space=pltpu.VMEM)


def smem():
    return pl.BlockSpec(memory_space=pltpu.SMEM)


def pick(lab_ref, rank_ref, g, slots):
    owner = lax.shift_right_logical(lab_ref[...].reshape(1, ROWS), GROUP_SHIFT)
    slot = jnp.where(owner == g, rank_ref[...], -1)
    return (iota((slots, ROWS), 0) == slot).astype(F32).astype(BF)


def pack_first_kernel(emb_ref, lab_ref, out_ref, rank_ref, *refs):
    *rests, unit = refs
    g = pl.program_id(0)
    lab = lab_ref[...].reshape(1, ROWS)

    @pl.when(g == 0)
    def _():
        values = emb_ref[...].astype(F32)
        total = jnp.sum(values * values, axis=1, keepdims=True)
        rows = (values * lax.rsqrt(total + EPSILON)).astype(BF)
        start = 0
        for ref in (unit, *rests):
            stop = start + ref.shape[1]
            ref[...] = rows[:, start:stop]
            start = stop
        owner = lax.shift_right_logical(lab, GROUP_SHIFT)
        onehot = (iota((TILE_ROWS, ROWS), 0) == owner).astype(F32)
        before = (iota((ROWS, ROWS), 0) < iota((ROWS, ROWS), 1)).astype(F32).astype(BF)
        seen = dot(onehot.astype(BF), before)
        rank_ref[...] = jnp.sum(onehot * seen, axis=0, keepdims=True).astype(jnp.int32)

    chosen = pick(lab_ref, rank_ref, g, LANES)
    out_ref[0] = dot(chosen[:PAIR], unit[...]).astype(BF)
    marks = jnp.broadcast_to(lab.astype(F32) + 1.0, (TAIL, ROWS)).astype(BF)
    out_ref[0, CAP:, :LANES] = (dot_nt(marks, chosen) - 1.0).astype(BF)
    out_ref[0, CAP:, LANES:] = jnp.zeros((TAIL, PIECE - LANES), BF)


def pack_first(embeddings, labels):
    return pl.pallas_call(
        pack_first_kernel,
        grid=(TILE_ROWS,),
        in_specs=[whole((ROWS, WIDTH)), whole((ROWS,))],
        out_specs=[
            pl.BlockSpec((1, PAIR, PIECE), lambda g: (g, 0, 0)),
            whole((1, ROWS)),
        ]
        + [whole((ROWS, w)) for w in PIECES[1:]],
        out_shape=[
            jax.ShapeDtypeStruct((TILE_ROWS, PAIR, PIECE), BF),
            jax.ShapeDtypeStruct((1, ROWS), jnp.int32),
        ]
        + [jax.ShapeDtypeStruct((ROWS, w), BF) for w in PIECES[1:]],
        scratch_shapes=[pltpu.VMEM((ROWS, PIECE), BF)],
        compiler_params=params(PACK_VMEM),
        name="pack_first",
    )(embeddings, labels)


def pack_rest_kernel(unit_ref, lab_ref, rank_ref, out_ref):
    chosen = pick(lab_ref, rank_ref, pl.program_id(0), CAP)
    out_ref[0] = dot(chosen, unit_ref[...]).astype(BF)


def pack_rest(unit, labels, rank):
    width = unit.shape[1]
    return pl.pallas_call(
        pack_rest_kernel,
        grid=(TILE_ROWS,),
        in_specs=[whole((ROWS, width)), whole((ROWS,)), whole((1, ROWS))],
        out_specs=pl.BlockSpec((1, CAP, width), lambda g: (g, 0, 0)),
        out_shape=jax.ShapeDtypeStruct((TILE_ROWS, CAP, width), BF),
        compiler_params=params(PACK_VMEM),
        cost_estimate=pl.CostEstimate(
            flops=2 * TILE_ROWS * CAP * ROWS * width,
            bytes_accessed=2 * TILE_ROWS * CAP * width,
            transcendentals=0,
        ),
        name="pack_rest",
    )(unit, labels, rank)


def close_gaps(got_ref, rows, offsets, counts):
    sent = got_ref.shape[1]
    rows[:16] = jnp.zeros((16, rows.shape[1]), BF)
    column = iota((PAIR, sent), 1)
    apart = iota((PAIR, sent), 0) - column
    for r in range(TILE_ROWS):
        base = pl.multiple_of(lax.shift_right_logical(offsets[r], 4) * 16, 16)
        move = (apart == offsets[r] - base) & (column < counts[r])
        moved = dot(move.astype(F32).astype(BF), got_ref[r]).astype(BF)
        rows[pl.ds(base, 16)] = rows[pl.ds(base, 16)] + moved[:16]
        rows[pl.ds(base + 16, PAIR - 16)] = moved[16:]


def compact_first_kernel(got_ref, out_ref, place_ref, rows):
    names = jnp.zeros((8, SPAN), F32)
    offset = jnp.int32(0)
    offsets, counts = [], []
    for r in range(TILE_ROWS):
        lab = got_ref[r, CAP:, :LANES].astype(F32)[:8]
        count = jnp.sum((lab[:1] >= 0.0).astype(F32)).astype(jnp.int32)
        held = jnp.concatenate(
            [jnp.maximum(lab, 0.0), jnp.zeros((8, SPAN - LANES), F32)], axis=1
        )
        names += pltpu.roll(held, offset, 1)
        place_ref[r] = offset
        place_ref[TILE_ROWS + r] = count
        offsets.append(offset)
        counts.append(count)
        offset = offset + count
    close_gaps(got_ref, rows, offsets, counts)
    out_ref[:ROWS] = rows[:ROWS]
    out_ref[ROWS:] = jnp.concatenate([names[:, :PIECE], names[:, PIECE : 2 * PIECE]], axis=0).astype(BF)


def compact_first(got):
    return pl.pallas_call(
        compact_first_kernel,
        in_specs=[vmem()],
        out_specs=[vmem(), smem()],
        out_shape=[
            jax.ShapeDtypeStruct((BLOCK, PIECE), BF),
            jax.ShapeDtypeStruct((2 * TILE_ROWS,), jnp.int32),
        ],
        scratch_shapes=[pltpu.VMEM((ROWS + PAIR, PIECE), BF)],
        compiler_params=params(),
        name="compact_first",
    )(got)


def compact_rest_kernel(place_ref, got_ref, out_ref, rows):
    places = [place_ref[i] for i in range(2 * TILE_ROWS)]
    close_gaps(got_ref, rows, places[:TILE_ROWS], places[TILE_ROWS:])
    out_ref[...] = rows[:ROWS]


def compact_rest(place, got):
    width = got.shape[2]
    return pl.pallas_call(
        compact_rest_kernel,
        in_specs=[smem(), vmem()],
        out_specs=vmem(),
        out_shape=jax.ShapeDtypeStruct((ROWS, width), BF),
        scratch_shapes=[pltpu.VMEM((ROWS + PAIR, width), BF)],
        compiler_params=params(),
        name="compact_rest",
    )(place, got)


def fold(tile):
    return tile.reshape(tile.shape[0] // 8, 8, tile.shape[1])


def merge(parts):
    top = functools.reduce(jnp.maximum, [p[0] for p in parts])
    factors = [jnp.exp2(p[0] - top) for p in parts]
    total = sum(p[1] * f for p, f in zip(parts, factors))
    weight = sum(p[2] * f for p, f in zip(parts, factors))
    return top, total, weight


def put_stats(ref, stats):
    for k, value in enumerate(stats):
        ref[k : k + 1] = value


def get_stats(ref):
    return tuple(ref[k : k + 1] for k in range(3))


def spread_names(block):
    tail = block[ROWS:].astype(F32)
    names = jnp.concatenate([tail[:1], tail[8:9, : ROWS - PIECE]], axis=1)
    return names, jnp.transpose(jnp.broadcast_to(names, (128, ROWS)))


def across(mark):
    return jnp.concatenate([mark] * (ROWS // 128), axis=1)


def gather_columns(top, total, weight):
    best = jnp.max(top, axis=0, keepdims=True)
    factor = jnp.exp2(top - best)
    return (
        best,
        jnp.sum(total * factor, axis=0, keepdims=True),
        jnp.sum(weight * factor, axis=0, keepdims=True),
    )


def own_kernel(block, *refs):
    *rests, out, scores = refs
    names, marks = spread_names(block)
    top = jnp.full((8, ROWS), FLOOR, F32)
    for start in range(0, ROWS, CHUNK):
        sims = dot_nt(block[start : start + CHUNK], block[:ROWS])
        for rest in rests:
            sims += dot_nt(rest[start : start + CHUNK], rest[...])
        sims = sims * SCALE2
        mask = (across(marks[start : start + CHUNK]) == names) & (
            iota((CHUNK, ROWS), 0) + start != iota((CHUNK, ROWS), 1)
        )
        sims = jnp.where(mask, sims, NEGATIVE)
        scores[start : start + CHUNK] = sims
        top = jnp.maximum(top, jnp.max(fold(sims), axis=0))
    total = jnp.zeros((8, ROWS), F32)
    weight = jnp.zeros((8, ROWS), F32)
    for start in range(0, ROWS, STRIP):
        sims = scores[start : start + STRIP]
        terms = jnp.exp2(fold(sims) - top)
        total += jnp.sum(terms, axis=0)
        weight += jnp.sum(terms * fold(sims), axis=0)
    put_stats(out, gather_columns(top, total, weight))


def own_pairs(pieces):
    return pl.pallas_call(
        own_kernel,
        out_shape=jax.ShapeDtypeStruct((8, ROWS), F32),
        in_specs=[vmem()] * len(pieces),
        out_specs=vmem(),
        scratch_shapes=[pltpu.VMEM((ROWS, ROWS), F32)],
        compiler_params=params(),
        cost_estimate=pl.CostEstimate(
            flops=2 * ROWS * ROWS * WIDTH,
            bytes_accessed=2 * BLOCK * WIDTH,
            transcendentals=ROWS * ROWS,
        ),
        name="own",
    )(*pieces)


def pair_kernel(plan, blocks, old, half_ref, *refs):
    n, n_old = len(blocks), len(old)
    m = len(PIECES)
    pieces = [refs[i * n : (i + 1) * n] for i in range(m)]
    ins, olds = pieces[0], refs[m * n : m * n + n_old]
    outs = refs[m * n + n_old : (m + 1) * n + n_old]
    marks, names, rows, tops, totals, weights, scores0, scores1 = refs[(m + 1) * n + n_old :]
    scores = (scores0, scores1)
    place = {b: i for i, b in enumerate(blocks)}
    lane = iota((1, 128), 1)
    empty = jnp.where(lane % 4 == 0, NEGATIVE, 0.0)
    for i in range(n):
        rows[i] = jnp.broadcast_to(empty, (ROWS, 128))
    tops[...] = jnp.full((n, 8, ROWS), FLOOR, F32)
    totals[...] = jnp.zeros((n, 8, ROWS), F32)
    weights[...] = jnp.zeros((n, 8, ROWS), F32)
    ready = set()

    def need(i):
        if i not in ready:
            ready.add(i)
            one, many = spread_names(ins[i])
            names[i] = jnp.broadcast_to(one, (8, ROWS))
            marks[i] = many

    steps = []
    for k, (left, right, axis) in enumerate(plan):
        left, right = place[left], place[right]
        if axis is None:
            steps += [(k, left, right, s, (left, right), None) for s in (0, HALF)]
        else:
            half = half_ref[axis]
            first = jnp.where(half == 0, left, right)
            second = jnp.where(half == 0, right, left)
            start = pl.multiple_of(half * HALF, HALF)
            steps.append((k, first, second, start, (left, right), half == 0))

    def product(step, out):
        _, _, _, start, both, first = step
        for i in both:
            need(i)
        here = pl.ds(start, HALF)

        def multiply(pieces):
            left, right = pieces[both[0]], pieces[both[1]]
            if first is None:
                return dot_nt(left[here], right[:ROWS])
            keys = jnp.where(first, left[here], right[here])
            return dot_nt(keys, jnp.where(first, right[:ROWS], left[:ROWS]))

        out[...] = sum(multiply(p) for p in pieces)

    def reduce(step, data):
        k, left, right, start, _, _ = step
        name = names[right][:1]
        top = tops[right]
        peak = top
        for at in range(0, HALF, STRIP):
            here = pl.ds(start + at, STRIP)
            mask = across(marks[left, here]) == name
            sims = jnp.where(mask, data[at : at + STRIP] * SCALE2, NEGATIVE)
            data[at : at + STRIP] = sims
            peak = jnp.maximum(peak, jnp.max(fold(sims), axis=0))
            best = jnp.maximum(jnp.max(sims, axis=1, keepdims=True), FLOOR)
            terms = jnp.exp2(sims - best)
            total = jnp.sum(terms, axis=1, keepdims=True)
            weight = jnp.sum(terms * sims, axis=1, keepdims=True)
            rows[left, here] = jnp.where(
                lane == 4 * k,
                best,
                jnp.where(
                    lane == 4 * k + 1, total, jnp.where(lane == 4 * k + 2, weight, rows[left, here])
                ),
            )
        factor = jnp.exp2(top - peak)
        total = totals[right] * factor
        weight = weights[right] * factor
        for at in range(0, HALF, STRIP):
            sims = fold(data[at : at + STRIP])
            terms = jnp.exp2(sims - peak)
            total += jnp.sum(terms, axis=0)
            weight += jnp.sum(terms * sims, axis=0)
        tops[right] = peak
        totals[right] = total
        weights[right] = weight

    product(steps[0], scores[0])
    for t, step in enumerate(steps):
        if t + 1 < len(steps):
            product(steps[t + 1], scores[(t + 1) % 2])
        reduce(step, scores[t % 2])

    for i, b in enumerate(blocks):
        parts = [gather_columns(tops[i], totals[i], weights[i])]
        mine = [k for k, (left, right, axis) in enumerate(plan) if left == b or (axis is not None and right == b)]
        if mine:
            turned = jnp.transpose(rows[i])
            parts += [tuple(turned[4 * k + j : 4 * k + j + 1] for j in range(3)) for k in mine]
        if b in old:
            parts.append(get_stats(olds[old.index(b)]))
        put_stats(outs[i], merge(parts))


def pairs(plan, blocks, old, halves):
    names, n = list(blocks), len(blocks)
    steps = sum(2 if axis is None else 1 for _, _, axis in plan)
    return pl.pallas_call(
        functools.partial(pair_kernel, plan, names, list(old)),
        out_shape=[jax.ShapeDtypeStruct((8, ROWS), F32)] * n,
        in_specs=[smem()] + [vmem()] * (len(PIECES) * n) + [vmem()] * len(old),
        out_specs=[vmem()] * n,
        scratch_shapes=[
            pltpu.VMEM((n, ROWS, 128), F32),
            pltpu.VMEM((n, 8, ROWS), F32),
            pltpu.VMEM((n, ROWS, 128), F32),
            pltpu.VMEM((n, 8, ROWS), F32),
            pltpu.VMEM((n, 8, ROWS), F32),
            pltpu.VMEM((n, 8, ROWS), F32),
            pltpu.VMEM((HALF, ROWS), F32),
            pltpu.VMEM((HALF, ROWS), F32),
        ],
        compiler_params=params(),
        cost_estimate=pl.CostEstimate(
            flops=2 * steps * HALF * ROWS * WIDTH,
            bytes_accessed=2 * n * BLOCK * WIDTH,
            transcendentals=2 * steps * HALF * ROWS,
        ),
        name="pairs",
    )(halves, *[b[i] for i in range(len(PIECES)) for b in blocks.values()], *old.values())


def spread_kernel(offset_ref, *refs):
    out_ref = refs[-1]
    top, total, weight = merge([get_stats(r) for r in refs[:-1]])
    best = top / SCALE2
    mean = weight / total / SCALE2
    row = iota((8, ROWS), 0)
    values = jnp.where(row == 0, best, jnp.where(row == 1, mean, 0.0))
    values = jnp.concatenate([values, jnp.zeros((8, SPAN - ROWS), F32)], axis=1)
    for r in range(TILE_ROWS):
        offset = offset_ref[r]
        moved = pltpu.roll(values, lax.rem(SPAN - offset, SPAN), 1)
        for k in range(6):
            lanes = slice(k % 3 * 128, k % 3 * 128 + 128)
            out_ref[r, k : k + 1] = moved[k // 3 : k // 3 + 1, lanes]
        out_ref[r, 6:] = jnp.zeros((2, 128), F32)


def spread(offsets, stats):
    return pl.pallas_call(
        spread_kernel,
        out_shape=jax.ShapeDtypeStruct((TILE_ROWS, 8, 128), F32),
        in_specs=[pl.BlockSpec(memory_space=pltpu.SMEM)]
        + [pl.BlockSpec(memory_space=pltpu.VMEM)] * len(stats),
        out_specs=pl.BlockSpec(memory_space=pltpu.VMEM),
        compiler_params=params(),
        name="spread",
    )(offsets, *stats)


def unpack_kernel(back_ref, lab_ref, rank_ref, best_ref, mean_ref, flag_ref):
    found = jnp.zeros((24, ROWS), F32)
    for g in range(TILE_ROWS):
        chosen = pick(lab_ref, rank_ref, g, LANES)
        rows = [back_ref[g, k : k + 1] for k in range(6)]
        best, mean = jnp.concatenate(rows[:3], axis=1), jnp.concatenate(rows[3:], axis=1)
        values = jnp.concatenate([best, mean, jnp.zeros((6, LANES), F32)], axis=0)
        high = values.astype(BF).astype(F32)
        mid = (values - high).astype(BF).astype(F32)
        low = values - high - mid
        found += dot(jnp.concatenate([high, mid, low], axis=0).astype(BF), chosen)
    found = found[:8] + (found[8:16] + found[16:])
    best = found[:1]
    best_ref[...] = best.reshape(ROWS)
    mean_ref[...] = found[1:2].reshape(ROWS)
    flag_ref[...] = (1.0 / (1.0 + jnp.exp(-SHARPNESS * (best - THRESHOLD)))).reshape(ROWS)


def unpack(back, labels, rank):
    return pl.pallas_call(
        unpack_kernel,
        out_shape=[jax.ShapeDtypeStruct((ROWS,), F32)] * 3,
        in_specs=[pl.BlockSpec(memory_space=pltpu.VMEM)] * 3,
        out_specs=[pl.BlockSpec(memory_space=pltpu.VMEM)] * 3,
        compiler_params=params(),
        name="unpack",
    )(back, labels, rank)


def shift(array, dx, dy):
    moves = []
    for tr in range(TILE_ROWS):
        sign = 1 - 2 * (tr % 2)
        for x in range(SIDE):
            for y in range(SIDE):
                to = ((x + sign * dx) % SIDE) * SIDE + (y + sign * dy) % SIDE
                base = tr * SIDE * SIDE
                moves.append((base + x * SIDE + y, base + to))
    return lax.ppermute(array, ("tr", "tc"), moves)


PLACES = {"O": (0, 0), "A": (1, 0), "B": (2, 0), "C": (0, 1), "D": (0, -1), "E": (0, 2)}
FIRST = [("O", "A", None)]
NEAR = [("O", "C", None), ("A", "C", None), ("D", "A", None), ("C", "D", 1)]
FAR_X = [("B", "O", 0), ("B", "C", None)]
FAR_Y = [("E", "A", None), ("E", "B", 0)]


def per_device(embeddings, labels):
    tie = lax.optimization_barrier
    tc = lax.axis_index("tc")
    halves = jnp.stack([tc // (2 * SIDE), (tc % SIDE) // 2]).astype(jnp.int32)

    def exchange(packed):
        return lax.all_to_all(packed, "tr", split_axis=0, concat_axis=0, tiled=True)

    packed, rank, *units = pack_first(embeddings, labels)
    got = exchange(packed)
    blocks = {q: [] for q in "OABCDE"}
    place = None
    last = len(PIECES) - 1
    for k in range(len(PIECES)):
        if k < last:
            packed = pack_rest(units[k], labels, rank)
            packed, got = tie((packed, got))
            later = exchange(packed)
        if k == 0:
            mine, place = compact_first(got)
        else:
            mine = compact_rest(place, got)
        a, c, d = shift(mine, -1, 0), shift(mine, 0, -1), shift(mine, 0, 1)
        if k == last:
            here, blocks["E"][-1] = tie((mine, blocks["E"][-1]))
            own = own_pairs([*blocks["O"], here])
            a, own, halves = tie((a, own, halves))
        b = shift(a, -1, 0)
        if k == last:
            sides = {"O": [*blocks["O"], mine], "A": [*blocks["A"], a]}
            stats = dict(zip(sides, pairs(FIRST, sides, {"O": own}, halves)))
            d, stats["O"] = tie((d, stats["O"]))
        e = shift(d, 0, 1)
        if k < last:
            got, d, c, b, a = tie((later, d, c, b, a))
        for q, piece in zip("OABCDE", (mine, a, b, c, d, e)):
            blocks[q].append(piece)
    near = {q: blocks[q] for q in "OACD"}
    stats.update(zip(near, pairs(NEAR, near, stats, halves)))
    wide = {q: blocks[q] for q in "OCB"}
    stats.update(zip(wide, pairs(FAR_X, wide, {q: stats[q] for q in "OC"}, halves)))
    wide = {q: blocks[q] for q in "ABE"}
    stats.update(zip(wide, pairs(FAR_Y, wide, {q: stats[q] for q in "AB"}, halves)))
    stats["D"], stats["B"] = tie((stats["D"], stats["B"]))
    parts = [stats["O"]] + [shift(stats[q], *PLACES[q]) for q in "ABCDE"]
    sent = spread(place, parts)
    back = exchange(sent)
    return unpack(back, labels, rank)


def solution(mesh):
    files = P(("tr", "tc"))
    return jax.shard_map(
        per_device,
        mesh=mesh,
        in_specs=(P(("tr", "tc"), None), files),
        out_specs=(files, files, files),
        check_vma=False,
    )
```

```python
import functools

import jax
import jax.numpy as jnp
from jax import lax
from jax.experimental import pallas as pl
from jax.experimental.pallas import tpu as pltpu
from jax.sharding import PartitionSpec as P

GROUP_SHIFT = 2
TILE_ROWS = 8
SIDE = 4
ROWS = 768
WIDTH = 1024
PIECES = (512, 512)
PIECE = PIECES[0]
CAP = 288
TAIL = 16
PAIR = CAP + TAIL
LANES = 384
BLOCK = ROWS + TAIL
SPAN = 1152
EPSILON = 1e-06
THRESHOLD = 0.3
SHARPNESS = 50.0
SCALE2 = 256.0 * 1.4426950408889634
NEGATIVE = -1e30
FLOOR = -5e29
CHUNK = 256
HALF = 384
AT_ONCE = 2
STRIP = 32
VMEM = 24 * 1024 * 1024
PACK_VMEM = 56 * 1024 * 1024
BF = jnp.bfloat16
F32 = jnp.float32


def iota(shape, axis):
    return lax.broadcasted_iota(jnp.int32, shape, axis)


def dot(a, b):
    return lax.dot_general(a, b, (((1,), (0,)), ((), ())), preferred_element_type=F32)


def dot_nt(a, b):
    return lax.dot_general(a, b, (((1,), (1,)), ((), ())), preferred_element_type=F32)


def params(limit=VMEM):
    return pltpu.CompilerParams(vmem_limit_bytes=limit)


def whole(shape):
    return pl.BlockSpec(shape, lambda *_: (0,) * len(shape))


def vmem():
    return pl.BlockSpec(memory_space=pltpu.VMEM)


def smem():
    return pl.BlockSpec(memory_space=pltpu.SMEM)


def pick(lab_ref, rank_ref, g, slots):
    owner = lax.shift_right_logical(lab_ref[...].reshape(1, ROWS), GROUP_SHIFT)
    slot = jnp.where(owner == g, rank_ref[...], -1)
    return (iota((slots, ROWS), 0) == slot).astype(F32).astype(BF)


def pack_first_kernel(emb_ref, lab_ref, out_ref, rank_ref, *refs):
    *rests, unit = refs
    g = pl.program_id(0)
    lab = lab_ref[...].reshape(1, ROWS)

    @pl.when(g == 0)
    def _():
        values = emb_ref[...].astype(F32)
        total = jnp.sum(values * values, axis=1, keepdims=True)
        rows = (values * lax.rsqrt(total + EPSILON)).astype(BF)
        start = 0
        for ref in (unit, *rests):
            stop = start + ref.shape[1]
            ref[...] = rows[:, start:stop]
            start = stop
        owner = lax.shift_right_logical(lab, GROUP_SHIFT)
        onehot = (iota((TILE_ROWS, ROWS), 0) == owner).astype(F32)
        before = (iota((ROWS, ROWS), 0) < iota((ROWS, ROWS), 1)).astype(F32).astype(BF)
        seen = dot(onehot.astype(BF), before)
        rank_ref[...] = jnp.sum(onehot * seen, axis=0, keepdims=True).astype(jnp.int32)

    marks = jnp.broadcast_to(lab.astype(F32) + 1.0, (TAIL, ROWS)).astype(BF)
    for k in range(AT_ONCE):
        chosen = pick(lab_ref, rank_ref, g * AT_ONCE + k, LANES)
        out_ref[k] = dot(chosen[:PAIR], unit[...]).astype(BF)
        out_ref[k, CAP:, :LANES] = (dot_nt(marks, chosen) - 1.0).astype(BF)
        out_ref[k, CAP:, LANES:] = jnp.zeros((TAIL, PIECE - LANES), BF)


def pack_first(embeddings, labels):
    return pl.pallas_call(
        pack_first_kernel,
        grid=(TILE_ROWS // AT_ONCE,),
        in_specs=[whole((ROWS, WIDTH)), whole((ROWS,))],
        out_specs=[
            pl.BlockSpec((AT_ONCE, PAIR, PIECE), lambda g: (g, 0, 0)),
            whole((1, ROWS)),
        ]
        + [whole((ROWS, w)) for w in PIECES[1:]],
        out_shape=[
            jax.ShapeDtypeStruct((TILE_ROWS, PAIR, PIECE), BF),
            jax.ShapeDtypeStruct((1, ROWS), jnp.int32),
        ]
        + [jax.ShapeDtypeStruct((ROWS, w), BF) for w in PIECES[1:]],
        scratch_shapes=[pltpu.VMEM((ROWS, PIECE), BF)],
        compiler_params=params(PACK_VMEM),
        name="pack_first",
    )(embeddings, labels)


def pack_rest_kernel(unit_ref, lab_ref, rank_ref, out_ref):
    chosen = pick(lab_ref, rank_ref, pl.program_id(0), CAP)
    out_ref[0] = dot(chosen, unit_ref[...]).astype(BF)


def pack_rest(unit, labels, rank):
    width = unit.shape[1]
    return pl.pallas_call(
        pack_rest_kernel,
        grid=(TILE_ROWS,),
        in_specs=[whole((ROWS, width)), whole((ROWS,)), whole((1, ROWS))],
        out_specs=pl.BlockSpec((1, CAP, width), lambda g: (g, 0, 0)),
        out_shape=jax.ShapeDtypeStruct((TILE_ROWS, CAP, width), BF),
        compiler_params=params(PACK_VMEM),
        cost_estimate=pl.CostEstimate(
            flops=2 * TILE_ROWS * CAP * ROWS * width,
            bytes_accessed=2 * TILE_ROWS * CAP * width,
            transcendentals=0,
        ),
        name="pack_rest",
    )(unit, labels, rank)


def close_gaps(got_ref, rows, offsets, counts):
    sent = got_ref.shape[1]
    rows[:16] = jnp.zeros((16, rows.shape[1]), BF)
    column = iota((PAIR, sent), 1)
    apart = iota((PAIR, sent), 0) - column
    for r in range(TILE_ROWS):
        base = pl.multiple_of(lax.shift_right_logical(offsets[r], 4) * 16, 16)
        move = (apart == offsets[r] - base) & (column < counts[r])
        moved = dot(move.astype(F32).astype(BF), got_ref[r]).astype(BF)
        rows[pl.ds(base, 16)] = rows[pl.ds(base, 16)] + moved[:16]
        rows[pl.ds(base + 16, PAIR - 16)] = moved[16:]


def compact_first_kernel(got_ref, out_ref, place_ref, rows):
    names = jnp.zeros((8, SPAN), F32)
    offset = jnp.int32(0)
    offsets, counts = [], []
    for r in range(TILE_ROWS):
        lab = got_ref[r, CAP:, :LANES].astype(F32)[:8]
        count = jnp.sum((lab[:1] >= 0.0).astype(F32)).astype(jnp.int32)
        held = jnp.concatenate(
            [jnp.maximum(lab, 0.0), jnp.zeros((8, SPAN - LANES), F32)], axis=1
        )
        names += pltpu.roll(held, offset, 1)
        place_ref[r] = offset
        place_ref[TILE_ROWS + r] = count
        offsets.append(offset)
        counts.append(count)
        offset = offset + count
    close_gaps(got_ref, rows, offsets, counts)
    out_ref[:ROWS] = rows[:ROWS]
    out_ref[ROWS:] = jnp.concatenate([names[:, :PIECE], names[:, PIECE : 2 * PIECE]], axis=0).astype(BF)


def compact_first(got):
    return pl.pallas_call(
        compact_first_kernel,
        in_specs=[vmem()],
        out_specs=[vmem(), smem()],
        out_shape=[
            jax.ShapeDtypeStruct((BLOCK, PIECE), BF),
            jax.ShapeDtypeStruct((2 * TILE_ROWS,), jnp.int32),
        ],
        scratch_shapes=[pltpu.VMEM((ROWS + PAIR, PIECE), BF)],
        compiler_params=params(),
        name="compact_first",
    )(got)


def compact_rest_kernel(place_ref, got_ref, out_ref, rows):
    places = [place_ref[i] for i in range(2 * TILE_ROWS)]
    close_gaps(got_ref, rows, places[:TILE_ROWS], places[TILE_ROWS:])
    out_ref[...] = rows[:ROWS]


def compact_rest(place, got):
    width = got.shape[2]
    return pl.pallas_call(
        compact_rest_kernel,
        in_specs=[smem(), vmem()],
        out_specs=vmem(),
        out_shape=jax.ShapeDtypeStruct((ROWS, width), BF),
        scratch_shapes=[pltpu.VMEM((ROWS + PAIR, width), BF)],
        compiler_params=params(),
        name="compact_rest",
    )(place, got)


def fold(tile):
    return tile.reshape(tile.shape[0] // 8, 8, tile.shape[1])


def merge(parts):
    top = functools.reduce(jnp.maximum, [p[0] for p in parts])
    factors = [jnp.exp2(p[0] - top) for p in parts]
    total = sum(p[1] * f for p, f in zip(parts, factors))
    weight = sum(p[2] * f for p, f in zip(parts, factors))
    return top, total, weight


def put_stats(ref, stats):
    for k, value in enumerate(stats):
        ref[k : k + 1] = value


def get_stats(ref):
    return tuple(ref[k : k + 1] for k in range(3))


def spread_names(block):
    tail = block[ROWS:].astype(F32)
    names = jnp.concatenate([tail[:1], tail[8:9, : ROWS - PIECE]], axis=1)
    return names, jnp.transpose(jnp.broadcast_to(names, (128, ROWS)))


def across(mark):
    return jnp.concatenate([mark] * (ROWS // 128), axis=1)


def gather_columns(top, total, weight):
    best = jnp.max(top, axis=0, keepdims=True)
    factor = jnp.exp2(top - best)
    return (
        best,
        jnp.sum(total * factor, axis=0, keepdims=True),
        jnp.sum(weight * factor, axis=0, keepdims=True),
    )


def own_kernel(block, *refs):
    *rests, out, scores = refs
    names, marks = spread_names(block)
    top = jnp.full((8, ROWS), FLOOR, F32)
    for start in range(0, ROWS, CHUNK):
        sims = dot_nt(block[start : start + CHUNK], block[:ROWS])
        for rest in rests:
            sims += dot_nt(rest[start : start + CHUNK], rest[...])
        sims = sims * SCALE2
        mask = (across(marks[start : start + CHUNK]) == names) & (
            iota((CHUNK, ROWS), 0) + start != iota((CHUNK, ROWS), 1)
        )
        sims = jnp.where(mask, sims, NEGATIVE)
        scores[start : start + CHUNK] = sims
        top = jnp.maximum(top, jnp.max(fold(sims), axis=0))
    total = jnp.zeros((8, ROWS), F32)
    weight = jnp.zeros((8, ROWS), F32)
    for start in range(0, ROWS, STRIP):
        sims = scores[start : start + STRIP]
        terms = jnp.exp2(fold(sims) - top)
        total += jnp.sum(terms, axis=0)
        weight += jnp.sum(terms * fold(sims), axis=0)
    put_stats(out, gather_columns(top, total, weight))


def own_pairs(pieces):
    return pl.pallas_call(
        own_kernel,
        out_shape=jax.ShapeDtypeStruct((8, ROWS), F32),
        in_specs=[vmem()] * len(pieces),
        out_specs=vmem(),
        scratch_shapes=[pltpu.VMEM((ROWS, ROWS), F32)],
        compiler_params=params(),
        cost_estimate=pl.CostEstimate(
            flops=2 * ROWS * ROWS * WIDTH,
            bytes_accessed=2 * BLOCK * WIDTH,
            transcendentals=ROWS * ROWS,
        ),
        name="own",
    )(*pieces)


def pair_kernel(plan, blocks, old, half_ref, *refs):
    n, n_old = len(blocks), len(old)
    m = len(PIECES)
    pieces = [refs[i * n : (i + 1) * n] for i in range(m)]
    ins, olds = pieces[0], refs[m * n : m * n + n_old]
    outs = refs[m * n + n_old : (m + 1) * n + n_old]
    marks, names, rows, tops, totals, weights, scores0, scores1 = refs[(m + 1) * n + n_old :]
    scores = (scores0, scores1)
    place = {b: i for i, b in enumerate(blocks)}
    lane = iota((1, 128), 1)
    empty = jnp.where(lane % 4 == 0, NEGATIVE, 0.0)
    for i in range(n):
        rows[i] = jnp.broadcast_to(empty, (ROWS, 128))
    tops[...] = jnp.full((n, 8, ROWS), FLOOR, F32)
    totals[...] = jnp.zeros((n, 8, ROWS), F32)
    weights[...] = jnp.zeros((n, 8, ROWS), F32)
    ready = set()

    def need(i):
        if i not in ready:
            ready.add(i)
            one, many = spread_names(ins[i])
            names[i] = jnp.broadcast_to(one, (8, ROWS))
            marks[i] = many

    steps = []
    for k, (left, right, axis) in enumerate(plan):
        left, right = place[left], place[right]
        if axis is None:
            steps += [(k, left, right, s, (left, right), None) for s in (0, HALF)]
        else:
            half = half_ref[axis]
            first = jnp.where(half == 0, left, right)
            second = jnp.where(half == 0, right, left)
            start = pl.multiple_of(half * HALF, HALF)
            steps.append((k, first, second, start, (left, right), half == 0))

    def product(step, out):
        _, _, _, start, both, first = step
        for i in both:
            need(i)
        here = pl.ds(start, HALF)

        def multiply(pieces):
            left, right = pieces[both[0]], pieces[both[1]]
            if first is None:
                return dot_nt(left[here], right[:ROWS])
            keys = jnp.where(first, left[here], right[here])
            return dot_nt(keys, jnp.where(first, right[:ROWS], left[:ROWS]))

        out[...] = sum(multiply(p) for p in pieces)

    def reduce(step, data):
        k, left, right, start, _, _ = step
        name = names[right][:1]
        top = tops[right]
        peak = top
        for at in range(0, HALF, STRIP):
            here = pl.ds(start + at, STRIP)
            mask = across(marks[left, here]) == name
            sims = jnp.where(mask, data[at : at + STRIP] * SCALE2, NEGATIVE)
            data[at : at + STRIP] = sims
            peak = jnp.maximum(peak, jnp.max(fold(sims), axis=0))
            best = jnp.maximum(jnp.max(sims, axis=1, keepdims=True), FLOOR)
            terms = jnp.exp2(sims - best)
            total = jnp.sum(terms, axis=1, keepdims=True)
            weight = jnp.sum(terms * sims, axis=1, keepdims=True)
            rows[left, here] = jnp.where(
                lane == 4 * k,
                best,
                jnp.where(
                    lane == 4 * k + 1, total, jnp.where(lane == 4 * k + 2, weight, rows[left, here])
                ),
            )
        factor = jnp.exp2(top - peak)
        total = totals[right] * factor
        weight = weights[right] * factor
        for at in range(0, HALF, STRIP):
            sims = fold(data[at : at + STRIP])
            terms = jnp.exp2(sims - peak)
            total += jnp.sum(terms, axis=0)
            weight += jnp.sum(terms * sims, axis=0)
        tops[right] = peak
        totals[right] = total
        weights[right] = weight

    product(steps[0], scores[0])
    for t, step in enumerate(steps):
        if t + 1 < len(steps):
            product(steps[t + 1], scores[(t + 1) % 2])
        reduce(step, scores[t % 2])

    for i, b in enumerate(blocks):
        parts = [gather_columns(tops[i], totals[i], weights[i])]
        mine = [k for k, (left, right, axis) in enumerate(plan) if left == b or (axis is not None and right == b)]
        if mine:
            turned = jnp.transpose(rows[i])
            parts += [tuple(turned[4 * k + j : 4 * k + j + 1] for j in range(3)) for k in mine]
        if b in old:
            parts.append(get_stats(olds[old.index(b)]))
        put_stats(outs[i], merge(parts))


def pairs(plan, blocks, old, halves):
    names, n = list(blocks), len(blocks)
    steps = sum(2 if axis is None else 1 for _, _, axis in plan)
    return pl.pallas_call(
        functools.partial(pair_kernel, plan, names, list(old)),
        out_shape=[jax.ShapeDtypeStruct((8, ROWS), F32)] * n,
        in_specs=[smem()] + [vmem()] * (len(PIECES) * n) + [vmem()] * len(old),
        out_specs=[vmem()] * n,
        scratch_shapes=[
            pltpu.VMEM((n, ROWS, 128), F32),
            pltpu.VMEM((n, 8, ROWS), F32),
            pltpu.VMEM((n, ROWS, 128), F32),
            pltpu.VMEM((n, 8, ROWS), F32),
            pltpu.VMEM((n, 8, ROWS), F32),
            pltpu.VMEM((n, 8, ROWS), F32),
            pltpu.VMEM((HALF, ROWS), F32),
            pltpu.VMEM((HALF, ROWS), F32),
        ],
        compiler_params=params(),
        cost_estimate=pl.CostEstimate(
            flops=2 * steps * HALF * ROWS * WIDTH,
            bytes_accessed=2 * n * BLOCK * WIDTH,
            transcendentals=2 * steps * HALF * ROWS,
        ),
        name="pairs",
    )(halves, *[b[i] for i in range(len(PIECES)) for b in blocks.values()], *old.values())


def spread_kernel(offset_ref, *refs):
    out_ref = refs[-1]
    top, total, weight = merge([get_stats(r) for r in refs[:-1]])
    best = top / SCALE2
    mean = weight / total / SCALE2
    row = iota((8, ROWS), 0)
    values = jnp.where(row == 0, best, jnp.where(row == 1, mean, 0.0))
    values = jnp.concatenate([values, jnp.zeros((8, SPAN - ROWS), F32)], axis=1)
    for r in range(TILE_ROWS):
        offset = offset_ref[r]
        moved = pltpu.roll(values, lax.rem(SPAN - offset, SPAN), 1)
        for k in range(6):
            lanes = slice(k % 3 * 128, k % 3 * 128 + 128)
            out_ref[r, k : k + 1] = moved[k // 3 : k // 3 + 1, lanes]
        out_ref[r, 6:] = jnp.zeros((2, 128), F32)


def spread(offsets, stats):
    return pl.pallas_call(
        spread_kernel,
        out_shape=jax.ShapeDtypeStruct((TILE_ROWS, 8, 128), F32),
        in_specs=[pl.BlockSpec(memory_space=pltpu.SMEM)]
        + [pl.BlockSpec(memory_space=pltpu.VMEM)] * len(stats),
        out_specs=pl.BlockSpec(memory_space=pltpu.VMEM),
        compiler_params=params(),
        name="spread",
    )(offsets, *stats)


def unpack_kernel(back_ref, lab_ref, rank_ref, best_ref, mean_ref, flag_ref):
    found = jnp.zeros((24, ROWS), F32)
    for g in range(TILE_ROWS):
        chosen = pick(lab_ref, rank_ref, g, LANES)
        rows = [back_ref[g, k : k + 1] for k in range(6)]
        best, mean = jnp.concatenate(rows[:3], axis=1), jnp.concatenate(rows[3:], axis=1)
        values = jnp.concatenate([best, mean, jnp.zeros((6, LANES), F32)], axis=0)
        high = values.astype(BF).astype(F32)
        mid = (values - high).astype(BF).astype(F32)
        low = values - high - mid
        found += dot(jnp.concatenate([high, mid, low], axis=0).astype(BF), chosen)
    found = found[:8] + (found[8:16] + found[16:])
    best = found[:1]
    best_ref[...] = best.reshape(ROWS)
    mean_ref[...] = found[1:2].reshape(ROWS)
    flag_ref[...] = (1.0 / (1.0 + jnp.exp(-SHARPNESS * (best - THRESHOLD)))).reshape(ROWS)


def unpack(back, labels, rank):
    return pl.pallas_call(
        unpack_kernel,
        out_shape=[jax.ShapeDtypeStruct((ROWS,), F32)] * 3,
        in_specs=[pl.BlockSpec(memory_space=pltpu.VMEM)] * 3,
        out_specs=[pl.BlockSpec(memory_space=pltpu.VMEM)] * 3,
        compiler_params=params(),
        name="unpack",
    )(back, labels, rank)


def shift(array, dx, dy):
    moves = []
    for tr in range(TILE_ROWS):
        sign = 1 - 2 * (tr % 2)
        for x in range(SIDE):
            for y in range(SIDE):
                to = ((x + sign * dx) % SIDE) * SIDE + (y + sign * dy) % SIDE
                base = tr * SIDE * SIDE
                moves.append((base + x * SIDE + y, base + to))
    return lax.ppermute(array, ("tr", "tc"), moves)


PLACES = {"O": (0, 0), "A": (1, 0), "B": (2, 0), "C": (0, 1), "D": (0, -1), "E": (0, 2)}
FIRST = [("O", "A", None)]
NEAR = [("O", "C", None), ("A", "C", None), ("D", "A", None), ("C", "D", 1)]
FAR_X = [("B", "O", 0), ("B", "C", None)]
FAR_Y = [("E", "A", None), ("E", "B", 0)]


def per_device(embeddings, labels):
    tie = lax.optimization_barrier
    tc = lax.axis_index("tc")
    halves = jnp.stack([tc // (2 * SIDE), (tc % SIDE) // 2]).astype(jnp.int32)

    def exchange(packed):
        return lax.all_to_all(packed, "tr", split_axis=0, concat_axis=0, tiled=True)

    packed, rank, *units = pack_first(embeddings, labels)
    got = exchange(packed)
    blocks = {q: [] for q in "OABCDE"}
    place = None
    last = len(PIECES) - 1
    for k in range(len(PIECES)):
        if k < last:
            packed = pack_rest(units[k], labels, rank)
            packed, got = tie((packed, got))
            later = exchange(packed)
        if k == 0:
            mine, place = compact_first(got)
        else:
            mine = compact_rest(place, got)
        a, c, d = shift(mine, -1, 0), shift(mine, 0, -1), shift(mine, 0, 1)
        if k == last:
            here, blocks["E"][-1] = tie((mine, blocks["E"][-1]))
            own = own_pairs([*blocks["O"], here])
            a, own, halves = tie((a, own, halves))
        b = shift(a, -1, 0)
        if k == last:
            sides = {"O": [*blocks["O"], mine], "A": [*blocks["A"], a]}
            stats = dict(zip(sides, pairs(FIRST, sides, {"O": own}, halves)))
            d, stats["O"] = tie((d, stats["O"]))
        e = shift(d, 0, 1)
        if k < last:
            got, d, c, b, a = tie((later, d, c, b, a))
        for q, piece in zip("OABCDE", (mine, a, b, c, d, e)):
            blocks[q].append(piece)
    near = {q: blocks[q] for q in "OACD"}
    stats.update(zip(near, pairs(NEAR, near, stats, halves)))
    wide = {q: blocks[q] for q in "OCB"}
    stats.update(zip(wide, pairs(FAR_X, wide, {q: stats[q] for q in "OC"}, halves)))
    wide = {q: blocks[q] for q in "ABE"}
    stats.update(zip(wide, pairs(FAR_Y, wide, {q: stats[q] for q in "AB"}, halves)))
    stats["D"], stats["B"] = tie((stats["D"], stats["B"]))
    parts = [stats["O"]] + [shift(stats[q], *PLACES[q]) for q in "ABCDE"]
    sent = spread(place, parts)
    back = exchange(sent)
    return unpack(back, labels, rank)


def solution(mesh):
    files = P(("tr", "tc"))
    return jax.shard_map(
        per_device,
        mesh=mesh,
        in_specs=(P(("tr", "tc"), None), files),
        out_specs=(files, files, files),
        check_vma=False,
    )
```

```python
import functools

import jax
import jax.numpy as jnp
from jax import lax
from jax.experimental import pallas as pl
from jax.experimental.pallas import tpu as pltpu
from jax.sharding import PartitionSpec as P

GROUP_SHIFT = 2
TILE_ROWS = 8
SIDE = 4
ROWS = 768
WIDTH = 1024
PIECES = (512, 512)
PIECE = PIECES[0]
CAP = 288
TAIL = 16
PAIR = CAP + TAIL
LANES = 384
BLOCK = ROWS + TAIL
SPAN = 1152
EPSILON = 1e-06
THRESHOLD = 0.3
SHARPNESS = 50.0
SCALE2 = 256.0 * 1.4426950408889634
NEGATIVE = -1e30
FLOOR = -5e29
CHUNK = 256
HALF = 384
AT_ONCE = 2
STRIP = 32
VMEM = 24 * 1024 * 1024
PACK_VMEM = 56 * 1024 * 1024
BF = jnp.bfloat16
F32 = jnp.float32


def iota(shape, axis):
    return lax.broadcasted_iota(jnp.int32, shape, axis)


def dot(a, b):
    return lax.dot_general(a, b, (((1,), (0,)), ((), ())), preferred_element_type=F32)


def dot_nt(a, b):
    return lax.dot_general(a, b, (((1,), (1,)), ((), ())), preferred_element_type=F32)


def params(limit=VMEM):
    return pltpu.CompilerParams(vmem_limit_bytes=limit)


def whole(shape):
    return pl.BlockSpec(shape, lambda *_: (0,) * len(shape))


def vmem():
    return pl.BlockSpec(memory_space=pltpu.VMEM)


def smem():
    return pl.BlockSpec(memory_space=pltpu.SMEM)


def pick(lab_ref, rank_ref, g, slots):
    owner = lax.shift_right_logical(lab_ref[...].reshape(1, ROWS), GROUP_SHIFT)
    slot = jnp.where(owner == g, rank_ref[...], -1)
    return (iota((slots, ROWS), 0) == slot).astype(F32).astype(BF)


def pack_first_kernel(emb_ref, lab_ref, out_ref, rank_ref, *refs):
    *rests, unit = refs
    g = pl.program_id(0)
    lab = lab_ref[...].reshape(1, ROWS)

    @pl.when(g == 0)
    def _():
        values = emb_ref[...].astype(F32)
        total = jnp.sum(values * values, axis=1, keepdims=True)
        rows = (values * lax.rsqrt(total + EPSILON)).astype(BF)
        start = 0
        for ref in (unit, *rests):
            stop = start + ref.shape[1]
            ref[...] = rows[:, start:stop]
            start = stop
        owner = lax.shift_right_logical(lab, GROUP_SHIFT)
        onehot = (iota((TILE_ROWS, ROWS), 0) == owner).astype(F32)
        before = (iota((ROWS, ROWS), 0) < iota((ROWS, ROWS), 1)).astype(F32).astype(BF)
        seen = dot(onehot.astype(BF), before)
        rank_ref[...] = jnp.sum(onehot * seen, axis=0, keepdims=True).astype(jnp.int32)

    marks = jnp.broadcast_to(lab.astype(F32) + 1.0, (TAIL, ROWS)).astype(BF)
    for k in range(AT_ONCE):
        chosen = pick(lab_ref, rank_ref, g * AT_ONCE + k, LANES)
        out_ref[k] = dot(chosen[:PAIR], unit[...]).astype(BF)
        out_ref[k, CAP:, :LANES] = (dot_nt(marks, chosen) - 1.0).astype(BF)
        out_ref[k, CAP:, LANES:] = jnp.zeros((TAIL, PIECE - LANES), BF)


def pack_first(embeddings, labels):
    return pl.pallas_call(
        pack_first_kernel,
        grid=(TILE_ROWS // AT_ONCE,),
        in_specs=[whole((ROWS, WIDTH)), whole((ROWS,))],
        out_specs=[
            pl.BlockSpec((AT_ONCE, PAIR, PIECE), lambda g: (g, 0, 0)),
            whole((1, ROWS)),
        ]
        + [whole((ROWS, w)) for w in PIECES[1:]],
        out_shape=[
            jax.ShapeDtypeStruct((TILE_ROWS, PAIR, PIECE), BF),
            jax.ShapeDtypeStruct((1, ROWS), jnp.int32),
        ]
        + [jax.ShapeDtypeStruct((ROWS, w), BF) for w in PIECES[1:]],
        scratch_shapes=[pltpu.VMEM((ROWS, PIECE), BF)],
        compiler_params=params(PACK_VMEM),
        name="pack_first",
    )(embeddings, labels)


def pack_rest_kernel(unit_ref, lab_ref, rank_ref, out_ref):
    chosen = pick(lab_ref, rank_ref, pl.program_id(0), CAP)
    out_ref[0] = dot(chosen, unit_ref[...]).astype(BF)


def pack_rest(unit, labels, rank):
    width = unit.shape[1]
    return pl.pallas_call(
        pack_rest_kernel,
        grid=(TILE_ROWS,),
        in_specs=[whole((ROWS, width)), whole((ROWS,)), whole((1, ROWS))],
        out_specs=pl.BlockSpec((1, CAP, width), lambda g: (g, 0, 0)),
        out_shape=jax.ShapeDtypeStruct((TILE_ROWS, CAP, width), BF),
        compiler_params=params(PACK_VMEM),
        cost_estimate=pl.CostEstimate(
            flops=2 * TILE_ROWS * CAP * ROWS * width,
            bytes_accessed=2 * TILE_ROWS * CAP * width,
            transcendentals=0,
        ),
        name="pack_rest",
    )(unit, labels, rank)


def close_gaps(got_ref, rows, offsets, counts):
    sent = got_ref.shape[1]
    rows[:16] = jnp.zeros((16, rows.shape[1]), BF)
    column = iota((PAIR, sent), 1)
    apart = iota((PAIR, sent), 0) - column
    for r in range(TILE_ROWS):
        base = pl.multiple_of(lax.shift_right_logical(offsets[r], 4) * 16, 16)
        move = (apart == offsets[r] - base) & (column < counts[r])
        moved = dot(move.astype(F32).astype(BF), got_ref[r]).astype(BF)
        rows[pl.ds(base, 16)] = rows[pl.ds(base, 16)] + moved[:16]
        rows[pl.ds(base + 16, PAIR - 16)] = moved[16:]


def compact_first_kernel(got_ref, out_ref, place_ref, rows):
    names = jnp.zeros((8, SPAN), F32)
    offset = jnp.int32(0)
    offsets, counts = [], []
    for r in range(TILE_ROWS):
        lab = got_ref[r, CAP:, :LANES].astype(F32)[:8]
        count = jnp.sum((lab[:1] >= 0.0).astype(F32)).astype(jnp.int32)
        held = jnp.concatenate(
            [jnp.maximum(lab, 0.0), jnp.zeros((8, SPAN - LANES), F32)], axis=1
        )
        names += pltpu.roll(held, offset, 1)
        place_ref[r] = offset
        place_ref[TILE_ROWS + r] = count
        offsets.append(offset)
        counts.append(count)
        offset = offset + count
    close_gaps(got_ref, rows, offsets, counts)
    out_ref[:ROWS] = rows[:ROWS]
    out_ref[ROWS:] = jnp.concatenate([names[:, :PIECE], names[:, PIECE : 2 * PIECE]], axis=0).astype(BF)


def compact_first(got):
    return pl.pallas_call(
        compact_first_kernel,
        in_specs=[vmem()],
        out_specs=[vmem(), smem()],
        out_shape=[
            jax.ShapeDtypeStruct((BLOCK, PIECE), BF),
            jax.ShapeDtypeStruct((2 * TILE_ROWS,), jnp.int32),
        ],
        scratch_shapes=[pltpu.VMEM((ROWS + PAIR, PIECE), BF)],
        compiler_params=params(),
        name="compact_first",
    )(got)


def compact_rest_kernel(place_ref, got_ref, out_ref, rows):
    places = [place_ref[i] for i in range(2 * TILE_ROWS)]
    close_gaps(got_ref, rows, places[:TILE_ROWS], places[TILE_ROWS:])
    out_ref[...] = rows[:ROWS]


def compact_rest(place, got):
    width = got.shape[2]
    return pl.pallas_call(
        compact_rest_kernel,
        in_specs=[smem(), vmem()],
        out_specs=vmem(),
        out_shape=jax.ShapeDtypeStruct((ROWS, width), BF),
        scratch_shapes=[pltpu.VMEM((ROWS + PAIR, width), BF)],
        compiler_params=params(),
        name="compact_rest",
    )(place, got)


def fold(tile):
    return tile.reshape(tile.shape[0] // 8, 8, tile.shape[1])


def merge(parts):
    top = functools.reduce(jnp.maximum, [p[0] for p in parts])
    factors = [jnp.exp2(p[0] - top) for p in parts]
    total = sum(p[1] * f for p, f in zip(parts, factors))
    weight = sum(p[2] * f for p, f in zip(parts, factors))
    return top, total, weight


def put_stats(ref, stats):
    for k, value in enumerate(stats):
        ref[k : k + 1] = value


def get_stats(ref):
    return tuple(ref[k : k + 1] for k in range(3))


def spread_names(block):
    tail = block[ROWS:].astype(F32)
    names = jnp.concatenate([tail[:1], tail[8:9, : ROWS - PIECE]], axis=1)
    return names, jnp.transpose(jnp.broadcast_to(names, (128, ROWS)))


def across(mark):
    return jnp.concatenate([mark] * (ROWS // 128), axis=1)


def gather_columns(top, total, weight):
    best = jnp.max(top, axis=0, keepdims=True)
    factor = jnp.exp2(top - best)
    return (
        best,
        jnp.sum(total * factor, axis=0, keepdims=True),
        jnp.sum(weight * factor, axis=0, keepdims=True),
    )


def own_kernel(block, *refs):
    *rests, out, scores = refs
    names, marks = spread_names(block)
    top = jnp.full((8, ROWS), FLOOR, F32)
    for start in range(0, ROWS, CHUNK):
        sims = dot_nt(block[start : start + CHUNK], block[:ROWS])
        for rest in rests:
            sims += dot_nt(rest[start : start + CHUNK], rest[...])
        sims = sims * SCALE2
        mask = (across(marks[start : start + CHUNK]) == names) & (
            iota((CHUNK, ROWS), 0) + start != iota((CHUNK, ROWS), 1)
        )
        sims = jnp.where(mask, sims, NEGATIVE)
        scores[start : start + CHUNK] = sims
        top = jnp.maximum(top, jnp.max(fold(sims), axis=0))
    total = jnp.zeros((8, ROWS), F32)
    weight = jnp.zeros((8, ROWS), F32)
    for start in range(0, ROWS, STRIP):
        sims = scores[start : start + STRIP]
        terms = jnp.exp2(fold(sims) - top)
        total += jnp.sum(terms, axis=0)
        weight += jnp.sum(terms * fold(sims), axis=0)
    put_stats(out, gather_columns(top, total, weight))


def own_pairs(pieces):
    return pl.pallas_call(
        own_kernel,
        out_shape=jax.ShapeDtypeStruct((8, ROWS), F32),
        in_specs=[vmem()] * len(pieces),
        out_specs=vmem(),
        scratch_shapes=[pltpu.VMEM((ROWS, ROWS), F32)],
        compiler_params=params(),
        cost_estimate=pl.CostEstimate(
            flops=2 * ROWS * ROWS * WIDTH,
            bytes_accessed=2 * BLOCK * WIDTH,
            transcendentals=ROWS * ROWS,
        ),
        name="own",
    )(*pieces)


def pair_kernel(plan, blocks, old, half_ref, *refs):
    n, n_old = len(blocks), len(old)
    m = len(PIECES)
    pieces = [refs[i * n : (i + 1) * n] for i in range(m)]
    ins, olds = pieces[0], refs[m * n : m * n + n_old]
    outs = refs[m * n + n_old : (m + 1) * n + n_old]
    marks, names, rows, tops, totals, weights, scores0, scores1 = refs[(m + 1) * n + n_old :]
    scores = (scores0, scores1)
    place = {b: i for i, b in enumerate(blocks)}
    lane = iota((1, 128), 1)
    empty = jnp.where(lane % 4 == 0, NEGATIVE, 0.0)
    lefts = {place[l] for l, _, _ in plan} | {place[r] for _, r, axis in plan if axis is not None}
    for i in lefts:
        rows[i] = jnp.broadcast_to(empty, (ROWS, 128))
    tops[...] = jnp.full((n, 8, ROWS), FLOOR, F32)
    totals[...] = jnp.zeros((n, 8, ROWS), F32)
    weights[...] = jnp.zeros((n, 8, ROWS), F32)
    ready = set()

    def need(i):
        if i not in ready:
            ready.add(i)
            one, many = spread_names(ins[i])
            names[i] = jnp.broadcast_to(one, (8, ROWS))
            if i in lefts:
                marks[i] = many

    steps = []
    for k, (left, right, axis) in enumerate(plan):
        left, right = place[left], place[right]
        if axis is None:
            steps += [(k, left, right, s, (left, right), None) for s in (0, HALF)]
        else:
            half = half_ref[axis]
            first = jnp.where(half == 0, left, right)
            second = jnp.where(half == 0, right, left)
            start = pl.multiple_of(half * HALF, HALF)
            steps.append((k, first, second, start, (left, right), half == 0))

    def product(step, out):
        _, _, _, start, both, first = step
        for i in both:
            need(i)
        here = pl.ds(start, HALF)

        def multiply(pieces):
            left, right = pieces[both[0]], pieces[both[1]]
            if first is None:
                return dot_nt(left[here], right[:ROWS])
            keys = jnp.where(first, left[here], right[here])
            return dot_nt(keys, jnp.where(first, right[:ROWS], left[:ROWS]))

        out[...] = sum(multiply(p) for p in pieces)

    def reduce(step, data):
        k, left, right, start, _, _ = step
        name = names[right][:1]
        top = tops[right]
        peak = top
        for at in range(0, HALF, STRIP):
            here = pl.ds(start + at, STRIP)
            mask = across(marks[left, here]) == name
            sims = jnp.where(mask, data[at : at + STRIP] * SCALE2, NEGATIVE)
            data[at : at + STRIP] = sims
            peak = jnp.maximum(peak, jnp.max(fold(sims), axis=0))
            best = jnp.maximum(jnp.max(sims, axis=1, keepdims=True), FLOOR)
            terms = jnp.exp2(sims - best)
            total = jnp.sum(terms, axis=1, keepdims=True)
            weight = jnp.sum(terms * sims, axis=1, keepdims=True)
            rows[left, here] = jnp.where(
                lane == 4 * k,
                best,
                jnp.where(
                    lane == 4 * k + 1, total, jnp.where(lane == 4 * k + 2, weight, rows[left, here])
                ),
            )
        factor = jnp.exp2(top - peak)
        total = totals[right] * factor
        weight = weights[right] * factor
        for at in range(0, HALF, STRIP):
            sims = fold(data[at : at + STRIP])
            terms = jnp.exp2(sims - peak)
            total += jnp.sum(terms, axis=0)
            weight += jnp.sum(terms * sims, axis=0)
        tops[right] = peak
        totals[right] = total
        weights[right] = weight

    product(steps[0], scores[0])
    for t, step in enumerate(steps):
        if t + 1 < len(steps):
            product(steps[t + 1], scores[(t + 1) % 2])
        reduce(step, scores[t % 2])

    for i, b in enumerate(blocks):
        parts = [gather_columns(tops[i], totals[i], weights[i])]
        mine = [k for k, (left, right, axis) in enumerate(plan) if left == b or (axis is not None and right == b)]
        if mine:
            turned = jnp.transpose(rows[i])
            parts += [tuple(turned[4 * k + j : 4 * k + j + 1] for j in range(3)) for k in mine]
        if b in old:
            parts.append(get_stats(olds[old.index(b)]))
        put_stats(outs[i], merge(parts))


def pairs(plan, blocks, old, halves):
    names, n = list(blocks), len(blocks)
    steps = sum(2 if axis is None else 1 for _, _, axis in plan)
    return pl.pallas_call(
        functools.partial(pair_kernel, plan, names, list(old)),
        out_shape=[jax.ShapeDtypeStruct((8, ROWS), F32)] * n,
        in_specs=[smem()] + [vmem()] * (len(PIECES) * n) + [vmem()] * len(old),
        out_specs=[vmem()] * n,
        scratch_shapes=[
            pltpu.VMEM((n, ROWS, 128), F32),
            pltpu.VMEM((n, 8, ROWS), F32),
            pltpu.VMEM((n, ROWS, 128), F32),
            pltpu.VMEM((n, 8, ROWS), F32),
            pltpu.VMEM((n, 8, ROWS), F32),
            pltpu.VMEM((n, 8, ROWS), F32),
            pltpu.VMEM((HALF, ROWS), F32),
            pltpu.VMEM((HALF, ROWS), F32),
        ],
        compiler_params=params(),
        cost_estimate=pl.CostEstimate(
            flops=2 * steps * HALF * ROWS * WIDTH,
            bytes_accessed=2 * n * BLOCK * WIDTH,
            transcendentals=2 * steps * HALF * ROWS,
        ),
        name="pairs",
    )(halves, *[b[i] for i in range(len(PIECES)) for b in blocks.values()], *old.values())


def spread_kernel(offset_ref, *refs):
    out_ref = refs[-1]
    top, total, weight = merge([get_stats(r) for r in refs[:-1]])
    best = top / SCALE2
    mean = weight / total / SCALE2
    row = iota((8, ROWS), 0)
    values = jnp.where(row == 0, best, jnp.where(row == 1, mean, 0.0))
    values = jnp.concatenate([values, jnp.zeros((8, SPAN - ROWS), F32)], axis=1)
    for r in range(TILE_ROWS):
        offset = offset_ref[r]
        moved = pltpu.roll(values, lax.rem(SPAN - offset, SPAN), 1)
        for k in range(6):
            lanes = slice(k % 3 * 128, k % 3 * 128 + 128)
            out_ref[r, k : k + 1] = moved[k // 3 : k // 3 + 1, lanes]
        out_ref[r, 6:] = jnp.zeros((2, 128), F32)


def spread(offsets, stats):
    return pl.pallas_call(
        spread_kernel,
        out_shape=jax.ShapeDtypeStruct((TILE_ROWS, 8, 128), F32),
        in_specs=[pl.BlockSpec(memory_space=pltpu.SMEM)]
        + [pl.BlockSpec(memory_space=pltpu.VMEM)] * len(stats),
        out_specs=pl.BlockSpec(memory_space=pltpu.VMEM),
        compiler_params=params(),
        name="spread",
    )(offsets, *stats)


def unpack_kernel(back_ref, lab_ref, rank_ref, best_ref, mean_ref, flag_ref):
    found = jnp.zeros((24, ROWS), F32)
    for g in range(TILE_ROWS):
        chosen = pick(lab_ref, rank_ref, g, LANES)
        rows = [back_ref[g, k : k + 1] for k in range(6)]
        best, mean = jnp.concatenate(rows[:3], axis=1), jnp.concatenate(rows[3:], axis=1)
        values = jnp.concatenate([best, mean, jnp.zeros((6, LANES), F32)], axis=0)
        high = values.astype(BF).astype(F32)
        mid = (values - high).astype(BF).astype(F32)
        low = values - high - mid
        found += dot(jnp.concatenate([high, mid, low], axis=0).astype(BF), chosen)
    found = found[:8] + (found[8:16] + found[16:])
    best = found[:1]
    best_ref[...] = best.reshape(ROWS)
    mean_ref[...] = found[1:2].reshape(ROWS)
    flag_ref[...] = (1.0 / (1.0 + jnp.exp(-SHARPNESS * (best - THRESHOLD)))).reshape(ROWS)


def unpack(back, labels, rank):
    return pl.pallas_call(
        unpack_kernel,
        out_shape=[jax.ShapeDtypeStruct((ROWS,), F32)] * 3,
        in_specs=[pl.BlockSpec(memory_space=pltpu.VMEM)] * 3,
        out_specs=[pl.BlockSpec(memory_space=pltpu.VMEM)] * 3,
        compiler_params=params(),
        name="unpack",
    )(back, labels, rank)


def shift(array, dx, dy):
    moves = []
    for tr in range(TILE_ROWS):
        sign = 1 - 2 * (tr % 2)
        for x in range(SIDE):
            for y in range(SIDE):
                to = ((x + sign * dx) % SIDE) * SIDE + (y + sign * dy) % SIDE
                base = tr * SIDE * SIDE
                moves.append((base + x * SIDE + y, base + to))
    return lax.ppermute(array, ("tr", "tc"), moves)


PLACES = {"O": (0, 0), "A": (1, 0), "B": (2, 0), "C": (0, 1), "D": (0, -1), "E": (0, 2)}
FIRST = [("O", "A", None)]
NEAR = [("O", "C", None), ("A", "C", None), ("D", "A", None), ("C", "D", 1)]
FAR_X = [("B", "O", 0), ("B", "C", None)]
FAR_Y = [("E", "A", None), ("E", "B", 0)]


def per_device(embeddings, labels):
    tie = lax.optimization_barrier
    tc = lax.axis_index("tc")
    halves = jnp.stack([tc // (2 * SIDE), (tc % SIDE) // 2]).astype(jnp.int32)

    def exchange(packed):
        return lax.all_to_all(packed, "tr", split_axis=0, concat_axis=0, tiled=True)

    packed, rank, *units = pack_first(embeddings, labels)
    got = exchange(packed)
    blocks = {q: [] for q in "OABCDE"}
    place = None
    last = len(PIECES) - 1
    for k in range(len(PIECES)):
        if k < last:
            packed = pack_rest(units[k], labels, rank)
            packed, got = tie((packed, got))
            later = exchange(packed)
        if k == 0:
            mine, place = compact_first(got)
        else:
            mine = compact_rest(place, got)
        a, c, d = shift(mine, -1, 0), shift(mine, 0, -1), shift(mine, 0, 1)
        if k == last:
            here, blocks["E"][-1] = tie((mine, blocks["E"][-1]))
            own = own_pairs([*blocks["O"], here])
            a, own, halves = tie((a, own, halves))
        b = shift(a, -1, 0)
        if k == last:
            sides = {"O": [*blocks["O"], mine], "A": [*blocks["A"], a]}
            stats = dict(zip(sides, pairs(FIRST, sides, {"O": own}, halves)))
            d, stats["O"] = tie((d, stats["O"]))
        e = shift(d, 0, 1)
        if k < last:
            got, d, c, b, a = tie((later, d, c, b, a))
        for q, piece in zip("OABCDE", (mine, a, b, c, d, e)):
            blocks[q].append(piece)
    near = {q: blocks[q] for q in "OACD"}
    stats.update(zip(near, pairs(NEAR, near, stats, halves)))
    wide = {q: blocks[q] for q in "OCB"}
    stats.update(zip(wide, pairs(FAR_X, wide, {q: stats[q] for q in "OC"}, halves)))
    wide = {q: blocks[q] for q in "ABE"}
    stats.update(zip(wide, pairs(FAR_Y, wide, {q: stats[q] for q in "AB"}, halves)))
    stats["D"], stats["B"] = tie((stats["D"], stats["B"]))
    parts = [stats["O"]] + [shift(stats[q], *PLACES[q]) for q in "ABCDE"]
    sent = spread(place, parts)
    back = exchange(sent)
    return unpack(back, labels, rank)


def solution(mesh):
    files = P(("tr", "tc"))
    return jax.shard_map(
        per_device,
        mesh=mesh,
        in_specs=(P(("tr", "tc"), None), files),
        out_specs=(files, files, files),
        check_vma=False,
    )
```
